512 devices in a mesh: fsdp: 32 (over z, y_hi, core), tp: 4 (over y_lo), dp: 4 (over x).
Axes of the slice: x: 4, y: 8 (y_hi: 2, y_lo: 4; y = y_hi * 4 + y_lo), z: 8, core: 2. Of those that a mesh axis runs over, the one named last changes fastest.
Arguments:
- acts: bfloat16 [12288, 8192], P('fsdp', ('tp', 'dp')), may hold values from -6 to 6
- kv_grad: bfloat16 [12288, 2048], P('fsdp', ('tp', 'dp')), may hold values from -6 to 6
- rewards: float32 [256], P('fsdp'), may hold values from -16 to 16
- group_ids: int32 [256], P('fsdp'), may hold values from 0 to 31, as said below
- kv_weight: bfloat16 [8192, 2048], P('fsdp', ('tp', 'dp')), may hold values from -0.0625 to 0.0625
- adam_m: float32 [8192, 2048], P('fsdp', ('tp', 'dp')), may hold values from -3 to 3
- adam_v: float32 [8192, 2048], P('fsdp', ('tp', 'dp')), may hold values from 0.5 to 50
- hidden: bfloat16 [4, 3072, 8192], P(None, ('fsdp', 'dp')), may hold values from -6 to 6
- queries: bfloat16 [4, 3072, 8192], P(None, ('fsdp', 'dp'), 'tp'), may hold values from -16 to 16
- cache_keys: bfloat16 [3072, 64, 1024], P(('fsdp', 'dp'), None, 'tp'), may hold values from -16 to 16
- cache_values: bfloat16 [3072, 64, 1024], P(('fsdp', 'dp'), None, 'tp'), may hold values from -6 to 6
- cache_lens: int32 [3072], P(('fsdp', 'dp')), may hold values from 16 to 64
Outputs:
- new_weight: bfloat16 [8192, 2048], P('fsdp', ('tp', 'dp'))
- new_m: float32 [8192, 2048], P('fsdp', ('tp', 'dp'))
- new_v: float32 [8192, 2048], P('fsdp', ('tp', 'dp'))
- new_entries: bfloat16 [4, 3072, 2048], P(None, ('fsdp', 'dp'), 'tp')
- attention: bfloat16 [4, 3072, 8192], P(None, ('fsdp', 'dp'), 'tp')
The draws below stay inside these ranges and needn't reach their ends.
Inputs may be any that keep to these rules, and one draw needn't show every extreme that they name: `group_ids`: each group number names exactly 8 sequences.
All inputs are finite; a program needn't handle non-finite values.
Results may differ from the reference program's by a relative error of at most 0.024.
Values may be sent and summed in bfloat16 or wider, within the bound.
A program may use at most 64 MiB of HBM per device.

```python
import math
from functools import partial
import jax
import jax.numpy as jnp
from jax import lax

D = 8192
HD = 128
KVH = 8
QH = 64
KVW = 1024
KVC = 2048
QW = 8192
LEN = 48
GSIZE = 8
TOK_DEV = 384
TOKENS = 12288
SEQS = 256
GROUPS = 32
ROWS = 3072
CACHE = 64
STEPS = 4
N_FSDP = 32


def draw_rewards(key, part):
    key = jax.random.fold_in(key, 1)
    position = jnp.arange(SEQS, dtype=jnp.float32) / max(SEQS - 1, 1)
    values_drawn = jnp.clip(jax.random.normal(key, (SEQS,), jnp.float32), -4.0, 4.0) * (1.0 + 2.0 * position)
    return values_drawn.astype(jnp.float32)


def draw_group_ids(key, part):
    key = jax.random.fold_in(key, 2)
    return (jax.random.permutation(key, SEQS) % GROUPS).astype(jnp.int32)


def draw_cache_lens(key, part):
    key = jax.random.fold_in(key, 3)
    first_key, second_key = jax.random.split(key)
    short_by = jax.random.randint(first_key, (ROWS,), 0, CACHE - CACHE // 4 + 1)
    lengths = CACHE - short_by
    full_row = jax.random.randint(second_key, (), 0, ROWS)
    lengths = jnp.where(jnp.arange(ROWS) == full_row, CACHE, lengths)
    return lengths.astype(jnp.int32)


def draw_cache_keys(key, part):
    key = jax.random.fold_in(key, 4)
    values_drawn = jnp.clip(jax.random.normal(key, (ROWS, CACHE, KVW), jnp.float32), -4.0, 4.0)
    return values_drawn.astype(jnp.bfloat16)


def draw_queries(key, part):
    key = jax.random.fold_in(key, 5)
    values_drawn = jnp.clip(jax.random.normal(key, (STEPS, ROWS, QW), jnp.float32), -4.0, 4.0)
    return values_drawn.astype(jnp.bfloat16)


def strengthened(drawn, rng, source, target, parts, factor):
    def block_of(dim):
        return (jnp.arange(drawn.shape[dim]) // (drawn.shape[dim] // parts)).reshape((-1,) + (1,) * (drawn.ndim - 1 - dim))

    one_side = jax.random.permutation(rng, parts)[block_of(target)]
    other_side = (block_of(target) + parts // 2) % parts
    return jnp.where((block_of(source) == one_side) | (block_of(source) == other_side), factor * drawn, drawn)


def steps_of(own_key, shape, shards, low, high):
    factor_of, own = 1.0, jax.random.fold_in(own_key, 6)
    for dim, blocks in shards:
        draws = jnp.exp(jax.random.uniform(jax.random.fold_in(own, dim), (blocks,), jnp.float32, low / len(shards), high / len(shards)))
        factor_of = factor_of * jnp.repeat(draws, shape[dim] // blocks).reshape([-1 if axis == dim else 1 for axis in range(len(shape))])
    return factor_of


def bell_draw(rng, shape, width, reach, cuts=(), kind=jnp.bfloat16):
    values = width * jax.random.normal(rng, shape, jnp.float32)
    if cuts:
        values = values * steps_of(rng, shape, cuts, -0.22, 0.18)
    return jnp.clip(values, -reach, reach).astype(kind)


def noise_with(key, dims, spread, most, cuts, heavy, held_as=jnp.bfloat16):
    values = spread * jax.random.normal(key, dims, jnp.float32)
    if cuts:
        values = values * steps_of(key, dims, cuts, -0.22, 0.18)
    return jnp.clip(strengthened(values, jax.random.fold_in(key, 3), *heavy), -most, most).astype(held_as)


def setup_inputs(seed: int = 0) -> dict:
    key_of = jax.random.split(jax.random.key(seed), 13)
    acts = noise_with(key_of[0], (TOKENS, D), 1.0, 6.0, ((0, 32), (1, 16)), (0, 1, 32, 2.75))
    kv_grad = bell_draw(key_of[1], (TOKENS, KVC), 1.0, 6.0, ((0, 32), (1, 16)))
    rewards = draw_rewards(jax.random.fold_in(key_of[12], 71), 0)
    group_ids = draw_group_ids(jax.random.fold_in(key_of[12], 71), 0)
    kv_weight = bell_draw(key_of[4], (D, KVC), D ** -0.5, 0.0625, ((0, 32), (1, 16)))
    adam_m = bell_draw(key_of[5], (D, KVC), 0.5, 3.0, ((0, 32), (1, 16)), jnp.float32)
    adam_v = jnp.clip(jnp.exp(math.log(50.0) - 4.6051702 * jax.random.uniform(key_of[6], (D, KVC), jnp.float32) ** steps_of(key_of[6], (D, KVC), ((0, 32), (1, 16)), -0.2, 0.2)), 0.5, 50.0)
    hidden = bell_draw(key_of[7], (STEPS, ROWS, D), 1.0, 6.0, ((1, 128),))
    queries = draw_queries(jax.random.fold_in(key_of[12], 71), 0)
    cache_keys = draw_cache_keys(jax.random.fold_in(key_of[12], 71), 0)
    cache_values = bell_draw(key_of[10], (ROWS, CACHE, KVW), 1.0, 6.0, ((0, 128), (2, 4)))
    cache_lens = draw_cache_lens(jax.random.fold_in(key_of[12], 71), 0)
    return {"acts": acts, "kv_grad": kv_grad, "rewards": rewards, "group_ids": group_ids, "kv_weight": kv_weight, "adam_m": adam_m, "adam_v": adam_v, "hidden": hidden, "queries": queries, "cache_keys": cache_keys, "cache_values": cache_values, "cache_lens": cache_lens}


beta_one = 0.9
beta_two = 0.95
learn_rate = 0.001
decay_rate = 0.1
adam_eps = 1e-08
correct_one = 1.0 - beta_one ** 10
correct_two = 1.0 - beta_two ** 10
masked_score = -1e+30

def attend_head(items, lens_rows):
    query_part, keys_part, values_part, fresh_keys, fresh_values = items
    query_f = query_part.astype(jnp.float32)
    score_scale = HD ** (-0.5)
    cache_scores = jnp.einsum('srgd,rcd->rgsc', query_f, keys_part.astype(jnp.float32)) * score_scale
    positions = jnp.arange(CACHE, dtype=jnp.int32)
    valid_mask = positions[None, :] < lens_rows[:, None]
    cache_scores = jnp.where(valid_mask[:, None, None, :], cache_scores, masked_score)
    new_scores = jnp.einsum('srgd,trd->rgst', query_f, fresh_keys.astype(jnp.float32)) * score_scale
    order = jnp.arange(STEPS, dtype=jnp.int32)
    causal_mask = order[:, None] >= order[None, :]
    new_scores = jnp.where(causal_mask, new_scores, masked_score)
    row_max = jnp.maximum(lax.optimization_barrier(jnp.max(cache_scores, axis=-1)), lax.optimization_barrier(jnp.max(new_scores, axis=-1)))
    cache_exp = jnp.exp(cache_scores - row_max[..., None])
    new_exp = jnp.exp(new_scores - row_max[..., None])
    total = lax.optimization_barrier(jnp.sum(cache_exp, axis=-1)) + lax.optimization_barrier(jnp.sum(new_exp, axis=-1))
    cache_probs = lax.optimization_barrier((cache_exp / total[..., None]).astype(jnp.bfloat16)).astype(jnp.float32)
    new_probs = lax.optimization_barrier((new_exp / total[..., None]).astype(jnp.bfloat16)).astype(jnp.float32)
    mixed = jnp.einsum('rgsc,rcd->srgd', cache_probs, values_part.astype(jnp.float32))
    mixed = mixed + jnp.einsum('rgst,trd->srgd', new_probs, fresh_values.astype(jnp.float32))
    return mixed.astype(jnp.bfloat16)

def reference(acts, kv_grad, rewards, group_ids, kv_weight, adam_m, adam_v, hidden, queries, cache_keys, cache_values, cache_lens):
    member = (group_ids[:, None] == jnp.arange(GROUPS, dtype=jnp.int32)[None, :]).astype(jnp.float32)
    group_sums = lax.optimization_barrier(jnp.sum(member * rewards[:, None], axis=0))
    advantage = rewards - lax.optimization_barrier(jnp.sum(member * group_sums[None, :], axis=1)) / GSIZE
    token_adv = jnp.repeat(advantage, LEN)
    weighted = (token_adv[:, None] * kv_grad.astype(jnp.float32)).astype(jnp.bfloat16)
    act_blocks = acts.reshape(N_FSDP, TOK_DEV, D)
    weighted_blocks = weighted.reshape(N_FSDP, TOK_DEV, KVC)

    def add_block(running, shard_pair):
        partial_sum = jnp.dot(shard_pair[0].astype(jnp.float32).T, shard_pair[1].astype(jnp.float32))
        rounded = lax.optimization_barrier(partial_sum.astype(jnp.bfloat16)).astype(jnp.float32)
        return (running + rounded, None)
    summed, unused = lax.scan(add_block, jnp.zeros((D, KVC), jnp.float32), (act_blocks, weighted_blocks))
    weight_grad = summed / LEN
    new_m = beta_one * adam_m + (1.0 - beta_one) * weight_grad
    new_v = beta_two * adam_v + (1.0 - beta_two) * weight_grad * weight_grad
    weight_f = kv_weight.astype(jnp.float32)
    direction = new_m / correct_one / (jnp.sqrt(new_v / correct_two) + adam_eps)
    new_weight = (weight_f - learn_rate * (direction + decay_rate * weight_f)).astype(jnp.bfloat16)
    flat_rows = hidden.reshape(STEPS * ROWS, D).astype(jnp.float32)
    projected = jnp.dot(flat_rows, new_weight.astype(jnp.float32))
    new_entries = projected.astype(jnp.bfloat16).reshape(STEPS, ROWS, KVC)
    fresh = new_entries.reshape(STEPS, ROWS, KVH, 2, HD)
    query_all = jnp.moveaxis(queries.reshape(STEPS, ROWS, KVH, QH // KVH, HD), 2, 0)
    keys_all = jnp.moveaxis(cache_keys.reshape(ROWS, CACHE, KVH, HD), 2, 0)
    values_all = jnp.moveaxis(cache_values.reshape(ROWS, CACHE, KVH, HD), 2, 0)
    fresh_keys = jnp.moveaxis(fresh[:, :, :, 0, :], 2, 0)
    fresh_values = jnp.moveaxis(fresh[:, :, :, 1, :], 2, 0)
    heads_out = lax.map(partial(attend_head, lens_rows=cache_lens), (query_all, keys_all, values_all, fresh_keys, fresh_values))
    attention = jnp.moveaxis(heads_out, 0, 2).reshape(STEPS, ROWS, QW)
    return (new_weight, new_m, new_v, new_entries, attention)
```

```python
import functools

import jax
import jax.numpy as jnp
from jax import lax
from jax.experimental import pallas as pl
from jax.experimental.pallas import tpu as pltpu
from jax.sharding import PartitionSpec as P

HD = 128
LEN = 48
GSIZE = 8
X = 4
T = 4
Z = 8
TOK = 384
SEQ = 8
FEAT = 512
HALF = 256
COL = 128
ROWS = 96
WIDTH = 8192
KSL = WIDTH // X

beta_one = 0.9
beta_two = 0.95
learn_rate = 0.001
decay_rate = 0.1
adam_eps = 1e-08
correct_one = 1.0 - beta_one**10
correct_two = 1.0 - beta_two**10
masked_score = -1e30

MESH = pl.DeviceIdType.MESH
F32 = jnp.float32
BF16 = jnp.bfloat16


def aligned(value, multiple):
    return pl.multiple_of(value * multiple, multiple)


def kernel(
    acts,
    kv,
    rew,
    ids,
    w_in,
    m_in,
    v_in,
    hid,
    nw_out,
    nm_out,
    nv_out,
    ent_out,
    abuf,
    kbuf,
    wbuf,
    wt,
    pbuf,
    rsbuf,
    own,
    hv,
    hl,
    hb,
    nwb,
    wall,
    acc,
    part,
    ebuf,
    rbuf,
    wv,
    mv,
    vv,
    loc_sem,
    a_send,
    a_recv,
    k_send,
    k_recv,
    r_send,
    r_recv,
    rs_send,
    rs_recv,
    o_send,
    o_recv,
    h_send,
    h_recv,
    c_send,
    c_recv,
    w_send,
    w_recv,
    e_send,
    e_recv,
):
    f, t, x = lax.axis_index("fsdp"), lax.axis_index("tp"), lax.axis_index("dp")
    z, g = lax.div(f, 4), lax.rem(f, 4)
    yh, c = lax.div(g, 2), lax.rem(g, 2)
    other, yo = 1 - c, 1 - yh

    def dev(z=z, yh=yh, c=c, t=t, x=x):
        return (z * 4 + yh * 2 + c, t, x)

    def copy(src, dst, send, recv, to):
        return pltpu.make_async_remote_copy(
            src_ref=src, dst_ref=dst, send_sem=send, recv_sem=recv, device_id=to, device_id_type=MESH
        )

    def arrived(dst, recv):
        copy(dst, dst, o_send.at[0], recv, dev(c=other)).wait_recv()

    def xs(step):
        return lax.rem(x + step + X, X)

    def zs(step):
        return lax.rem(z + step + Z, Z)

    def owner_of(slot):
        u = lax.rem(slot - 2 * t + Z, Z)
        a = jnp.where((u >= 1) & (u <= 4), 1, 0)
        w = jnp.where(a == 1, u - 1, lax.rem(Z - u, Z))
        return a, lax.rem(t + 1 + w, T)

    half = pl.ds(aligned(c, HALF), HALF)
    mine = pl.ds(aligned(c, TOK), TOK)
    local = [
        pltpu.make_async_copy(acts.at[:, half], abuf.at[x, mine], loc_sem.at[0]),
        pltpu.make_async_copy(kv, kbuf.at[mine, pl.ds(aligned(t, COL), COL)], loc_sem.at[1]),
        pltpu.make_async_copy(hid, hv, loc_sem.at[2]),
        pltpu.make_async_copy(w_in, wv, loc_sem.at[3]),
        pltpu.make_async_copy(m_in, mv, loc_sem.at[4]),
        pltpu.make_async_copy(v_in, vv, loc_sem.at[5]),
    ]
    for item in local:
        item.start()

    barrier = pltpu.get_barrier_semaphore()
    senders = [dev(c=other)]
    for step in range(1, X):
        senders += [dev(x=xs(step)), dev(x=xs(step), c=other)]
    senders += [dev(t=lax.rem(t + step, T)) for step in range(1, T)]
    senders += [dev(z=zs(step)) for step in range(1, Z)]
    senders += [dev(yh=yo), dev(yh=yo, c=other)]
    t_src, a_own = lax.div(z, 2), lax.rem(z, 2)
    w_src = lax.rem(t - t_src - 1 + 2 * T, T)
    u_src = jnp.where(a_own == 1, 1 + w_src, lax.rem(Z - w_src, Z))
    z_src = lax.rem(2 * t_src + u_src, Z)
    senders += [dev(z=z_src, t=t_src, yh=0), dev(z=z_src, t=t_src, yh=1)]
    senders += [dev(yh=yo, c=lax.div(x, 2), x=2 * c), dev(yh=yo, c=lax.div(x, 2), x=2 * c + 1)]
    for sender in senders:
        pl.semaphore_signal(barrier, inc=1, device_id=sender, device_id_type=MESH)

    rbuf[g, z] = jnp.full((8, 128), -1.0, F32)
    rbuf[g, z, 0:1, 0:SEQ] = rew[...]
    rbuf[g, z, 1:2, 0:SEQ] = ids[...].astype(F32)

    pl.semaphore_wait(barrier, len(senders))

    sends = []

    def start(item):
        item.start()
        sends.append(item)

    for step, sign in ((0, 1), (1, -1)):
        for core in range(2):
            start(
                copy(
                    acts.at[:, pl.ds(core * HALF, HALF)],
                    abuf.at[x, mine],
                    a_send.at[2 * step + core],
                    a_recv.at[x, c],
                    dev(x=xs(sign), c=core),
                )
            )
    kslot = kbuf.at[mine, pl.ds(aligned(t, COL), COL)]
    for step in range(1, T):
        start(copy(kv, kslot, k_send.at[step], k_recv.at[t, c], dev(t=lax.rem(t + step, T))))
    for step in range(1, Z):
        start(copy(rbuf.at[g, z], rbuf.at[g, z], r_send.at[step], r_recv.at[z], dev(z=zs(step))))
    start(
        copy(
            acts.at[:, pl.ds(aligned(other, HALF), HALF)],
            abuf.at[x, mine],
            a_send.at[4],
            a_recv.at[x, c],
            dev(c=other),
        )
    )
    start(copy(kv, kslot, k_send.at[0], k_recv.at[t, c], dev(c=other)))

    for step in range(1, Z):
        arrived(rbuf.at[g, zs(step)], r_recv.at[zs(step)])
    for step, (to_yh, to_c) in enumerate(((yh, other), (yo, c), (yo, other))):
        start(copy(rbuf.at[g], rbuf.at[g], r_send.at[Z + step], r_recv.at[Z + g], dev(yh=to_yh, c=to_c)))

    local[2].wait()
    for q in range(WIDTH // FEAT):
        for to in range(X):
            hl[to, :, q * 128 : (q + 1) * 128] = hv[:, q * FEAT + to * 128 : q * FEAT + (to + 1) * 128]

    left, right = xs(-1), xs(1)
    first, second = pl.ds(0, TOK), pl.ds(TOK, TOK)
    arrived(abuf.at[left, first], a_recv.at[left, 0])
    start(copy(abuf.at[left, first], abuf.at[left, first], a_send.at[5], a_recv.at[left, 0], dev(x=right)))
    arrived(abuf.at[right, second], a_recv.at[right, 1])
    start(copy(abuf.at[right, second], abuf.at[right, second], a_send.at[6], a_recv.at[right, 1], dev(x=left)))

    for step in range(1, T):
        tt = lax.rem(t + step, T)
        slot = kbuf.at[mine, pl.ds(aligned(tt, COL), COL)]
        arrived(slot, k_recv.at[tt, c])
        start(copy(slot, slot, k_send.at[T - 1 + step], k_recv.at[tt, c], dev(c=other)))

    for to_yh, to_c in ((yh, other), (yo, c), (yo, other)):
        group = to_yh * 2 + to_c
        arrived(rbuf.at[group], r_recv.at[Z + group])
    eye = lax.broadcasted_iota(jnp.int32, (8, 128), 0) == lax.broadcasted_iota(jnp.int32, (8, 128), 1)
    advantages = []
    for core in range(2):
        slot = rbuf[yh * 2 + core, z]
        rew_col = jnp.sum(jnp.where(eye, slot[0:1, :], 0.0), axis=1, keepdims=True)
        id_col = jnp.sum(jnp.where(eye, slot[1:2, :], 0.0), axis=1, keepdims=True)
        sums = jnp.zeros((8, 128), F32)
        for group in range(4):
            for zz in range(Z):
                sums += jnp.where(rbuf[group, zz, 1:2, :] == id_col, rbuf[group, zz, 0:1, :], 0.0)
        advantages.append(rew_col - jnp.sum(sums, axis=1, keepdims=True) / GSIZE)

    local[1].wait()
    other_rows = pl.ds(aligned(other, TOK), TOK)
    for step in range(T):
        tt = lax.rem(t + step, T)
        arrived(kbuf.at[other_rows, pl.ds(aligned(tt, COL), COL)], k_recv.at[tt, other])
    for core in range(2):
        for seq in range(SEQ):
            rows = pl.ds(core * TOK + seq * LEN, LEN)
            wbuf[rows, :] = (advantages[core][seq : seq + 1, 0:1] * kbuf[rows, :].astype(F32)).astype(BF16)
    wt[...] = wbuf[...].T

    def multiply(src):
        pbuf[src] = jnp.dot(wt[...], abuf[src], preferred_element_type=F32).astype(BF16)

    local[0].wait()
    arrived(abuf.at[x, other_rows], a_recv.at[x, other])
    multiply(x)
    arrived(abuf.at[left, second], a_recv.at[left, 1])
    multiply(left)
    arrived(abuf.at[right, first], a_recv.at[right, 0])
    multiply(right)
    across = xs(2)
    arrived(abuf.at[across, first], a_recv.at[across, 0])
    arrived(abuf.at[across, second], a_recv.at[across, 1])

    hslot = hb.at[x * 2 + c]
    hid_local = pltpu.make_async_copy(hl.at[x], hslot, loc_sem.at[6])
    hid_local.start()
    for step in (1, -1, 2):
        start(copy(hl.at[xs(step)], hslot, h_send.at[step % X], h_recv.at[x, c], dev(x=xs(step))))
    start(copy(hl.at[x], hslot, h_send.at[0], h_recv.at[x, c], dev(c=other)))

    multiply(across)

    def piece(slot, way, chunk):
        a, tt = owner_of(slot)
        return pbuf.at[2 * a + way, pl.ds(aligned(2 * tt + chunk, COL // 2), COL // 2)]

    def ring_copy(src, way, step, chunk):
        return copy(
            src,
            rsbuf.at[way, step, pl.ds(chunk * 64, 64)],
            rs_send.at[way, chunk, step],
            rs_recv.at[way, chunk, step],
            dev(z=zs(1 if way == 0 else -1)),
        )

    def add_own(way, step, chunk):
        here = rsbuf.at[way, step, pl.ds(chunk * 64, 64)]
        arrived(here, rs_recv.at[way, chunk, step])
        slot = lax.rem(z - 2 - step + 2 * Z, Z) if way == 0 else lax.rem(z + 2 + step, Z)
        here[...] = (here[...].astype(F32) + piece(slot, way, chunk)[...].astype(F32)).astype(BF16)
        return here

    for chunk in range(2):
        for way in range(2):
            ring_copy(piece(zs(-1 if way == 0 else 1), way, chunk), way, 0, chunk).start()

    def ring_step(step, carry):
        for chunk in range(2):
            for way in range(2):
                ring_copy(add_own(way, step, chunk), way, step + 1, chunk).start()
        return carry

    lax.fori_loop(0, Z - 2, ring_step, 0)
    a_here, t_here = owner_of(z)
    for chunk in range(2):
        for way in range(2):
            here = add_own(way, Z - 2, chunk)
            start(
                copy(
                    here,
                    own.at[yh, pl.ds(chunk * 64, 64)],
                    o_send.at[2 * way + chunk],
                    o_recv.at[yh, chunk],
                    dev(z=2 * t + a_here, yh=way, t=t_here),
                )
            )

    def ring_done(step, carry):
        for chunk in range(2):
            for way in range(2):
                here = rsbuf.at[way, step, pl.ds(chunk * 64, 64)]
                ring_copy(here, way, step, chunk).wait_send()
        return carry

    lax.fori_loop(0, Z - 1, ring_done, 0)

    for item in local[3:]:
        item.wait()
    for from_yh in range(2):
        for chunk in range(2):
            arrived(own.at[from_yh, pl.ds(chunk * 64, 64)], o_recv.at[from_yh, chunk])
    weight_grad = (own[0].astype(F32) + own[1].astype(F32)).T / LEN
    new_m = beta_one * mv[...] + (1.0 - beta_one) * weight_grad
    new_v = beta_two * vv[...] + (1.0 - beta_two) * weight_grad * weight_grad
    weight_f = wv[...].astype(F32)
    direction = new_m / correct_one / (jnp.sqrt(new_v / correct_two) + adam_eps)
    new_weight = (weight_f - learn_rate * (direction + decay_rate * weight_f)).astype(BF16)
    nwb[...] = new_weight

    is_self = c == lax.div(x, 2)
    cols = pl.ds(aligned(lax.rem(x, 2), COL), COL)
    slices = []
    for r in range(2):
        src = nwb.at[pl.ds(r * COL, COL)]
        dst = wall.at[z * 2 + yh, :, cols]
        recv = c_recv.at[yh, lax.rem(x, 2)]
        near = copy(src, dst, c_send.at[r], recv, dev(c=lax.div(x, 2), x=2 * c + r))
        far = copy(src, dst, c_send.at[2 + r], recv, dev(yh=yo, c=lax.div(x, 2), x=2 * c + r))
        here = is_self & (lax.rem(x, 2) == r)
        start(far)
        pl.when(jnp.logical_not(here))(near.start)
        pl.when(here)(pltpu.make_async_copy(src, dst, recv).start)
        slices.append((here, near))

    nw_out[...] = new_weight
    nm_out[...] = new_m
    nv_out[...] = new_v

    for yy in range(2):
        for hh in range(2):
            arrived(wall.at[z * 2 + yy, :, pl.ds(hh * COL, COL)], c_recv.at[yy, hh])

    def pass_on(zz, yy, way, step):
        slot = wall.at[zz * 2 + yy]
        start(copy(slot, slot, w_send.at[way, yy, step], w_recv.at[zz * 2 + yy], dev(z=zs(1 if way == 0 else -1))))

    for yy in range(2):
        for way in range(2):
            pass_on(z, yy, way, 0)

    for step in (1, -1, 2):
        slot = hb.at[xs(step) * 2 + c]
        arrived(slot, h_recv.at[xs(step), c])
        start(copy(slot, slot, h_send.at[X + step % X], h_recv.at[xs(step), c], dev(c=other)))
    hid_local.wait()
    for step in range(X):
        arrived(hb.at[xs(step) * 2 + other], h_recv.at[xs(step), other])

    def project(zz):
        rows = hb[:, :, pl.ds(aligned(zz, 2 * COL), 2 * COL)].reshape(2 * X * ROWS, 2 * COL)
        block = wall[pl.ds(zz * 2, 2)].reshape(2 * COL, 2 * COL)
        return jnp.dot(rows, block, preferred_element_type=F32)

    acc[...] = project(z)
    for step in range(1, Z // 2):
        for yy, way in ((0, 0), (1, 1), (1, 0), (0, 1)):
            zz = zs(-step if way == 0 else step)
            arrived(wall.at[zz * 2 + yy], w_recv.at[zz * 2 + yy])
            if step < Z // 2 - 1 or yy == way:
                pass_on(zz, yy, way, step)
        acc[...] += project(zs(-step))
        acc[...] += project(zs(step))
    for yy in range(2):
        arrived(wall.at[zs(4) * 2 + yy], w_recv.at[zs(4) * 2 + yy])
    part[...] = (acc[...] + project(zs(4))).astype(BF16).reshape(2 * X, ROWS, 2 * HD)

    for step in (2, 1, -1, 0):
        for core in range(2):
            to_c = c if core == 0 else other
            if step == 0 and core == 0:
                ebuf[x, c] = part[x * 2 + c]
                continue
            start(
                copy(
                    part.at[xs(step) * 2 + to_c],
                    ebuf.at[x, c],
                    e_send.at[2 * (step % X) + core],
                    e_recv.at[x, c],
                    dev(x=xs(step), c=to_c),
                )
            )
    for step in (0, 1, -1, 2):
        for core in range(2):
            from_c = c if core == 0 else other
            if step == 0 and core == 0:
                continue
            arrived(ebuf.at[xs(step), from_c], e_recv.at[xs(step), from_c])
    for head in range(2):
        total = ebuf[0, head].astype(F32)
        for src in range(1, X):
            total += ebuf[src, head].astype(F32)
        ent_out[:, head * 2 * HD : (head + 1) * 2 * HD] = total.astype(BF16)

    for item in sends:
        item.wait_send()
    for here, near in slices:
        pl.when(jnp.logical_not(here))(near.wait_send)


def update_and_project(acts, kv_grad, rewards, group_ids, kv_weight, adam_m, adam_v, hidden):
    any_spec = pl.BlockSpec(memory_space=pl.ANY)
    vmem = pl.BlockSpec(memory_space=pltpu.VMEM)
    dma = pltpu.SemaphoreType.DMA
    return pl.pallas_call(
        kernel,
        out_shape=(
            jax.ShapeDtypeStruct((HALF, COL), BF16),
            jax.ShapeDtypeStruct((HALF, COL), F32),
            jax.ShapeDtypeStruct((HALF, COL), F32),
            jax.ShapeDtypeStruct((ROWS, 4 * HD), BF16),
        ),
        in_specs=[any_spec, any_spec, vmem, vmem, any_spec, any_spec, any_spec, any_spec],
        out_specs=(vmem, vmem, vmem, vmem),
        scratch_shapes=[
            pltpu.VMEM((X, 2 * TOK, HALF), BF16),
            pltpu.VMEM((2 * TOK, T * COL), BF16),
            pltpu.VMEM((2 * TOK, T * COL), BF16),
            pltpu.VMEM((T * COL, 2 * TOK), BF16),
            pltpu.VMEM((X, T * COL, HALF), BF16),
            pltpu.VMEM((2, Z - 1, COL, HALF), BF16),
            pltpu.VMEM((2, COL, HALF), BF16),
            pltpu.VMEM((ROWS, WIDTH), BF16),
            pltpu.VMEM((X, ROWS, KSL), BF16),
            pltpu.VMEM((2 * X, ROWS, KSL), BF16),
            pltpu.VMEM((HALF, COL), BF16),
            pltpu.VMEM((2 * Z, COL, 2 * COL), BF16),
            pltpu.VMEM((2 * X * ROWS, 2 * COL), F32),
            pltpu.VMEM((2 * X, ROWS, 2 * COL), BF16),
            pltpu.VMEM((X, 2, ROWS, 2 * COL), BF16),
            pltpu.VMEM((4, Z, 8, 128), F32),
            pltpu.VMEM((HALF, COL), BF16),
            pltpu.VMEM((HALF, COL), F32),
            pltpu.VMEM((HALF, COL), F32),
            dma((7,)),
            dma((7,)),
            dma((X, 2)),
            dma((2 * T,)),
            dma((T, 2)),
            dma((Z + 3,)),
            dma((Z + 4,)),
            dma((2, 2, Z - 1)),
            dma((2, 2, Z - 1)),
            dma((4,)),
            dma((2, 2)),
            dma((2 * X,)),
            dma((X, 2)),
            dma((4,)),
            dma((2, 2)),
            dma((2, 2, Z // 2)),
            dma((2 * Z,)),
            dma((2 * X,)),
            dma((X, 2)),
        ],
        compiler_params=pltpu.CompilerParams(
            collective_id=0, has_side_effects=True, vmem_limit_bytes=40 * 1024 * 1024
        ),
        name="update_and_project",
    )(
        acts,
        kv_grad,
        rewards.reshape(1, SEQ),
        group_ids.reshape(1, SEQ),
        kv_weight,
        adam_m,
        adam_v,
        hidden.reshape(ROWS, WIDTH),
    )


def body(
    acts,
    kv_grad,
    rewards,
    group_ids,
    kv_weight,
    adam_m,
    adam_v,
    hidden,
    queries,
    cache_keys,
    cache_values,
    cache_lens,
):
    new_weight, new_m, new_v, new_entries = update_and_project(
        acts, kv_grad, rewards, group_ids, kv_weight, adam_m, adam_v, hidden
    )
    step_total, rows_local, width = hidden.shape
    kv_local = cache_keys.shape[2] // HD
    group = queries.shape[2] // HD // kv_local
    score_scale = HD ** (-0.5)
    query_heads = queries.reshape(step_total, rows_local, kv_local, group, HD)
    keys_local = cache_keys.reshape(rows_local, cache_keys.shape[1], kv_local, HD)
    values_local = cache_values.reshape(rows_local, cache_values.shape[1], kv_local, HD)
    cache_scores = (
        jnp.einsum("srhgd,rchd->rhgsc", query_heads, keys_local, preferred_element_type=jnp.float32)
        * score_scale
    )
    positions = jnp.arange(keys_local.shape[1], dtype=jnp.int32)
    valid_mask = positions[None, :] < cache_lens[:, None]
    cache_scores = jnp.where(valid_mask[:, None, None, None, :], cache_scores, masked_score)
    cache_max = jnp.max(cache_scores, axis=-1)
    new_entries = new_entries.reshape(step_total, rows_local, -1)
    fresh = new_entries.reshape(step_total, rows_local, kv_local, 2, HD)
    new_scores = (
        jnp.einsum(
            "srhgd,trhd->rhgst",
            query_heads,
            fresh[:, :, :, 0, :],
            preferred_element_type=jnp.float32,
        )
        * score_scale
    )
    order = jnp.arange(step_total, dtype=jnp.int32)
    causal_mask = order[:, None] >= order[None, :]
    new_scores = jnp.where(causal_mask, new_scores, masked_score)
    row_max = jnp.maximum(cache_max, jnp.max(new_scores, axis=-1))
    cache_exp = jnp.exp(cache_scores - row_max[..., None])
    new_exp = jnp.exp(new_scores - row_max[..., None])
    total = jnp.sum(cache_exp, axis=-1) + jnp.sum(new_exp, axis=-1)
    cache_probs = (cache_exp / total[..., None]).astype(jnp.bfloat16)
    new_probs = (new_exp / total[..., None]).astype(jnp.bfloat16)
    mixed = jnp.einsum(
        "rhgsc,rchd->srhgd", cache_probs, values_local, preferred_element_type=jnp.float32
    )
    mixed = mixed + jnp.einsum(
        "rhgst,trhd->srhgd", new_probs, fresh[:, :, :, 1, :], preferred_element_type=jnp.float32
    )
    attention = mixed.astype(jnp.bfloat16).reshape(step_total, rows_local, -1)
    return (new_weight, new_m, new_v, new_entries, attention)


def solution(mesh):
    return jax.shard_map(
        body,
        mesh=mesh,
        in_specs=(
            P("fsdp", ("tp", "dp")),
            P("fsdp", ("tp", "dp")),
            P("fsdp"),
            P("fsdp"),
            P("fsdp", ("tp", "dp")),
            P("fsdp", ("tp", "dp")),
            P("fsdp", ("tp", "dp")),
            P(None, ("fsdp", "dp"), None),
            P(None, ("fsdp", "dp"), "tp"),
            P(("fsdp", "dp"), None, "tp"),
            P(("fsdp", "dp"), None, "tp"),
            P(("fsdp", "dp")),
        ),
        out_specs=(
            P("fsdp", ("tp", "dp")),
            P("fsdp", ("tp", "dp")),
            P("fsdp", ("tp", "dp")),
            P(None, ("fsdp", "dp"), "tp"),
            P(None, ("fsdp", "dp"), "tp"),
        ),
        check_vma=False,
    )
```

```python
import jax
import jax.numpy as jnp
from jax import lax
from jax.experimental import pallas as pl
from jax.experimental.pallas import tpu as pltpu
from jax.sharding import PartitionSpec as P

HD = 128
LEN = 48
GSIZE = 8
X = 4
T = 4
Z = 8
TOK = 384
SEQ = 8
FEAT = 512
HALF = 256
COL = 128
STEPS = 4
DROWS = 24
ROWS = 96
CACHE = 64
QW = 2048
WIDTH = 8192
KSL = WIDTH // X

beta_one = 0.9
beta_two = 0.95
learn_rate = 0.001
decay_rate = 0.1
adam_eps = 1e-08
correct_one = 1.0 - beta_one**10
correct_two = 1.0 - beta_two**10
masked_score = -1e30

MESH = pl.DeviceIdType.MESH
F32 = jnp.float32
BF16 = jnp.bfloat16


def aligned(value, multiple):
    return pl.multiple_of(value * multiple, multiple)

NAMES = (
    "acts", "kv", "rew", "ids", "w_in", "m_in", "v_in", "hid", "qry", "ckey", "cval", "lens", "nw_out",
    "nm_out", "nv_out", "ent_out", "att_out", "abuf", "kbuf", "wt", "pbuf", "rsbuf", "own", "hv", "hl", "hb",
    "nwb", "wall", "acc", "part", "ebuf", "rbuf", "wv", "mv", "vv", "rs", "ls", "ns", "qv", "qb", "ck", "cv",
    "oc", "mc", "lc", "loc_sem", "a_send", "a_recv", "k_send", "k_recv", "r_send", "r_recv", "rs_send",
    "rs_recv", "o_send", "o_recv", "h_send", "h_recv", "c_send", "c_recv", "w_send", "w_recv", "e_send",
    "e_recv",
)


def kernel(*all_refs):
    refs = dict(zip(NAMES, all_refs))
    acts, kv, hid = refs["acts"], refs["kv"], refs["hid"]
    abuf, kbuf, wt, pbuf, rsbuf, own = (refs[k] for k in ("abuf", "kbuf", "wt", "pbuf", "rsbuf", "own"))
    hv, hl, hb, nwb, wall, acc = (refs[k] for k in ("hv", "hl", "hb", "nwb", "wall", "acc"))
    part, ebuf, rbuf, wv, mv, vv = (refs[k] for k in ("part", "ebuf", "rbuf", "wv", "mv", "vv"))
    qv, qb, ck, cv, oc, mc, lc = (refs[k] for k in ("qv", "qb", "ck", "cv", "oc", "mc", "lc"))
    loc_sem, a_send, a_recv, k_send, k_recv = (refs[k] for k in NAMES[NAMES.index("loc_sem") :][:5])
    r_send, r_recv, rs_send, rs_recv, o_send, o_recv = (refs[k] for k in NAMES[NAMES.index("r_send") :][:6])
    h_send, h_recv, c_send, c_recv = (refs[k] for k in NAMES[NAMES.index("h_send") :][:4])
    w_send, w_recv, e_send, e_recv = (refs[k] for k in NAMES[NAMES.index("w_send") :][:4])

    f, t, x = lax.axis_index("fsdp"), lax.axis_index("tp"), lax.axis_index("dp")
    z, g = lax.div(f, 4), lax.rem(f, 4)
    yh, c = lax.div(g, 2), lax.rem(g, 2)
    other, yo = 1 - c, 1 - yh

    def dev(z=z, yh=yh, c=c, t=t, x=x):
        return (z * 4 + yh * 2 + c, t, x)

    def copy(src, dst, send, recv, to):
        return pltpu.make_async_remote_copy(
            src_ref=src, dst_ref=dst, send_sem=send, recv_sem=recv, device_id=to, device_id_type=MESH
        )

    def arrived(dst, recv):
        copy(dst, dst, o_send.at[0], recv, dev(c=other)).wait_recv()

    def xs(step):
        return lax.rem(x + step + X, X)

    def zs(step):
        return lax.rem(z + step + Z, Z)

    def run_of(order):
        return jnp.bitwise_xor(jnp.bitwise_xor(t, order), 1)

    def half_of(src, slot):
        u = lax.rem(slot - 2 * t - lax.div(src, 2) + 2 * Z, Z)
        upper = jnp.where((u >= 1) & (u <= 4), 1, 0)
        return run_of(jnp.where(upper == 1, u - 1, lax.rem(Z - u, Z))), upper

    half = pl.ds(aligned(c, HALF), HALF)
    mine, other_rows = pl.ds(aligned(c, TOK), TOK), pl.ds(aligned(other, TOK), TOK)
    local = [
        pltpu.make_async_copy(src, dst, loc_sem.at[i])
        for i, (src, dst) in enumerate(
            (
                (refs["rew"], refs["rs"]),
                (refs["ids"], refs["ls"]),
                (kv, kbuf.at[t]),
                (refs["lens"], refs["ns"]),
                (refs["qry"], qv),
                (refs["ckey"], ck),
                (refs["cval"], cv),
                (acts.at[:, half], abuf.at[x, mine]),
                (hid, hv),
                (refs["w_in"], wv),
                (refs["m_in"], mv),
                (refs["v_in"], vv),
            )
        )
    ]
    for item in local:
        item.start()

    barrier = pltpu.get_barrier_semaphore()
    senders = [dev(z=zs(step)) for step in (4, 3, -3, 2, -2, 1, -1)]
    senders += [dev(yh=yo), dev(yh=yo, c=other)]
    senders += [dev(t=lax.rem(t + step, T)) for step in range(1, T)]
    senders += [dev(x=xs(step), c=core) for step in (1, -1) for core in range(2)]
    senders += [dev(c=other)]
    for sender in senders:
        pl.semaphore_signal(barrier, inc=1, device_id=sender, device_id_type=MESH)

    local[0].wait()
    local[1].wait()
    sub = lax.broadcasted_iota(jnp.int32, (8, 128), 0)
    lane = lax.broadcasted_iota(jnp.int32, (8, 128), 1)
    rew_row = jnp.full((8, 128), -1.0, F32)
    id_row = jnp.full((8, 128), -1, jnp.int32)
    for seq in range(SEQ):
        rew_row = jnp.where(lane == seq, refs["rs"][seq], rew_row)
        id_row = jnp.where(lane == seq, refs["ls"][seq], id_row)
    rbuf[g, z] = jnp.where(sub == 0, rew_row, id_row.astype(F32))

    pl.semaphore_wait(barrier, len(senders))

    sends = []

    def start(item):
        item.start()
        sends.append(item)

    for step, sign in ((0, 1 - 2 * c), (1, 2 * c - 1)):
        for core in range(2):
            start(
                copy(
                    acts.at[:, pl.ds(core * HALF, HALF)],
                    abuf.at[x, mine],
                    a_send.at[2 * step + core],
                    a_recv.at[x, c],
                    dev(x=xs(sign), c=core),
                )
            )
    for step in range(1, T):
        start(copy(kv, kbuf.at[t], k_send.at[step], k_recv.at[t], dev(t=lax.rem(t + step, T))))
    for step in range(1, Z):
        start(copy(rbuf.at[g, z], rbuf.at[g, z], r_send.at[step], r_recv.at[z], dev(z=zs(step))))
    start(
        copy(
            acts.at[:, pl.ds(aligned(other, HALF), HALF)],
            abuf.at[x, mine],
            a_send.at[4],
            a_recv.at[x, c],
            dev(c=other),
        )
    )

    for item in local[3:7]:
        item.wait()
    for h in range(2):
        tiles = [qv[:, (8 * h + j) * HD : (8 * h + j + 1) * HD].astype(F32) for j in range(8)]
        for G in range(3):
            rows = [tiles[j][s * DROWS + 8 * G : s * DROWS + 8 * G + 8] for j in range(8) for s in range(STEPS)]
            qb[h, G] = jnp.concatenate(rows, axis=0).astype(BF16)

    def cached(h, G):
        keys = ck[8 * G : 8 * G + 8, :, h * HD : (h + 1) * HD].reshape(8 * CACHE, HD)
        values = cv[8 * G : 8 * G + 8, :, h * HD : (h + 1) * HD].reshape(8 * CACHE, HD)
        scores = lax.dot_general(qb[h, G], keys, (((1,), (1,)), ((), ())), preferred_element_type=F32)
        scores *= HD ** (-0.5)
        column = lax.broadcasted_iota(jnp.int32, (1, 8 * CACHE), 1)
        limit = jnp.zeros((1, 8 * CACHE), jnp.int32)
        for row in range(8):
            limit = jnp.where(lax.div(column, CACHE) == row, refs["ns"][8 * G + row], limit)
        owner = jnp.where(lax.rem(column, CACHE) < limit, lax.div(column, CACHE), -1)
        row = lax.rem(lax.broadcasted_iota(jnp.int32, (256, 1), 0), 8)
        scores = jnp.where(row == owner, scores, masked_score)
        top = jnp.max(scores, axis=1, keepdims=True)
        weights = jnp.exp(scores - top)
        mc[h, G] = jnp.broadcast_to(top, (256, HD))
        lc[h, G] = jnp.broadcast_to(jnp.sum(weights, axis=1, keepdims=True), (256, HD))
        oc[h, G] = jnp.dot(weights.astype(BF16), values, preferred_element_type=F32)

    for step in range(1, Z):
        arrived(rbuf.at[g, zs(step)], r_recv.at[zs(step)])
    for step, (to_yh, to_c) in enumerate(((yh, other), (yo, c), (yo, other))):
        start(copy(rbuf.at[g], rbuf.at[g], r_send.at[Z + step], r_recv.at[Z + g], dev(yh=to_yh, c=to_c)))

    for G in range(3):
        cached(0, G)

    left, right, across = xs(-1), xs(1), xs(2)
    first, second = pl.ds(0, TOK), pl.ds(TOK, TOK)
    arrived(abuf.at[left, first], a_recv.at[left, 0])
    start(copy(abuf.at[left, first], abuf.at[left, first], a_send.at[5], a_recv.at[left, 0], dev(x=right)))
    arrived(abuf.at[right, second], a_recv.at[right, 1])
    start(copy(abuf.at[right, second], abuf.at[right, second], a_send.at[6], a_recv.at[right, 1], dev(x=left)))

    for to_yh, to_c in ((yh, other), (yo, c), (yo, other)):
        group = to_yh * 2 + to_c
        arrived(rbuf.at[group], r_recv.at[Z + group])
    slot = rbuf[g, z]
    rew_col = jnp.sum(jnp.where(sub == lane, slot[0:1, :], 0.0), axis=1, keepdims=True)
    id_col = jnp.sum(jnp.where(sub == lane, slot[1:2, :], 0.0), axis=1, keepdims=True)
    sums = jnp.zeros((8, 128), F32)
    for group in range(4):
        for zz in range(Z):
            sums += jnp.where(rbuf[group, zz, 1:2, :] == id_col, rbuf[group, zz, 0:1, :], 0.0)
    advantage = rew_col - jnp.sum(sums, axis=1, keepdims=True) / GSIZE

    def weigh(src, step):
        columns = [
            advantage[seq : seq + 1, 0:1] * kbuf[src, seq * LEN : (seq + 1) * LEN, :].astype(F32) for seq in range(SEQ)
        ]
        rows = pl.ds(aligned(src, COL), COL)
        wt[rows, mine] = jnp.concatenate(columns, axis=0).T.astype(BF16)
        start(copy(wt.at[rows, mine], wt.at[rows, mine], k_send.at[T + step], k_recv.at[T + src], dev(c=other)))

    local[2].wait()
    weigh(t, 0)
    cached(1, 0)
    for step in (1, 3, 2):
        src = jnp.bitwise_xor(t, step)
        arrived(kbuf.at[src], k_recv.at[src])
        weigh(src, step)
        if step != 2:
            cached(1, 1 + step // 2)

    local[8].wait()
    for q in range(WIDTH // FEAT):
        for to in range(X):
            hl[to, :, q * 128 : (q + 1) * 128] = hv[:, q * FEAT + to * 128 : q * FEAT + (to + 1) * 128]
    for src in range(T):
        arrived(wt.at[pl.ds(src * COL, COL), other_rows], k_recv.at[T + src])

    blocks = (x, left, right, across)
    ways = (1, -1)

    def hops(block, way):
        return Z // 2 if way == block % 2 else Z // 2 - 1

    def own_piece(block, slot):
        run, upper = half_of(blocks[block], slot)
        return pbuf.at[block, pl.ds(aligned(2 * run + upper, COL // 2), COL // 2)]

    def ring_copy(src, block, way, step):
        return copy(
            src,
            rsbuf.at[block, way, step],
            rs_send.at[block, way, step],
            rs_recv.at[block, way, step],
            dev(z=zs(ways[way])),
        )

    def multiply(block):
        pbuf[block] = jnp.dot(wt[...], abuf[blocks[block]], preferred_element_type=F32).astype(BF16)
        for way in range(2):
            start(ring_copy(own_piece(block, zs(ways[way] * hops(block, way))), block, way, 0))

    local[7].wait()
    arrived(abuf.at[x, other_rows], a_recv.at[x, other])
    multiply(0)
    arrived(abuf.at[left, second], a_recv.at[left, 1])
    multiply(1)
    arrived(abuf.at[right, first], a_recv.at[right, 0])
    multiply(2)
    arrived(abuf.at[across, first], a_recv.at[across, 0])
    arrived(abuf.at[across, second], a_recv.at[across, 1])
    multiply(3)

    hslot = hb.at[x * 2 + c]
    hid_local = pltpu.make_async_copy(hl.at[x], hslot, loc_sem.at[12])
    hid_local.start()
    for step in (1, -1, 2):
        start(copy(hl.at[xs(step)], hslot, h_send.at[step % X], h_recv.at[x, c], dev(x=xs(step))))
    start(copy(hl.at[x], hslot, h_send.at[0], h_recv.at[x, c], dev(c=other)))

    for step in range(Z // 2 - 1):
        for block in range(X):
            for way in range(2):
                if step + 1 < hops(block, way):
                    here = rsbuf.at[block, way, step]
                    arrived(here, rs_recv.at[block, way, step])
                    mine_too = own_piece(block, zs(ways[way] * (hops(block, way) - 1 - step)))
                    here[...] = (here[...].astype(F32) + mine_too[...].astype(F32)).astype(BF16)
                    start(ring_copy(here, block, way, step + 1))
    for block in range(X):
        total = own_piece(block, z)[...].astype(F32)
        for way in range(2):
            here = rsbuf.at[block, way, hops(block, way) - 1]
            arrived(here, rs_recv.at[block, way, hops(block, way) - 1])
            total += here[...].astype(F32)
        here = rsbuf.at[block, block % 2, Z // 2 - 1]
        here[...] = total.astype(BF16)
        src = blocks[block]
        run, upper = half_of(src, z)
        start(
            copy(
                here,
                own.at[yh, pl.ds(aligned(upper, COL // 2), COL // 2)],
                o_send.at[block],
                o_recv.at[yh, upper],
                dev(z=2 * t + lax.div(src, 2), yh=lax.rem(src, 2), t=run),
            )
        )

    for item in local[9:]:
        item.wait()
    for from_yh in range(2):
        for upper in range(2):
            arrived(own.at[from_yh, pl.ds(upper * COL // 2, COL // 2)], o_recv.at[from_yh, upper])
    weight_grad = (own[0].astype(F32) + own[1].astype(F32)).T / LEN
    new_m = beta_one * mv[...] + (1.0 - beta_one) * weight_grad
    new_v = beta_two * vv[...] + (1.0 - beta_two) * weight_grad * weight_grad
    weight_f = wv[...].astype(F32)
    direction = new_m / correct_one / (jnp.sqrt(new_v / correct_two) + adam_eps)
    new_weight = (weight_f - learn_rate * (direction + decay_rate * weight_f)).astype(BF16)
    nwb[...] = new_weight

    is_self = c == lax.div(x, 2)
    cols = pl.ds(aligned(lax.rem(x, 2), COL), COL)
    slices = []
    for r in range(2):
        src = nwb.at[pl.ds(r * COL, COL)]
        dst = wall.at[z * 2 + yh, :, cols]
        recv = c_recv.at[yh, lax.rem(x, 2)]
        near = copy(src, dst, c_send.at[r], recv, dev(c=lax.div(x, 2), x=2 * c + r))
        far = copy(src, dst, c_send.at[2 + r], recv, dev(yh=yo, c=lax.div(x, 2), x=2 * c + r))
        here = is_self & (lax.rem(x, 2) == r)
        pl.when(jnp.logical_not(here))(near.start)
        pl.when(here)(pltpu.make_async_copy(src, dst, recv).start)
        start(far)
        slices.append((here, near))

    refs["nw_out"][...] = new_weight
    refs["nm_out"][...] = new_m
    refs["nv_out"][...] = new_v

    pairs = (yh, yo)

    def pass_on(zz, k, part_of, way, step):
        slot = wall.at[zz * 2 + pairs[k], pl.ds(part_of * 64, 64)]
        sem = 2 * k + part_of
        start(copy(slot, slot, w_send.at[way, sem, step], w_recv.at[zz, sem], dev(z=zs(ways[way]))))

    for k in range(2):
        for hh in range(2):
            arrived(wall.at[z * 2 + pairs[k], :, pl.ds(hh * COL, COL)], c_recv.at[pairs[k], hh])
        for part_of in range(2):
            for way in range(2):
                pass_on(z, k, part_of, way, 0)

    for step in (1, -1, 2):
        slot = hb.at[xs(step) * 2 + c]
        arrived(slot, h_recv.at[xs(step), c])
        start(copy(slot, slot, h_send.at[X + step % X], h_recv.at[xs(step), c], dev(c=other)))
    hid_local.wait()
    for step in range(X):
        arrived(hb.at[xs(step) * 2 + other], h_recv.at[xs(step), other])

    def project(zz):
        rows = hb[:, :, pl.ds(aligned(zz, 2 * COL), 2 * COL)].reshape(2 * X * ROWS, 2 * COL)
        block = wall[pl.ds(zz * 2, 2)].reshape(2 * COL, 2 * COL)
        return jnp.dot(rows, block, preferred_element_type=F32)

    acc[...] = project(z)
    for step in range(1, Z // 2 + 1):
        for k in range(2):
            for part_of in range(2):
                for way in range(2):
                    if step == Z // 2 and way != k:
                        continue
                    zz = zs(-ways[way] * step)
                    sem = 2 * k + part_of
                    arrived(wall.at[zz * 2 + pairs[k], pl.ds(part_of * 64, 64)], w_recv.at[zz, sem])
                    if step < Z // 2 - 1 or (step == Z // 2 - 1 and way == k):
                        pass_on(zz, k, part_of, way, step)
        if step < Z // 2:
            acc[...] += project(zs(-step)) + project(zs(step))
    part[...] = (acc[...] + project(zs(Z // 2))).astype(BF16).reshape(2 * X, ROWS, 2 * HD)

    for step in (2, 1, -1, 0):
        for core in range(2):
            to_c = c if core == 0 else other
            if step == 0 and core == 0:
                ebuf[x, c] = part[x * 2 + c]
                continue
            start(
                copy(
                    part.at[xs(step) * 2 + to_c],
                    ebuf.at[x, c],
                    e_send.at[2 * (step % X) + core],
                    e_recv.at[x, c],
                    dev(x=xs(step), c=to_c),
                )
            )
    for step in (0, 1, -1, 2):
        for core in range(2):
            from_c = c if core == 0 else other
            if step == 0 and core == 0:
                continue
            arrived(ebuf.at[xs(step), from_c], e_recv.at[xs(step), from_c])

    row = lax.broadcasted_iota(jnp.int32, (256, 32), 0)
    column = lax.broadcasted_iota(jnp.int32, (256, 32), 1)
    seen = (lax.rem(row, 8) == lax.rem(column, 8)) & (lax.rem(lax.div(row, 8), STEPS) >= lax.div(column, 8))
    for h in range(2):
        total = ebuf[0, h].astype(F32)
        for src in range(1, X):
            total += ebuf[src, h].astype(F32)
        entries = total.astype(BF16)
        refs["ent_out"][:, h * 2 * HD : (h + 1) * 2 * HD] = entries
        fresh = entries.astype(F32)
        outs = []
        for G in range(3):
            rows = [fresh[s * DROWS + 8 * G : s * DROWS + 8 * G + 8] for s in range(STEPS)]
            new = jnp.concatenate(rows, axis=0).astype(BF16)
            scores = lax.dot_general(qb[h, G], new[:, :HD], (((1,), (1,)), ((), ())), preferred_element_type=F32)
            scores = jnp.where(seen, scores * HD ** (-0.5), masked_score)
            before = mc[h, G]
            top = jnp.maximum(before, jnp.max(scores, axis=1, keepdims=True))
            weights = jnp.exp(scores - top[:, :32])
            scale = jnp.exp(before - top)
            whole = lc[h, G] * scale + jnp.sum(weights, axis=1, keepdims=True)
            mixed = jnp.dot(weights.astype(BF16), new[:, HD:], preferred_element_type=F32)
            outs.append((oc[h, G] * scale + mixed) / whole)
        for j in range(8):
            rows = [
                outs[G][(j * STEPS + s) * 8 : (j * STEPS + s) * 8 + 8] for s in range(STEPS) for G in range(3)
            ]
            refs["att_out"][:, (8 * h + j) * HD : (8 * h + j + 1) * HD] = jnp.concatenate(rows, axis=0).astype(BF16)

    for item in sends:
        item.wait_send()
    for here, near in slices:
        pl.when(jnp.logical_not(here))(near.wait_send)


OUT_SHAPES = (
    jax.ShapeDtypeStruct((HALF, COL), BF16),
    jax.ShapeDtypeStruct((HALF, COL), F32),
    jax.ShapeDtypeStruct((HALF, COL), F32),
    jax.ShapeDtypeStruct((ROWS, 4 * HD), BF16),
    jax.ShapeDtypeStruct((ROWS, QW), BF16),
)


def write_out(*refs):
    count = len(OUT_SHAPES)
    for i in range(count):
        refs[count + i][...] = refs[i][...]


def body(
    acts,
    kv_grad,
    rewards,
    group_ids,
    kv_weight,
    adam_m,
    adam_v,
    hidden,
    queries,
    cache_keys,
    cache_values,
    cache_lens,
):
    hbm = pl.BlockSpec(memory_space=pltpu.HBM)
    vmem = pl.BlockSpec(memory_space=pltpu.VMEM)
    dma = pltpu.SemaphoreType.DMA
    results = pl.pallas_call(
        kernel,
        out_shape=OUT_SHAPES,
        in_specs=[hbm] * 12,
        out_specs=(vmem,) * 5,
        scratch_shapes=[
            pltpu.VMEM((X, 2 * TOK, HALF), BF16),
            pltpu.VMEM((T, TOK, COL), BF16),
            pltpu.VMEM((T * COL, 2 * TOK), BF16),
            pltpu.VMEM((X, T * COL, HALF), BF16),
            pltpu.VMEM((X, 2, Z // 2, COL // 2, HALF), BF16),
            pltpu.VMEM((2, COL, HALF), BF16),
            pltpu.VMEM((ROWS, WIDTH), BF16),
            pltpu.VMEM((X, ROWS, KSL), BF16),
            pltpu.VMEM((2 * X, ROWS, KSL), BF16),
            pltpu.VMEM((HALF, COL), BF16),
            pltpu.VMEM((2 * Z, COL, 2 * COL), BF16),
            pltpu.VMEM((2 * X * ROWS, 2 * COL), F32),
            pltpu.VMEM((2 * X, ROWS, 2 * COL), BF16),
            pltpu.VMEM((X, 2, ROWS, 2 * COL), BF16),
            pltpu.VMEM((4, Z, 8, 128), F32),
            pltpu.VMEM((HALF, COL), BF16),
            pltpu.VMEM((HALF, COL), F32),
            pltpu.VMEM((HALF, COL), F32),
            pltpu.SMEM((SEQ,), F32),
            pltpu.SMEM((SEQ,), jnp.int32),
            pltpu.SMEM((DROWS,), jnp.int32),
            pltpu.VMEM((ROWS, QW), BF16),
            pltpu.VMEM((2, 3, 256, HD), BF16),
            pltpu.VMEM((DROWS, CACHE, 2 * HD), BF16),
            pltpu.VMEM((DROWS, CACHE, 2 * HD), BF16),
            pltpu.VMEM((2, 3, 256, HD), F32),
            pltpu.VMEM((2, 3, 256, HD), F32),
            pltpu.VMEM((2, 3, 256, HD), F32),
            dma((13,)),
            dma((7,)),
            dma((X, 2)),
            dma((2 * T,)),
            dma((2 * T,)),
            dma((Z + 3,)),
            dma((Z + 4,)),
            dma((X, 2, Z // 2)),
            dma((X, 2, Z // 2)),
            dma((X,)),
            dma((2, 2)),
            dma((2 * X,)),
            dma((X, 2)),
            dma((4,)),
            dma((2, 2)),
            dma((2, 4, Z // 2)),
            dma((Z, 4)),
            dma((2 * X,)),
            dma((X, 2)),
        ],
        compiler_params=pltpu.CompilerParams(
            collective_id=0, has_side_effects=True, vmem_limit_bytes=63400000
        ),
        name="update_and_decode",
    )(
        acts,
        kv_grad,
        rewards,
        group_ids,
        kv_weight,
        adam_m,
        adam_v,
        hidden.reshape(ROWS, WIDTH),
        queries.reshape(ROWS, QW),
        cache_keys,
        cache_values,
        cache_lens,
    )
    new_weight, new_m, new_v, new_entries, attention = pl.pallas_call(
        write_out,
        out_shape=OUT_SHAPES,
        in_specs=[vmem] * 5,
        out_specs=(vmem,) * 5,
        name="write_out",
    )(*results)
    return (
        new_weight,
        new_m,
        new_v,
        new_entries.reshape(STEPS, DROWS, 4 * HD),
        attention.reshape(STEPS, DROWS, QW),
    )


def solution(mesh):
    return jax.shard_map(
        body,
        mesh=mesh,
        in_specs=(
            P("fsdp", ("tp", "dp")),
            P("fsdp", ("tp", "dp")),
            P("fsdp"),
            P("fsdp"),
            P("fsdp", ("tp", "dp")),
            P("fsdp", ("tp", "dp")),
            P("fsdp", ("tp", "dp")),
            P(None, ("fsdp", "dp"), None),
            P(None, ("fsdp", "dp"), "tp"),
            P(("fsdp", "dp"), None, "tp"),
            P(("fsdp", "dp"), None, "tp"),
            P(("fsdp", "dp")),
        ),
        out_specs=(
            P("fsdp", ("tp", "dp")),
            P("fsdp", ("tp", "dp")),
            P("fsdp", ("tp", "dp")),
            P(None, ("fsdp", "dp"), "tp"),
            P(None, ("fsdp", "dp"), "tp"),
        ),
        check_vma=False,
    )
```

```python
import jax
import jax.numpy as jnp
from jax import lax
from jax.experimental import pallas as pl
from jax.experimental.pallas import tpu as pltpu
from jax.sharding import PartitionSpec as P

HD = 128
LEN = 48
GSIZE = 8
X = 4
T = 4
Z = 8
TOK = 384
SEQ = 8
FEAT = 512
HALF = 256
COL = 128
STEPS = 4
DROWS = 24
ROWS = 96
CACHE = 64
QW = 2048
WIDTH = 8192
KSL = WIDTH // X

beta_one = 0.9
beta_two = 0.95
learn_rate = 0.001
decay_rate = 0.1
adam_eps = 1e-08
correct_one = 1.0 - beta_one**10
correct_two = 1.0 - beta_two**10
masked_score = -1e30

MESH = pl.DeviceIdType.MESH
F32 = jnp.float32
BF16 = jnp.bfloat16


def aligned(value, multiple):
    return pl.multiple_of(value * multiple, multiple)

NAMES = (
    "acts", "kv", "rew", "ids", "w_in", "m_in", "v_in", "hid", "qry", "ckey", "cval", "lens", "nw_out",
    "nm_out", "nv_out", "ent_out", "att_out", "abuf", "kbuf", "wt", "pbuf", "rsbuf", "own", "hv", "hl", "hb",
    "nwb", "wall", "acc", "part", "ebuf", "rbuf", "wv", "mv", "vv", "rs", "ls", "ns", "qv", "qb", "ck", "cv",
    "oc", "mc", "lc", "loc_sem", "a_send", "a_recv", "k_send", "k_recv", "r_send", "r_recv", "rs_send",
    "rs_recv", "o_send", "o_recv", "h_send", "h_recv", "c_send", "c_recv", "w_send", "w_recv", "e_send",
    "e_recv",
)


def kernel(*all_refs):
    refs = dict(zip(NAMES, all_refs))
    acts, kv, hid = refs["acts"], refs["kv"], refs["hid"]
    abuf, kbuf, wt, pbuf, rsbuf, own = (refs[k] for k in ("abuf", "kbuf", "wt", "pbuf", "rsbuf", "own"))
    hv, hl, hb, nwb, wall, acc = (refs[k] for k in ("hv", "hl", "hb", "nwb", "wall", "acc"))
    part, ebuf, rbuf, wv, mv, vv = (refs[k] for k in ("part", "ebuf", "rbuf", "wv", "mv", "vv"))
    qv, qb, ck, cv, oc, mc, lc = (refs[k] for k in ("qv", "qb", "ck", "cv", "oc", "mc", "lc"))
    loc_sem, a_send, a_recv, k_send, k_recv = (refs[k] for k in NAMES[NAMES.index("loc_sem") :][:5])
    r_send, r_recv, rs_send, rs_recv, o_send, o_recv = (refs[k] for k in NAMES[NAMES.index("r_send") :][:6])
    h_send, h_recv, c_send, c_recv = (refs[k] for k in NAMES[NAMES.index("h_send") :][:4])
    w_send, w_recv, e_send, e_recv = (refs[k] for k in NAMES[NAMES.index("w_send") :][:4])

    f, t, x = lax.axis_index("fsdp"), lax.axis_index("tp"), lax.axis_index("dp")
    z, g = lax.div(f, 4), lax.rem(f, 4)
    yh, c = lax.div(g, 2), lax.rem(g, 2)
    other, yo = 1 - c, 1 - yh

    def dev(z=z, yh=yh, c=c, t=t, x=x):
        return (z * 4 + yh * 2 + c, t, x)

    def copy(src, dst, send, recv, to):
        return pltpu.make_async_remote_copy(
            src_ref=src, dst_ref=dst, send_sem=send, recv_sem=recv, device_id=to, device_id_type=MESH
        )

    def arrived(dst, recv):
        copy(dst, dst, o_send.at[0], recv, dev(c=other)).wait_recv()

    def xs(step):
        return lax.rem(x + step + X, X)

    def zs(step):
        return lax.rem(z + step + Z, Z)

    def run_of(order):
        return jnp.bitwise_xor(jnp.bitwise_xor(t, order), 1)

    def half_of(src, slot):
        u = lax.rem(slot - 2 * t - lax.div(src, 2) + 2 * Z, Z)
        upper = jnp.where((u >= 1) & (u <= 4), 1, 0)
        return run_of(jnp.where(upper == 1, u - 1, lax.rem(Z - u, Z))), upper

    half = pl.ds(aligned(c, HALF), HALF)
    mine, other_rows = pl.ds(aligned(c, TOK), TOK), pl.ds(aligned(other, TOK), TOK)
    local = [
        pltpu.make_async_copy(src, dst, loc_sem.at[i])
        for i, (src, dst) in enumerate(
            (
                (refs["rew"], refs["rs"]),
                (refs["ids"], refs["ls"]),
                (kv, kbuf.at[t]),
                (refs["lens"], refs["ns"]),
                (refs["qry"], qv),
                (refs["ckey"], ck),
                (refs["cval"], cv),
                (acts.at[:, half], abuf.at[x, mine]),
                (hid, hv),
                (refs["w_in"], wv),
                (refs["m_in"], mv),
                (refs["v_in"], vv),
            )
        )
    ]
    for item in local[:2]:
        item.start()

    barrier = pltpu.get_barrier_semaphore()
    senders = [dev(z=zs(step)) for step in (4, 3, -3, 2, -2, 1, -1)]
    senders += [dev(yh=yo), dev(yh=yo, c=other)]
    senders += [dev(t=lax.rem(t + step, T)) for step in range(1, T)]
    senders += [dev(x=xs(step), c=core) for step in (1, -1) for core in range(2)]
    senders += [dev(c=other)]
    for sender in senders:
        pl.semaphore_signal(barrier, inc=1, device_id=sender, device_id_type=MESH)

    pl.semaphore_wait(barrier, len(senders))

    sends = []

    def start(item):
        item.start()
        sends.append(item)

    for step, sign in ((0, 1 - 2 * c), (1, 2 * c - 1)):
        for core in range(2):
            start(
                copy(
                    acts.at[:, pl.ds(core * HALF, HALF)],
                    abuf.at[x, mine],
                    a_send.at[2 * step + core],
                    a_recv.at[x, c],
                    dev(x=xs(sign), c=core),
                )
            )
    for step in range(1, T):
        start(copy(kv, kbuf.at[t], k_send.at[step], k_recv.at[t], dev(t=lax.rem(t + step, T))))
    start(
        copy(
            acts.at[:, pl.ds(aligned(other, HALF), HALF)],
            abuf.at[x, mine],
            a_send.at[4],
            a_recv.at[x, c],
            dev(c=other),
        )
    )

    local[0].wait()
    local[1].wait()
    sub = lax.broadcasted_iota(jnp.int32, (8, 128), 0)
    lane = lax.broadcasted_iota(jnp.int32, (8, 128), 1)
    rew_row = jnp.full((8, 128), -1.0, F32)
    id_row = jnp.full((8, 128), -1, jnp.int32)
    for seq in range(SEQ):
        rew_row = jnp.where(lane == seq, refs["rs"][seq], rew_row)
        id_row = jnp.where(lane == seq, refs["ls"][seq], id_row)
    rbuf[g, z] = jnp.where(sub == 0, rew_row, id_row.astype(F32))

    for step in range(1, Z):
        start(copy(rbuf.at[g, z], rbuf.at[g, z], r_send.at[step], r_recv.at[z], dev(z=zs(step))))
    for item in local[2:]:
        item.start()

    def cached(h, G):
        keys = ck[8 * G : 8 * G + 8, :, h * HD : (h + 1) * HD].reshape(8 * CACHE, HD)
        values = cv[8 * G : 8 * G + 8, :, h * HD : (h + 1) * HD].reshape(8 * CACHE, HD)
        scores = lax.dot_general(qb[h, G], keys, (((1,), (1,)), ((), ())), preferred_element_type=F32)
        scores *= HD ** (-0.5)
        column = lax.broadcasted_iota(jnp.int32, (1, 8 * CACHE), 1)
        limit = jnp.zeros((1, 8 * CACHE), jnp.int32)
        for row in range(8):
            limit = jnp.where(lax.div(column, CACHE) == row, refs["ns"][8 * G + row], limit)
        owner = jnp.where(lax.rem(column, CACHE) < limit, lax.div(column, CACHE), -1)
        row = lax.rem(lax.broadcasted_iota(jnp.int32, (256, 1), 0), 8)
        scores = jnp.where(row == owner, scores, masked_score)
        top = jnp.max(scores, axis=1, keepdims=True)
        weights = jnp.exp(scores - top)
        mc[h, G] = jnp.broadcast_to(top, (256, HD))
        lc[h, G] = jnp.broadcast_to(jnp.sum(weights, axis=1, keepdims=True), (256, HD))
        oc[h, G] = jnp.dot(weights.astype(BF16), values, preferred_element_type=F32)

    for step in range(1, Z):
        arrived(rbuf.at[g, zs(step)], r_recv.at[zs(step)])
    for step, (to_yh, to_c) in enumerate(((yh, other), (yo, c), (yo, other))):
        start(copy(rbuf.at[g], rbuf.at[g], r_send.at[Z + step], r_recv.at[Z + g], dev(yh=to_yh, c=to_c)))

    left, right, across = xs(-1), xs(1), xs(2)
    first, second = pl.ds(0, TOK), pl.ds(TOK, TOK)
    arrived(abuf.at[left, first], a_recv.at[left, 0])
    start(copy(abuf.at[left, first], abuf.at[left, first], a_send.at[5], a_recv.at[left, 0], dev(x=right)))
    arrived(abuf.at[right, second], a_recv.at[right, 1])
    start(copy(abuf.at[right, second], abuf.at[right, second], a_send.at[6], a_recv.at[right, 1], dev(x=left)))

    for to_yh, to_c in ((yh, other), (yo, c), (yo, other)):
        group = to_yh * 2 + to_c
        arrived(rbuf.at[group], r_recv.at[Z + group])
    slot = rbuf[g, z]
    rew_col = jnp.sum(jnp.where(sub == lane, slot[0:1, :], 0.0), axis=1, keepdims=True)
    id_col = jnp.sum(jnp.where(sub == lane, slot[1:2, :], 0.0), axis=1, keepdims=True)
    sums = jnp.zeros((8, 128), F32)
    for group in range(4):
        for zz in range(Z):
            sums += jnp.where(rbuf[group, zz, 1:2, :] == id_col, rbuf[group, zz, 0:1, :], 0.0)
    advantage = rew_col - jnp.sum(sums, axis=1, keepdims=True) / GSIZE

    def weigh(src, step):
        columns = [
            advantage[seq : seq + 1, 0:1] * kbuf[src, seq * LEN : (seq + 1) * LEN, :].astype(F32) for seq in range(SEQ)
        ]
        rows = pl.ds(aligned(src, COL), COL)
        wt[rows, mine] = jnp.concatenate(columns, axis=0).T.astype(BF16)
        start(copy(wt.at[rows, mine], wt.at[rows, mine], k_send.at[T + step], k_recv.at[T + src], dev(c=other)))

    local[2].wait()
    weigh(t, 0)
    for step in (1, 3, 2):
        src = jnp.bitwise_xor(t, step)
        arrived(kbuf.at[src], k_recv.at[src])
        weigh(src, step)

    for src in range(T):
        arrived(wt.at[pl.ds(src * COL, COL), other_rows], k_recv.at[T + src])

    blocks = (x, left, right, across)
    ways = (1, -1)

    last = Z // 2 - 1

    def far_way(block):
        return block % 2

    def own_piece(block, slot):
        run, upper = half_of(blocks[block], slot)
        return pbuf.at[block, pl.ds(aligned(2 * run + upper, COL // 2), COL // 2)]

    def ring_copy(src, block, way, step, jump=1):
        return copy(
            src,
            rsbuf.at[block, way, step],
            rs_send.at[block, way, step],
            rs_recv.at[block, way, step],
            dev(z=zs(ways[way] * jump)),
        )

    def multiply(block):
        pbuf[block] = jnp.dot(wt[...], abuf[blocks[block]], preferred_element_type=F32).astype(BF16)
        start(ring_copy(own_piece(block, zs(Z // 2)), block, far_way(block), last, 2))
        for way in range(2):
            start(ring_copy(own_piece(block, zs(ways[way] * last)), block, way, 0))

    local[7].wait()
    arrived(abuf.at[x, other_rows], a_recv.at[x, other])
    multiply(0)
    arrived(abuf.at[left, second], a_recv.at[left, 1])
    multiply(1)
    arrived(abuf.at[right, first], a_recv.at[right, 0])
    multiply(2)
    arrived(abuf.at[across, first], a_recv.at[across, 0])
    arrived(abuf.at[across, second], a_recv.at[across, 1])
    multiply(3)

    local[8].wait()
    for q in range(WIDTH // FEAT):
        for to in range(X):
            hl[to, :, q * 128 : (q + 1) * 128] = hv[:, q * FEAT + to * 128 : q * FEAT + (to + 1) * 128]

    hslot = hb.at[x * 2 + c]
    hid_local = pltpu.make_async_copy(hl.at[x], hslot, loc_sem.at[12])
    hid_local.start()
    for step in (1, -1, 2):
        start(copy(hl.at[xs(step)], hslot, h_send.at[step % X], h_recv.at[x, c], dev(x=xs(step))))
    start(copy(hl.at[x], hslot, h_send.at[0], h_recv.at[x, c], dev(c=other)))

    for step in range(last - 1):
        for block in range(X):
            for way in range(2):
                here = rsbuf.at[block, way, step]
                arrived(here, rs_recv.at[block, way, step])
                total = here[...].astype(F32) + own_piece(block, zs(ways[way] * (last - 1 - step)))[...].astype(F32)
                if step == 0 and way == far_way(block):
                    arrived(rsbuf.at[block, way, last], rs_recv.at[block, way, last])
                    total += rsbuf[block, way, last].astype(F32)
                here[...] = total.astype(BF16)
                start(ring_copy(here, block, way, step + 1))
    for block in range(X):
        total = own_piece(block, z)[...].astype(F32)
        for way in range(2):
            here = rsbuf.at[block, way, last - 1]
            arrived(here, rs_recv.at[block, way, last - 1])
            total += here[...].astype(F32)
        here = rsbuf.at[block, 1 - far_way(block), last]
        here[...] = total.astype(BF16)
        src = blocks[block]
        run, upper = half_of(src, z)
        start(
            copy(
                here,
                own.at[yh, pl.ds(aligned(upper, COL // 2), COL // 2)],
                o_send.at[block],
                o_recv.at[yh, upper],
                dev(z=2 * t + lax.div(src, 2), yh=lax.rem(src, 2), t=run),
            )
        )

    for item in local[3:7]:
        item.wait()
    for h in range(2):
        tiles = [qv[:, (8 * h + j) * HD : (8 * h + j + 1) * HD].astype(F32) for j in range(8)]
        for G in range(3):
            rows = [tiles[j][s * DROWS + 8 * G : s * DROWS + 8 * G + 8] for j in range(8) for s in range(STEPS)]
            qb[h, G] = jnp.concatenate(rows, axis=0).astype(BF16)

    for G in range(3):
        cached(0, G)
    cached(1, 0)

    for item in local[9:]:
        item.wait()
    for from_yh in range(2):
        for upper in range(2):
            arrived(own.at[from_yh, pl.ds(upper * COL // 2, COL // 2)], o_recv.at[from_yh, upper])
    weight_grad = (own[0].astype(F32) + own[1].astype(F32)).T / LEN
    new_m = beta_one * mv[...] + (1.0 - beta_one) * weight_grad
    new_v = beta_two * vv[...] + (1.0 - beta_two) * weight_grad * weight_grad
    weight_f = wv[...].astype(F32)
    direction = new_m / correct_one / (jnp.sqrt(new_v / correct_two) + adam_eps)
    new_weight = (weight_f - learn_rate * (direction + decay_rate * weight_f)).astype(BF16)
    nwb[...] = new_weight

    is_self = c == lax.div(x, 2)
    cols = pl.ds(aligned(lax.rem(x, 2), COL), COL)
    slices = []
    for r in range(2):
        src = nwb.at[pl.ds(r * COL, COL)]
        dst = wall.at[z * 2 + yh, :, cols]
        recv = c_recv.at[yh, lax.rem(x, 2)]
        near = copy(src, dst, c_send.at[r], recv, dev(c=lax.div(x, 2), x=2 * c + r))
        far = copy(src, dst, c_send.at[2 + r], recv, dev(yh=yo, c=lax.div(x, 2), x=2 * c + r))
        here = is_self & (lax.rem(x, 2) == r)
        pl.when(jnp.logical_not(here))(near.start)
        pl.when(here)(pltpu.make_async_copy(src, dst, recv).start)
        start(far)
        slices.append((here, near))

    cached(1, 1)
    cached(1, 2)
    refs["nw_out"][...] = new_weight
    refs["nm_out"][...] = new_m
    refs["nv_out"][...] = new_v

    pairs = (yh, yo)

    def pass_on(zz, k, part_of, way, step, jump=1):
        slot = wall.at[zz * 2 + pairs[k], pl.ds(part_of * 64, 64)]
        sem = 2 * k + part_of
        to = dev(z=zs(ways[way] * jump))
        start(copy(slot, slot, w_send.at[way, sem, step], w_recv.at[zz, sem], to))

    for k in range(2):
        for hh in range(2):
            arrived(wall.at[z * 2 + pairs[k], :, pl.ds(hh * COL, COL)], c_recv.at[pairs[k], hh])
        for part_of in range(2):
            for way in range(2):
                pass_on(z, k, part_of, way, 0)

    for step in (1, -1, 2):
        slot = hb.at[xs(step) * 2 + c]
        arrived(slot, h_recv.at[xs(step), c])
        start(copy(slot, slot, h_send.at[X + step % X], h_recv.at[xs(step), c], dev(c=other)))
    hid_local.wait()
    for step in range(X):
        arrived(hb.at[xs(step) * 2 + other], h_recv.at[xs(step), other])

    def project(zz):
        rows = hb[:, :, pl.ds(aligned(zz, 2 * COL), 2 * COL)].reshape(2 * X * ROWS, 2 * COL)
        block = wall[pl.ds(zz * 2, 2)].reshape(2 * COL, 2 * COL)
        return jnp.dot(rows, block, preferred_element_type=F32)

    acc[...] = project(z)
    for step in range(1, Z // 2 + 1):
        for k in range(2):
            for part_of in range(2):
                for way in range(2):
                    if step == Z // 2 and way != k:
                        continue
                    zz = zs(-ways[way] * step)
                    sem = 2 * k + part_of
                    arrived(wall.at[zz * 2 + pairs[k], pl.ds(part_of * 64, 64)], w_recv.at[zz, sem])
                    if step == last - 1 and way == k:
                        pass_on(zz, k, part_of, way, last, 2)
                    if step < last:
                        pass_on(zz, k, part_of, way, step)
        if step < Z // 2:
            acc[...] += project(zs(-step)) + project(zs(step))

    early = list(sends)
    far = zs(Z // 2)
    far_cols = pl.ds(aligned(far, 2 * COL), 2 * COL)
    far_block = wall[pl.ds(far * 2, 2)].reshape(2 * COL, 2 * COL)
    for step in (2, 1, -1, 0):
        to = xs(step)
        rows = hb[pl.ds(to * 2, 2), :, far_cols].reshape(2 * ROWS, 2 * COL)
        sums = acc[pl.ds(aligned(to, 2 * ROWS), 2 * ROWS), :] + jnp.dot(rows, far_block, preferred_element_type=F32)
        part[pl.ds(to * 2, 2)] = sums.astype(BF16).reshape(2, ROWS, 2 * HD)
        for core in range(2):
            to_c = c if core == 0 else other
            if step == 0 and core == 0:
                ebuf[x, c] = part[x * 2 + c]
                continue
            start(
                copy(
                    part.at[to * 2 + to_c],
                    ebuf.at[x, c],
                    e_send.at[2 * (step % X) + core],
                    e_recv.at[x, c],
                    dev(x=to, c=to_c),
                )
            )
    for item in early:
        item.wait_send()
    for here, near in slices:
        pl.when(jnp.logical_not(here))(near.wait_send)
    for step in (0, 1, -1, 2):
        for core in range(2):
            from_c = c if core == 0 else other
            if step == 0 and core == 0:
                continue
            arrived(ebuf.at[xs(step), from_c], e_recv.at[xs(step), from_c])

    row = lax.broadcasted_iota(jnp.int32, (256, 32), 0)
    column = lax.broadcasted_iota(jnp.int32, (256, 32), 1)
    seen = (lax.rem(row, 8) == lax.rem(column, 8)) & (lax.rem(lax.div(row, 8), STEPS) >= lax.div(column, 8))
    for h in range(2):
        total = ebuf[0, h].astype(F32)
        for src in range(1, X):
            total += ebuf[src, h].astype(F32)
        entries = total.astype(BF16)
        refs["ent_out"][:, h * 2 * HD : (h + 1) * 2 * HD] = entries
        fresh = entries.astype(F32)
        outs = []
        for G in range(3):
            rows = [fresh[s * DROWS + 8 * G : s * DROWS + 8 * G + 8] for s in range(STEPS)]
            new = jnp.concatenate(rows, axis=0).astype(BF16)
            scores = lax.dot_general(qb[h, G], new[:, :HD], (((1,), (1,)), ((), ())), preferred_element_type=F32)
            scores = jnp.where(seen, scores * HD ** (-0.5), masked_score)
            before = mc[h, G]
            top = jnp.maximum(before, jnp.max(scores, axis=1, keepdims=True))
            weights = jnp.exp(scores - top[:, :32])
            scale = jnp.exp(before - top)
            whole = lc[h, G] * scale + jnp.sum(weights, axis=1, keepdims=True)
            mixed = jnp.dot(weights.astype(BF16), new[:, HD:], preferred_element_type=F32)
            outs.append((oc[h, G] * scale + mixed) / whole)
        for j in range(8):
            rows = [
                outs[G][(j * STEPS + s) * 8 : (j * STEPS + s) * 8 + 8] for s in range(STEPS) for G in range(3)
            ]
            refs["att_out"][:, (8 * h + j) * HD : (8 * h + j + 1) * HD] = jnp.concatenate(rows, axis=0).astype(BF16)

    for item in sends[len(early) :]:
        item.wait_send()


OUT_SHAPES = (
    jax.ShapeDtypeStruct((HALF, COL), BF16),
    jax.ShapeDtypeStruct((HALF, COL), F32),
    jax.ShapeDtypeStruct((HALF, COL), F32),
    jax.ShapeDtypeStruct((ROWS, 4 * HD), BF16),
    jax.ShapeDtypeStruct((ROWS, QW), BF16),
)


def write_out(*refs):
    count = len(OUT_SHAPES)
    for i in range(count):
        refs[count + i][...] = refs[i][...]


def body(
    acts,
    kv_grad,
    rewards,
    group_ids,
    kv_weight,
    adam_m,
    adam_v,
    hidden,
    queries,
    cache_keys,
    cache_values,
    cache_lens,
):
    hbm = pl.BlockSpec(memory_space=pltpu.HBM)
    vmem = pl.BlockSpec(memory_space=pltpu.VMEM)
    dma = pltpu.SemaphoreType.DMA
    results = pl.pallas_call(
        kernel,
        out_shape=OUT_SHAPES,
        in_specs=[hbm] * 12,
        out_specs=(vmem,) * 5,
        scratch_shapes=[
            pltpu.VMEM((X, 2 * TOK, HALF), BF16),
            pltpu.VMEM((T, TOK, COL), BF16),
            pltpu.VMEM((T * COL, 2 * TOK), BF16),
            pltpu.VMEM((X, T * COL, HALF), BF16),
            pltpu.VMEM((X, 2, Z // 2, COL // 2, HALF), BF16),
            pltpu.VMEM((2, COL, HALF), BF16),
            pltpu.VMEM((ROWS, WIDTH), BF16),
            pltpu.VMEM((X, ROWS, KSL), BF16),
            pltpu.VMEM((2 * X, ROWS, KSL), BF16),
            pltpu.VMEM((HALF, COL), BF16),
            pltpu.VMEM((2 * Z, COL, 2 * COL), BF16),
            pltpu.VMEM((2 * X * ROWS, 2 * COL), F32),
            pltpu.VMEM((2 * X, ROWS, 2 * COL), BF16),
            pltpu.VMEM((X, 2, ROWS, 2 * COL), BF16),
            pltpu.VMEM((4, Z, 8, 128), F32),
            pltpu.VMEM((HALF, COL), BF16),
            pltpu.VMEM((HALF, COL), F32),
            pltpu.VMEM((HALF, COL), F32),
            pltpu.SMEM((SEQ,), F32),
            pltpu.SMEM((SEQ,), jnp.int32),
            pltpu.SMEM((DROWS,), jnp.int32),
            pltpu.VMEM((ROWS, QW), BF16),
            pltpu.VMEM((2, 3, 256, HD), BF16),
            pltpu.VMEM((DROWS, CACHE, 2 * HD), BF16),
            pltpu.VMEM((DROWS, CACHE, 2 * HD), BF16),
            pltpu.VMEM((2, 3, 256, HD), F32),
            pltpu.VMEM((2, 3, 256, HD), F32),
            pltpu.VMEM((2, 3, 256, HD), F32),
            dma((13,)),
            dma((7,)),
            dma((X, 2)),
            dma((2 * T,)),
            dma((2 * T,)),
            dma((Z + 3,)),
            dma((Z + 4,)),
            dma((X, 2, Z // 2)),
            dma((X, 2, Z // 2)),
            dma((X,)),
            dma((2, 2)),
            dma((2 * X,)),
            dma((X, 2)),
            dma((4,)),
            dma((2, 2)),
            dma((2, 4, Z // 2)),
            dma((Z, 4)),
            dma((2 * X,)),
            dma((X, 2)),
        ],
        compiler_params=pltpu.CompilerParams(
            collective_id=0, has_side_effects=True, vmem_limit_bytes=63400000
        ),
        name="update_and_decode",
    )(
        acts,
        kv_grad,
        rewards,
        group_ids,
        kv_weight,
        adam_m,
        adam_v,
        hidden.reshape(ROWS, WIDTH),
        queries.reshape(ROWS, QW),
        cache_keys,
        cache_values,
        cache_lens,
    )
    new_weight, new_m, new_v, new_entries, attention = pl.pallas_call(
        write_out,
        out_shape=OUT_SHAPES,
        in_specs=[vmem] * 5,
        out_specs=(vmem,) * 5,
        name="write_out",
    )(*results)
    return (
        new_weight,
        new_m,
        new_v,
        new_entries.reshape(STEPS, DROWS, 4 * HD),
        attention.reshape(STEPS, DROWS, QW),
    )


def solution(mesh):
    return jax.shard_map(
        body,
        mesh=mesh,
        in_specs=(
            P("fsdp", ("tp", "dp")),
            P("fsdp", ("tp", "dp")),
            P("fsdp"),
            P("fsdp"),
            P("fsdp", ("tp", "dp")),
            P("fsdp", ("tp", "dp")),
            P("fsdp", ("tp", "dp")),
            P(None, ("fsdp", "dp"), None),
            P(None, ("fsdp", "dp"), "tp"),
            P(("fsdp", "dp"), None, "tp"),
            P(("fsdp", "dp"), None, "tp"),
            P(("fsdp", "dp")),
        ),
        out_specs=(
            P("fsdp", ("tp", "dp")),
            P("fsdp", ("tp", "dp")),
            P("fsdp", ("tp", "dp")),
            P(None, ("fsdp", "dp"), "tp"),
            P(None, ("fsdp", "dp"), "tp"),
        ),
        check_vma=False,
    )
```

```python
import jax
import jax.numpy as jnp
from jax import lax
from jax.experimental import pallas as pl
from jax.experimental.pallas import tpu as pltpu
from jax.sharding import PartitionSpec as P

HD = 128
LEN = 48
GSIZE = 8
X = 4
T = 4
Z = 8
TOK = 384
SEQ = 8
FEAT = 512
HALF = 256
COL = 128
STEPS = 4
DROWS = 24
ROWS = 96
CACHE = 64
QW = 2048
WIDTH = 8192
KSL = WIDTH // X

beta_one = 0.9
beta_two = 0.95
learn_rate = 0.001
decay_rate = 0.1
adam_eps = 1e-08
correct_one = 1.0 - beta_one**10
correct_two = 1.0 - beta_two**10
masked_score = -1e30

MESH = pl.DeviceIdType.MESH
F32 = jnp.float32
BF16 = jnp.bfloat16


def aligned(value, multiple):
    return pl.multiple_of(value * multiple, multiple)

NAMES = (
    "acts", "kv", "rew", "ids", "w_in", "m_in", "v_in", "hid", "qry", "ckey", "cval", "lens", "nw_out",
    "nm_out", "nv_out", "ent_out", "att_out", "abuf", "kbuf", "wt", "pbuf", "rsbuf", "own", "hv", "hl", "hb",
    "nwb", "wall", "acc", "part", "ebuf", "ra", "rb", "wv", "mv", "vv", "rs", "ls", "ns", "qv", "qb", "ck", "cv",
    "oc", "ml",  "loc_sem", "a_send", "a_recv", "k_send", "k_recv", "r_send", "r_recv", "rs_send",
    "rs_recv", "o_send", "o_recv", "h_send", "h_recv", "c_send", "c_recv", "w_send", "w_recv", "e_send",
    "e_recv",
)


def kernel(*all_refs):
    refs = dict(zip(NAMES, all_refs))
    acts, kv, hid = refs["acts"], refs["kv"], refs["hid"]
    abuf, kbuf, wt, pbuf, rsbuf, own = (refs[k] for k in ("abuf", "kbuf", "wt", "pbuf", "rsbuf", "own"))
    hv, hl, hb, nwb, wall, acc = (refs[k] for k in ("hv", "hl", "hb", "nwb", "wall", "acc"))
    part, ebuf, ra, rb = (refs[k] for k in ("part", "ebuf", "ra", "rb"))
    wv, mv, vv = (refs[k] for k in ("wv", "mv", "vv"))
    qv, qb, ck, cv, oc, ml = (refs[k] for k in ("qv", "qb", "ck", "cv", "oc", "ml"))
    loc_sem, a_send, a_recv, k_send, k_recv = (refs[k] for k in NAMES[NAMES.index("loc_sem") :][:5])
    r_send, r_recv, rs_send, rs_recv, o_send, o_recv = (refs[k] for k in NAMES[NAMES.index("r_send") :][:6])
    h_send, h_recv, c_send, c_recv = (refs[k] for k in NAMES[NAMES.index("h_send") :][:4])
    w_send, w_recv, e_send, e_recv = (refs[k] for k in NAMES[NAMES.index("w_send") :][:4])

    f, t, x = lax.axis_index("fsdp"), lax.axis_index("tp"), lax.axis_index("dp")
    z, g = lax.div(f, 4), lax.rem(f, 4)
    yh, c = lax.div(g, 2), lax.rem(g, 2)
    other, yo = 1 - c, 1 - yh

    def dev(z=z, yh=yh, c=c, t=t, x=x):
        return (z * 4 + yh * 2 + c, t, x)

    def copy(src, dst, send, recv, to):
        return pltpu.make_async_remote_copy(
            src_ref=src, dst_ref=dst, send_sem=send, recv_sem=recv, device_id=to, device_id_type=MESH
        )

    def arrived(dst, recv):
        copy(dst, dst, o_send.at[0], recv, dev(c=other)).wait_recv()

    def xs(step):
        return lax.rem(x + step + X, X)

    def zs(step):
        return lax.rem(z + step + Z, Z)

    def run_of(order):
        return jnp.bitwise_xor(jnp.bitwise_xor(t, order), 1)

    def half_of(src, slot):
        u = lax.rem(slot - 2 * t - lax.div(src, 2) + 2 * Z, Z)
        upper = jnp.where((u >= 1) & (u <= 4), 1, 0)
        return run_of(jnp.where(upper == 1, u - 1, lax.rem(Z - u, Z))), upper

    half = pl.ds(aligned(c, HALF), HALF)
    mine, other_rows = pl.ds(aligned(c, TOK), TOK), pl.ds(aligned(other, TOK), TOK)
    local = [
        pltpu.make_async_copy(src, dst, loc_sem.at[i])
        for i, (src, dst) in enumerate(
            (
                (refs["rew"], refs["rs"]),
                (refs["ids"], refs["ls"]),
                (kv, kbuf.at[t]),
                (refs["lens"], refs["ns"]),
                (refs["qry"], qv),
                (refs["ckey"], ck),
                (refs["cval"], cv),
                (acts.at[:, half], abuf.at[x, mine]),
                (hid, hv),
                (refs["w_in"], wv),
                (refs["m_in"], mv),
                (refs["v_in"], vv),
            )
        )
    ]
    for item in local[:2]:
        item.start()

    barrier = pltpu.get_barrier_semaphore()
    senders = [dev(z=zs(step)) for step in (4, 3, -3, 2, -2, 1, -1)]
    senders += [dev(yh=yo), dev(yh=yo, c=other)]
    senders += [dev(t=lax.rem(t + step, T)) for step in range(1, T)]
    senders += [dev(x=xs(step), c=core) for step in (1, -1) for core in range(2)]
    senders += [dev(c=other)]
    for sender in senders:
        pl.semaphore_signal(barrier, inc=1, device_id=sender, device_id_type=MESH)

    local[0].wait()
    local[1].wait()
    sub = lax.broadcasted_iota(jnp.int32, (8, 128), 0)
    lane = lax.broadcasted_iota(jnp.int32, (8, 128), 1)
    rew_row = jnp.zeros((8, 128), F32)
    id_row = jnp.full((8, 128), -1, jnp.int32)
    for seq in range(SEQ):
        rew_row = jnp.where(lane == seq, refs["rs"][seq], rew_row)
        id_row = jnp.where(lane == seq, refs["ls"][seq], id_row)
    id_row = id_row.astype(F32)
    ra[g] = jnp.where(sub == 2 * g, rew_row, jnp.where(sub == 2 * g + 1, id_row, 0.0))

    pl.semaphore_wait(barrier, len(senders))

    sends = []

    def start(item):
        item.start()
        sends.append(item)

    trio = ((yh, other), (yo, c), (yo, other))
    for step, (to_yh, to_c) in enumerate(trio):
        start(copy(ra.at[g], ra.at[g], r_send.at[step], r_recv.at[g], dev(yh=to_yh, c=to_c)))

    for step, sign in ((0, 1 - 2 * c), (1, 2 * c - 1)):
        for core in range(2):
            start(
                copy(
                    acts.at[:, pl.ds(core * HALF, HALF)],
                    abuf.at[x, mine],
                    a_send.at[2 * step + core],
                    a_recv.at[x, c],
                    dev(x=xs(sign), c=core),
                )
            )
    for step in range(1, T):
        start(copy(kv, kbuf.at[t], k_send.at[step], k_recv.at[t], dev(t=lax.rem(t + step, T))))
    start(
        copy(
            acts.at[:, pl.ds(aligned(other, HALF), HALF)],
            abuf.at[x, mine],
            a_send.at[4],
            a_recv.at[x, c],
            dev(c=other),
        )
    )

    for item in local[2:]:
        item.start()

    def cached(h, G):
        keys = ck[8 * G : 8 * G + 8, :, h * HD : (h + 1) * HD].reshape(8 * CACHE, HD)
        values = cv[8 * G : 8 * G + 8, :, h * HD : (h + 1) * HD].reshape(8 * CACHE, HD)
        scores = lax.dot_general(qb[h, G], keys, (((1,), (1,)), ((), ())), preferred_element_type=F32)
        scores *= HD ** (-0.5)
        column = lax.broadcasted_iota(jnp.int32, (1, 8 * CACHE), 1)
        limit = jnp.zeros((1, 8 * CACHE), jnp.int32)
        for row in range(8):
            limit = jnp.where(lax.div(column, CACHE) == row, refs["ns"][8 * G + row], limit)
        owner = jnp.where(lax.rem(column, CACHE) < limit, lax.div(column, CACHE), -1)
        row = lax.rem(lax.broadcasted_iota(jnp.int32, (256, 1), 0), 8)
        scores = jnp.where(row == owner, scores, masked_score)
        top = jnp.max(scores, axis=1, keepdims=True)
        weights = jnp.exp(scores - top)
        place = lax.broadcasted_iota(jnp.int32, (256, HD), 1)
        stats = jnp.where(place == 0, top, jnp.where(place == 1, jnp.sum(weights, axis=1, keepdims=True), 0.0))
        ml[h, G] = stats.T[0:8, :]
        oc[h, G] = jnp.dot(weights.astype(BF16), values, preferred_element_type=F32)

    for to_yh, to_c in trio:
        arrived(ra.at[to_yh * 2 + to_c], r_recv.at[to_yh * 2 + to_c])
    rb[z] = ra[0] + ra[1] + ra[2] + ra[3]
    for step in range(1, Z):
        start(copy(rb.at[z], rb.at[z], r_send.at[3 + step], r_recv.at[4 + z], dev(z=zs(step))))

    local[8].wait()
    for q in range(WIDTH // FEAT):
        for to in range(X):
            hl[to, :, q * 128 : (q + 1) * 128] = hv[:, q * FEAT + to * 128 : q * FEAT + (to + 1) * 128]

    for step in range(1, Z):
        arrived(rb.at[zs(step)], r_recv.at[4 + zs(step)])
    rew_col = jnp.sum(jnp.where(sub == lane, rew_row, 0.0), axis=1, keepdims=True)
    id_col = jnp.sum(jnp.where(sub == lane, id_row, 0.0), axis=1, keepdims=True)
    sums = jnp.zeros((8, 128), F32)
    for zz in range(Z):
        for group in range(4):
            same = rb[zz, 2 * group + 1 : 2 * group + 2, :] == id_col
            sums += jnp.where(same, rb[zz, 2 * group : 2 * group + 1, :], 0.0)
    advantage = rew_col - jnp.sum(sums, axis=1, keepdims=True) / GSIZE

    def weigh(src, step):
        columns = [
            advantage[seq : seq + 1, 0:1] * kbuf[src, seq * LEN : (seq + 1) * LEN, :].astype(F32) for seq in range(SEQ)
        ]
        rows = pl.ds(aligned(src, COL), COL)
        wt[rows, mine] = jnp.concatenate(columns, axis=0).T.astype(BF16)
        start(copy(wt.at[rows, mine], wt.at[rows, mine], k_send.at[T + step], k_recv.at[T + src], dev(c=other)))

    local[2].wait()
    weigh(t, 0)

    left, right, across = xs(-1), xs(1), xs(2)
    first, second = pl.ds(0, TOK), pl.ds(TOK, TOK)
    arrived(abuf.at[left, first], a_recv.at[left, 0])
    start(copy(abuf.at[left, first], abuf.at[left, first], a_send.at[5], a_recv.at[left, 0], dev(x=right)))
    arrived(abuf.at[right, second], a_recv.at[right, 1])
    start(copy(abuf.at[right, second], abuf.at[right, second], a_send.at[6], a_recv.at[right, 1], dev(x=left)))

    for step in (1, 3, 2):
        src = jnp.bitwise_xor(t, step)
        arrived(kbuf.at[src], k_recv.at[src])
        weigh(src, step)

    for src in range(T):
        arrived(wt.at[pl.ds(src * COL, COL), other_rows], k_recv.at[T + src])

    blocks = (x, left, right, across)
    ways = (1, -1)

    last = Z // 2 - 1

    def hops(block, way):
        return last if block == X - 1 or way != block % 2 else last + 1

    def jumps(block, way):
        return block == X - 1 and way == block % 2

    def own_piece(block, slot):
        run, upper = half_of(blocks[block], slot)
        return pbuf.at[block, pl.ds(aligned(2 * run + upper, COL // 2), COL // 2)]

    def ring_copy(src, block, way, step, jump=1):
        return copy(
            src,
            rsbuf.at[block, way, step],
            rs_send.at[block, way, step],
            rs_recv.at[block, way, step],
            dev(z=zs(ways[way] * jump)),
        )

    def multiply(block):
        pbuf[block] = jnp.dot(wt[...], abuf[blocks[block]], preferred_element_type=F32).astype(BF16)
        for way in range(2):
            if jumps(block, way):
                start(ring_copy(own_piece(block, zs(Z // 2)), block, way, last, 2))
            start(ring_copy(own_piece(block, zs(ways[way] * hops(block, way))), block, way, 0))

    local[7].wait()
    arrived(abuf.at[x, other_rows], a_recv.at[x, other])
    multiply(0)
    arrived(abuf.at[left, second], a_recv.at[left, 1])
    multiply(1)
    arrived(abuf.at[right, first], a_recv.at[right, 0])
    multiply(2)
    arrived(abuf.at[across, first], a_recv.at[across, 0])
    arrived(abuf.at[across, second], a_recv.at[across, 1])

    hslot = hb.at[x * 2 + c]
    hid_local = pltpu.make_async_copy(hl.at[x], hslot, loc_sem.at[12])
    hid_local.start()
    for step in (1, -1, 2):
        start(copy(hl.at[xs(step)], hslot, h_send.at[step % X], h_recv.at[x, c], dev(x=xs(step))))
    start(copy(hl.at[x], hslot, h_send.at[0], h_recv.at[x, c], dev(c=other)))

    multiply(3)

    def ring_step(block, step):
        for way in range(2):
            if step + 1 >= hops(block, way):
                continue
            here = rsbuf.at[block, way, step]
            arrived(here, rs_recv.at[block, way, step])
            slot = zs(ways[way] * (hops(block, way) - 1 - step))
            total = here[...].astype(F32) + own_piece(block, slot)[...].astype(F32)
            if step == 0 and jumps(block, way):
                arrived(rsbuf.at[block, way, last], rs_recv.at[block, way, last])
                total += rsbuf[block, way, last].astype(F32)
            here[...] = total.astype(BF16)
            start(ring_copy(here, block, way, step + 1))

    def ring_end(block):
        total = own_piece(block, z)[...].astype(F32)
        for way in range(2):
            here = rsbuf.at[block, way, hops(block, way) - 1]
            arrived(here, rs_recv.at[block, way, hops(block, way) - 1])
            total += here[...].astype(F32)
        here = rsbuf.at[block, 1 - block % 2, last]
        here[...] = total.astype(BF16)
        src = blocks[block]
        run, upper = half_of(src, z)
        start(
            copy(
                here,
                own.at[yh, pl.ds(aligned(upper, COL // 2), COL // 2)],
                o_send.at[block],
                o_recv.at[yh, upper],
                dev(z=2 * t + lax.div(src, 2), yh=lax.rem(src, 2), t=run),
            )
        )

    for step in range(2):
        for block in range(X - 1):
            ring_step(block, step)
    ring_step(X - 1, 0)
    for block in range(X - 1):
        ring_step(block, 2)
    ring_step(X - 1, 1)
    for block in range(X):
        ring_end(block)

    for item in local[3:7]:
        item.wait()
    for h in range(2):
        tiles = [qv[:, (8 * h + j) * HD : (8 * h + j + 1) * HD].astype(F32) for j in range(8)]
        for G in range(3):
            rows = [tiles[j][s * DROWS + 8 * G : s * DROWS + 8 * G + 8] for j in range(8) for s in range(STEPS)]
            qb[h, G] = jnp.concatenate(rows, axis=0).astype(BF16)

    for G in range(3):
        cached(0, G)
    cached(1, 0)

    for item in local[9:]:
        item.wait()
    for from_yh in range(2):
        for upper in range(2):
            arrived(own.at[from_yh, pl.ds(upper * COL // 2, COL // 2)], o_recv.at[from_yh, upper])
    weight_grad = (own[0].astype(F32) + own[1].astype(F32)).T / LEN
    new_m = beta_one * mv[...] + (1.0 - beta_one) * weight_grad
    new_v = beta_two * vv[...] + (1.0 - beta_two) * weight_grad * weight_grad
    weight_f = wv[...].astype(F32)
    direction = new_m / correct_one / (jnp.sqrt(new_v / correct_two) + adam_eps)
    new_weight = (weight_f - learn_rate * (direction + decay_rate * weight_f)).astype(BF16)
    nwb[...] = new_weight

    is_self = c == lax.div(x, 2)
    cols = pl.ds(aligned(lax.rem(x, 2), COL), COL)
    slices = []
    for r in range(2):
        src = nwb.at[pl.ds(r * COL, COL)]
        dst = wall.at[z * 2 + yh, :, cols]
        recv = c_recv.at[yh, lax.rem(x, 2)]
        near = copy(src, dst, c_send.at[r], recv, dev(c=lax.div(x, 2), x=2 * c + r))
        far = copy(src, dst, c_send.at[2 + r], recv, dev(yh=yo, c=lax.div(x, 2), x=2 * c + r))
        here = is_self & (lax.rem(x, 2) == r)
        pl.when(jnp.logical_not(here))(near.start)
        pl.when(here)(pltpu.make_async_copy(src, dst, recv).start)
        start(far)
        slices.append((here, near))

    cached(1, 1)
    cached(1, 2)
    refs["nw_out"][...] = new_weight
    refs["nm_out"][...] = new_m
    refs["nv_out"][...] = new_v

    pairs = (yh, yo)

    def pass_on(zz, k, part_of, way, step, jump=1):
        slot = wall.at[zz * 2 + pairs[k], pl.ds(part_of * 64, 64)]
        sem = 2 * k + part_of
        to = dev(z=zs(ways[way] * jump))
        start(copy(slot, slot, w_send.at[way, sem, step], w_recv.at[zz, sem], to))

    for k in range(2):
        for hh in range(2):
            arrived(wall.at[z * 2 + pairs[k], :, pl.ds(hh * COL, COL)], c_recv.at[pairs[k], hh])
        for part_of in range(2):
            for way in range(2):
                pass_on(z, k, part_of, way, 0)

    for step in (1, -1, 2):
        slot = hb.at[xs(step) * 2 + c]
        arrived(slot, h_recv.at[xs(step), c])
        start(copy(slot, slot, h_send.at[X + step % X], h_recv.at[xs(step), c], dev(c=other)))
    hid_local.wait()
    for step in range(X):
        arrived(hb.at[xs(step) * 2 + other], h_recv.at[xs(step), other])

    def project(zz):
        rows = hb[:, :, pl.ds(aligned(zz, 2 * COL), 2 * COL)].reshape(2 * X * ROWS, 2 * COL)
        block = wall[pl.ds(zz * 2, 2)].reshape(2 * COL, 2 * COL)
        return jnp.dot(rows, block, preferred_element_type=F32)

    acc[...] = project(z)
    for step in range(1, Z // 2 + 1):
        for k in range(2):
            for part_of in range(2):
                for way in range(2):
                    if step == Z // 2 and way != k:
                        continue
                    zz = zs(-ways[way] * step)
                    sem = 2 * k + part_of
                    arrived(wall.at[zz * 2 + pairs[k], pl.ds(part_of * 64, 64)], w_recv.at[zz, sem])
                    if step == last - 1 and way == k:
                        pass_on(zz, k, part_of, way, last, 2)
                    if step < last:
                        pass_on(zz, k, part_of, way, step)
        if step < Z // 2:
            acc[...] += project(zs(-step)) + project(zs(step))

    early = list(sends)
    far = zs(Z // 2)
    far_cols = pl.ds(aligned(far, 2 * COL), 2 * COL)
    far_block = wall[pl.ds(far * 2, 2)].reshape(2 * COL, 2 * COL)
    for step in (2, 1, -1, 0):
        to = xs(step)
        rows = hb[pl.ds(to * 2, 2), :, far_cols].reshape(2 * ROWS, 2 * COL)
        sums = acc[pl.ds(aligned(to, 2 * ROWS), 2 * ROWS), :] + jnp.dot(rows, far_block, preferred_element_type=F32)
        part[pl.ds(to * 2, 2)] = sums.astype(BF16).reshape(2, ROWS, 2 * HD)
        for core in range(2):
            to_c = c if core == 0 else other
            if step == 0 and core == 0:
                ebuf[x, c] = part[x * 2 + c]
                continue
            start(
                copy(
                    part.at[to * 2 + to_c],
                    ebuf.at[x, c],
                    e_send.at[2 * (step % X) + core],
                    e_recv.at[x, c],
                    dev(x=to, c=to_c),
                )
            )
    for item in early:
        item.wait_send()
    for here, near in slices:
        pl.when(jnp.logical_not(here))(near.wait_send)
    for step in (0, 1, -1, 2):
        for core in range(2):
            from_c = c if core == 0 else other
            if step == 0 and core == 0:
                continue
            arrived(ebuf.at[xs(step), from_c], e_recv.at[xs(step), from_c])

    row = lax.broadcasted_iota(jnp.int32, (32, 256), 0)
    column = lax.broadcasted_iota(jnp.int32, (32, 256), 1)
    seen = (lax.rem(row, 8) == lax.rem(column, 8)) & (lax.rem(lax.div(column, 8), STEPS) >= lax.div(row, 8))
    for h in range(2):
        total = ebuf[0, h].astype(F32)
        for src in range(1, X):
            total += ebuf[src, h].astype(F32)
        entries = total.astype(BF16)
        refs["ent_out"][:, h * 2 * HD : (h + 1) * 2 * HD] = entries
        fresh = entries.astype(F32)
        outs = []
        for G in range(3):
            rows = [fresh[s * DROWS + 8 * G : s * DROWS + 8 * G + 8] for s in range(STEPS)]
            new = jnp.concatenate(rows, axis=0).astype(BF16)
            scores = lax.dot_general(new[:, :HD], qb[h, G], (((1,), (1,)), ((), ())), preferred_element_type=F32)
            scores = jnp.where(seen, scores * HD ** (-0.5), masked_score)
            before, count = ml[h, G, 0:1, :], ml[h, G, 1:2, :]
            top = jnp.maximum(before, jnp.max(scores, axis=0, keepdims=True))
            weights = jnp.exp(scores - top)
            scale = jnp.exp(before - top)
            whole = count * scale + jnp.sum(weights, axis=0, keepdims=True)
            probs = (weights / whole).astype(BF16)
            mixed = lax.dot_general(probs, new[:, HD:], (((0,), (0,)), ((), ())), preferred_element_type=F32)
            outs.append(oc[h, G] * jnp.broadcast_to(scale / whole, (HD, 256)).T + mixed)
        for j in range(8):
            rows = [
                outs[G][(j * STEPS + s) * 8 : (j * STEPS + s) * 8 + 8] for s in range(STEPS) for G in range(3)
            ]
            refs["att_out"][:, (8 * h + j) * HD : (8 * h + j + 1) * HD] = jnp.concatenate(rows, axis=0).astype(BF16)

    for item in sends[len(early) :]:
        item.wait_send()


OUT_SHAPES = (
    jax.ShapeDtypeStruct((HALF, COL), BF16),
    jax.ShapeDtypeStruct((HALF, COL), F32),
    jax.ShapeDtypeStruct((HALF, COL), F32),
    jax.ShapeDtypeStruct((ROWS, 4 * HD), BF16),
    jax.ShapeDtypeStruct((ROWS, QW), BF16),
)


def write_out(*refs):
    count = len(OUT_SHAPES)
    for i in range(count):
        refs[count + i][...] = refs[i][...]


def body(
    acts,
    kv_grad,
    rewards,
    group_ids,
    kv_weight,
    adam_m,
    adam_v,
    hidden,
    queries,
    cache_keys,
    cache_values,
    cache_lens,
):
    hbm = pl.BlockSpec(memory_space=pltpu.HBM)
    vmem = pl.BlockSpec(memory_space=pltpu.VMEM)
    dma = pltpu.SemaphoreType.DMA
    results = pl.pallas_call(
        kernel,
        out_shape=OUT_SHAPES,
        in_specs=[hbm] * 12,
        out_specs=(vmem,) * 5,
        scratch_shapes=[
            pltpu.VMEM((X, 2 * TOK, HALF), BF16),
            pltpu.VMEM((T, TOK, COL), BF16),
            pltpu.VMEM((T * COL, 2 * TOK), BF16),
            pltpu.VMEM((X, T * COL, HALF), BF16),
            pltpu.VMEM((X, 2, Z // 2, COL // 2, HALF), BF16),
            pltpu.VMEM((2, COL, HALF), BF16),
            pltpu.VMEM((ROWS, WIDTH), BF16),
            pltpu.VMEM((X, ROWS, KSL), BF16),
            pltpu.VMEM((2 * X, ROWS, KSL), BF16),
            pltpu.VMEM((HALF, COL), BF16),
            pltpu.VMEM((2 * Z, COL, 2 * COL), BF16),
            pltpu.VMEM((2 * X * ROWS, 2 * COL), F32),
            pltpu.VMEM((2 * X, ROWS, 2 * COL), BF16),
            pltpu.VMEM((X, 2, ROWS, 2 * COL), BF16),
            pltpu.VMEM((4, 8, 128), F32),
            pltpu.VMEM((Z, 8, 128), F32),
            pltpu.VMEM((HALF, COL), BF16),
            pltpu.VMEM((HALF, COL), F32),
            pltpu.VMEM((HALF, COL), F32),
            pltpu.SMEM((SEQ,), F32),
            pltpu.SMEM((SEQ,), jnp.int32),
            pltpu.SMEM((DROWS,), jnp.int32),
            pltpu.VMEM((ROWS, QW), BF16),
            pltpu.VMEM((2, 3, 256, HD), BF16),
            pltpu.VMEM((DROWS, CACHE, 2 * HD), BF16),
            pltpu.VMEM((DROWS, CACHE, 2 * HD), BF16),
            pltpu.VMEM((2, 3, 256, HD), F32),
            pltpu.VMEM((2, 3, 8, 256), F32),
            dma((13,)),
            dma((7,)),
            dma((X, 2)),
            dma((2 * T,)),
            dma((2 * T,)),
            dma((Z + 3,)),
            dma((Z + 4,)),
            dma((X, 2, Z // 2)),
            dma((X, 2, Z // 2)),
            dma((X,)),
            dma((2, 2)),
            dma((2 * X,)),
            dma((X, 2)),
            dma((4,)),
            dma((2, 2)),
            dma((2, 4, Z // 2)),
            dma((Z, 4)),
            dma((2 * X,)),
            dma((X, 2)),
        ],
        compiler_params=pltpu.CompilerParams(
            collective_id=0, has_side_effects=True, vmem_limit_bytes=63400000
        ),
        name="update_and_decode",
    )(
        acts,
        kv_grad,
        rewards,
        group_ids,
        kv_weight,
        adam_m,
        adam_v,
        hidden.reshape(ROWS, WIDTH),
        queries.reshape(ROWS, QW),
        cache_keys,
        cache_values,
        cache_lens,
    )
    new_weight, new_m, new_v, new_entries, attention = pl.pallas_call(
        write_out,
        out_shape=OUT_SHAPES,
        in_specs=[vmem] * 5,
        out_specs=(vmem,) * 5,
        name="write_out",
    )(*results)
    return (
        new_weight,
        new_m,
        new_v,
        new_entries.reshape(STEPS, DROWS, 4 * HD),
        attention.reshape(STEPS, DROWS, QW),
    )


def solution(mesh):
    return jax.shard_map(
        body,
        mesh=mesh,
        in_specs=(
            P("fsdp", ("tp", "dp")),
            P("fsdp", ("tp", "dp")),
            P("fsdp"),
            P("fsdp"),
            P("fsdp", ("tp", "dp")),
            P("fsdp", ("tp", "dp")),
            P("fsdp", ("tp", "dp")),
            P(None, ("fsdp", "dp"), None),
            P(None, ("fsdp", "dp"), "tp"),
            P(("fsdp", "dp"), None, "tp"),
            P(("fsdp", "dp"), None, "tp"),
            P(("fsdp", "dp")),
        ),
        out_specs=(
            P("fsdp", ("tp", "dp")),
            P("fsdp", ("tp", "dp")),
            P("fsdp", ("tp", "dp")),
            P(None, ("fsdp", "dp"), "tp"),
            P(None, ("fsdp", "dp"), "tp"),
        ),
        check_vma=False,
    )
```

```python
import jax
import jax.numpy as jnp
from jax import lax
from jax.experimental import pallas as pl
from jax.experimental.pallas import tpu as pltpu
from jax.sharding import PartitionSpec as P

HD = 128
LEN = 48
GSIZE = 8
X = 4
T = 4
Z = 8
TOK = 384
SEQ = 8
FEAT = 512
HALF = 256
COL = 128
STEPS = 4
DROWS = 24
ROWS = 96
CACHE = 64
QW = 2048
WIDTH = 8192
KSL = WIDTH // X

beta_one = 0.9
beta_two = 0.95
learn_rate = 0.001
decay_rate = 0.1
adam_eps = 1e-08
correct_one = 1.0 - beta_one**10
correct_two = 1.0 - beta_two**10
masked_score = -1e30

MESH = pl.DeviceIdType.MESH
F32 = jnp.float32
BF16 = jnp.bfloat16


def aligned(value, multiple):
    return pl.multiple_of(value * multiple, multiple)

NAMES = (
    "acts", "kv", "rew", "ids", "w_in", "m_in", "v_in", "hid", "qry", "ckey", "cval", "lens", "nw_out",
    "nm_out", "nv_out", "ent_out", "att_out", "abuf", "kbuf", "wt", "pbuf", "rsbuf", "own", "hv", "hl", "hb",
    "nwb", "wall", "acc", "part", "ebuf", "ra", "rb", "wv", "mv", "vv", "rs", "ls", "ns", "qv", "qb", "ck", "cv",
    "oc", "ml", "ent", "att",  "loc_sem", "a_send", "a_recv", "k_send", "k_recv", "r_send", "r_recv", "rs_send",
    "rs_recv", "o_send", "o_recv", "h_send", "h_recv", "c_send", "c_recv", "w_send", "w_recv", "e_send",
    "e_recv", "out_sem",
)


def kernel(*all_refs):
    refs = dict(zip(NAMES, all_refs))
    acts, kv, hid = refs["acts"], refs["kv"], refs["hid"]
    abuf, kbuf, wt, pbuf, rsbuf, own = (refs[k] for k in ("abuf", "kbuf", "wt", "pbuf", "rsbuf", "own"))
    hv, hl, hb, nwb, wall, acc = (refs[k] for k in ("hv", "hl", "hb", "nwb", "wall", "acc"))
    part, ebuf, ra, rb = (refs[k] for k in ("part", "ebuf", "ra", "rb"))
    wv, mv, vv = (refs[k] for k in ("wv", "mv", "vv"))
    qv, qb, ck, cv, oc, ml = (refs[k] for k in ("qv", "qb", "ck", "cv", "oc", "ml"))
    loc_sem, a_send, a_recv, k_send, k_recv = (refs[k] for k in NAMES[NAMES.index("loc_sem") :][:5])
    r_send, r_recv, rs_send, rs_recv, o_send, o_recv = (refs[k] for k in NAMES[NAMES.index("r_send") :][:6])
    h_send, h_recv, c_send, c_recv = (refs[k] for k in NAMES[NAMES.index("h_send") :][:4])
    w_send, w_recv, e_send, e_recv, out_sem = (refs[k] for k in NAMES[NAMES.index("w_send") :][:5])
    ent, att = refs["ent"], refs["att"]

    f, t, x = lax.axis_index("fsdp"), lax.axis_index("tp"), lax.axis_index("dp")
    z, g = lax.div(f, 4), lax.rem(f, 4)
    yh, c = lax.div(g, 2), lax.rem(g, 2)
    other, yo = 1 - c, 1 - yh

    def dev(z=z, yh=yh, c=c, t=t, x=x):
        return (z * 4 + yh * 2 + c, t, x)

    def copy(src, dst, send, recv, to):
        return pltpu.make_async_remote_copy(
            src_ref=src, dst_ref=dst, send_sem=send, recv_sem=recv, device_id=to, device_id_type=MESH
        )

    def arrived(dst, recv):
        copy(dst, dst, o_send.at[0], recv, dev(c=other)).wait_recv()

    def xs(step):
        return lax.rem(x + step + X, X)

    def zs(step):
        return lax.rem(z + step + Z, Z)

    def run_of(order):
        return jnp.bitwise_xor(jnp.bitwise_xor(t, order), 1)

    def half_of(src, slot):
        u = lax.rem(slot - 2 * t - lax.div(src, 2) + 2 * Z, Z)
        upper = jnp.where((u >= 1) & (u <= 4), 1, 0)
        return run_of(jnp.where(upper == 1, u - 1, lax.rem(Z - u, Z))), upper

    half = pl.ds(aligned(c, HALF), HALF)
    mine, other_rows = pl.ds(aligned(c, TOK), TOK), pl.ds(aligned(other, TOK), TOK)
    local = [
        pltpu.make_async_copy(src, dst, loc_sem.at[i])
        for i, (src, dst) in enumerate(
            (
                (refs["rew"], refs["rs"]),
                (refs["ids"], refs["ls"]),
                (kv, kbuf.at[t]),
                (refs["lens"], refs["ns"]),
                (refs["qry"], qv),
                (refs["ckey"], ck),
                (refs["cval"], cv),
                (acts.at[:, half], abuf.at[x, mine]),
                (hid, hv),
                (refs["w_in"], wv),
                (refs["m_in"], mv),
                (refs["v_in"], vv),
            )
        )
    ]
    for item in local[:2]:
        item.start()

    barrier = pltpu.get_barrier_semaphore()
    senders = [dev(z=zs(step)) for step in (4, 3, -3, 2, -2, 1, -1)]
    senders += [dev(yh=yo), dev(yh=yo, c=other)]
    senders += [dev(t=lax.rem(t + step, T)) for step in range(1, T)]
    senders += [dev(x=xs(step), c=core) for step in (1, -1) for core in range(2)]
    senders += [dev(c=other)]
    for sender in senders:
        pl.semaphore_signal(barrier, inc=1, device_id=sender, device_id_type=MESH)

    local[0].wait()
    local[1].wait()
    sub = lax.broadcasted_iota(jnp.int32, (8, 128), 0)
    lane = lax.broadcasted_iota(jnp.int32, (8, 128), 1)
    rew_row = jnp.zeros((8, 128), F32)
    id_row = jnp.full((8, 128), -1, jnp.int32)
    for seq in range(SEQ):
        rew_row = jnp.where(lane == seq, refs["rs"][seq], rew_row)
        id_row = jnp.where(lane == seq, refs["ls"][seq], id_row)
    id_row = id_row.astype(F32)
    ra[g] = jnp.where(sub == 2 * g, rew_row, jnp.where(sub == 2 * g + 1, id_row, 0.0))

    pl.semaphore_wait(barrier, len(senders))

    sends = []

    def start(item):
        item.start()
        sends.append(item)

    trio = ((yh, other), (yo, c), (yo, other))
    for step, (to_yh, to_c) in enumerate(trio):
        start(copy(ra.at[g], ra.at[g], r_send.at[step], r_recv.at[g], dev(yh=to_yh, c=to_c)))

    for step, sign in ((0, 1 - 2 * c), (1, 2 * c - 1)):
        for core in range(2):
            start(
                copy(
                    acts.at[:, pl.ds(core * HALF, HALF)],
                    abuf.at[x, mine],
                    a_send.at[2 * step + core],
                    a_recv.at[x, c],
                    dev(x=xs(sign), c=core),
                )
            )
    for step in range(1, T):
        start(copy(kv, kbuf.at[t], k_send.at[step], k_recv.at[t], dev(t=lax.rem(t + step, T))))
    start(
        copy(
            acts.at[:, pl.ds(aligned(other, HALF), HALF)],
            abuf.at[x, mine],
            a_send.at[4],
            a_recv.at[x, c],
            dev(c=other),
        )
    )

    for item in local[2:]:
        item.start()

    def cached(h, G):
        keys = ck[8 * G : 8 * G + 8, :, h * HD : (h + 1) * HD].reshape(8 * CACHE, HD)
        values = cv[8 * G : 8 * G + 8, :, h * HD : (h + 1) * HD].reshape(8 * CACHE, HD)
        scores = lax.dot_general(qb[h, G], keys, (((1,), (1,)), ((), ())), preferred_element_type=F32)
        scores *= HD ** (-0.5)
        column = lax.broadcasted_iota(jnp.int32, (1, 8 * CACHE), 1)
        limit = jnp.zeros((1, 8 * CACHE), jnp.int32)
        for row in range(8):
            limit = jnp.where(lax.div(column, CACHE) == row, refs["ns"][8 * G + row], limit)
        owner = jnp.where(lax.rem(column, CACHE) < limit, lax.div(column, CACHE), -1)
        row = lax.rem(lax.broadcasted_iota(jnp.int32, (256, 1), 0), 8)
        scores = jnp.where(row == owner, scores, masked_score)
        top = jnp.max(scores, axis=1, keepdims=True)
        weights = jnp.exp(scores - top)
        place = lax.broadcasted_iota(jnp.int32, (256, HD), 1)
        stats = jnp.where(place == 0, top, jnp.where(place == 1, jnp.sum(weights, axis=1, keepdims=True), 0.0))
        ml[h, G] = stats.T[0:8, :]
        oc[h, G] = jnp.dot(weights.astype(BF16), values, preferred_element_type=F32)

    for to_yh, to_c in trio:
        arrived(ra.at[to_yh * 2 + to_c], r_recv.at[to_yh * 2 + to_c])
    rb[z] = ra[0] + ra[1] + ra[2] + ra[3]
    for step in range(1, Z):
        start(copy(rb.at[z], rb.at[z], r_send.at[3 + step], r_recv.at[4 + z], dev(z=zs(step))))

    local[8].wait()
    for q in range(WIDTH // FEAT):
        for to in range(X):
            hl[to, :, q * 128 : (q + 1) * 128] = hv[:, q * FEAT + to * 128 : q * FEAT + (to + 1) * 128]

    for step in range(1, Z):
        arrived(rb.at[zs(step)], r_recv.at[4 + zs(step)])
    rew_col = jnp.sum(jnp.where(sub == lane, rew_row, 0.0), axis=1, keepdims=True)
    id_col = jnp.sum(jnp.where(sub == lane, id_row, 0.0), axis=1, keepdims=True)
    sums = jnp.zeros((8, 128), F32)
    for zz in range(Z):
        for group in range(4):
            same = rb[zz, 2 * group + 1 : 2 * group + 2, :] == id_col
            sums += jnp.where(same, rb[zz, 2 * group : 2 * group + 1, :], 0.0)
    advantage = rew_col - jnp.sum(sums, axis=1, keepdims=True) / GSIZE

    def weigh(src, step):
        columns = [
            advantage[seq : seq + 1, 0:1] * kbuf[src, seq * LEN : (seq + 1) * LEN, :].astype(F32) for seq in range(SEQ)
        ]
        rows = pl.ds(aligned(src, COL), COL)
        wt[rows, mine] = jnp.concatenate(columns, axis=0).T.astype(BF16)
        start(copy(wt.at[rows, mine], wt.at[rows, mine], k_send.at[T + step], k_recv.at[T + src], dev(c=other)))

    local[2].wait()
    weigh(t, 0)

    left, right, across = xs(-1), xs(1), xs(2)
    first, second = pl.ds(0, TOK), pl.ds(TOK, TOK)
    arrived(abuf.at[left, first], a_recv.at[left, 0])
    start(copy(abuf.at[left, first], abuf.at[left, first], a_send.at[5], a_recv.at[left, 0], dev(x=right)))
    arrived(abuf.at[right, second], a_recv.at[right, 1])
    start(copy(abuf.at[right, second], abuf.at[right, second], a_send.at[6], a_recv.at[right, 1], dev(x=left)))

    for step in (1, 3, 2):
        src = jnp.bitwise_xor(t, step)
        arrived(kbuf.at[src], k_recv.at[src])
        weigh(src, step)

    for src in range(T):
        arrived(wt.at[pl.ds(src * COL, COL), other_rows], k_recv.at[T + src])

    blocks = (x, left, right, across)
    ways = (1, -1)

    last = Z // 2 - 1

    def hops(block, way):
        return last if block == X - 1 or way != block % 2 else last + 1

    def jumps(block, way):
        return block == X - 1 and way == block % 2

    def own_piece(block, slot):
        run, upper = half_of(blocks[block], slot)
        return pbuf.at[block, pl.ds(aligned(2 * run + upper, COL // 2), COL // 2)]

    def ring_copy(src, block, way, step, jump=1):
        return copy(
            src,
            rsbuf.at[block, way, step],
            rs_send.at[block, way, step],
            rs_recv.at[block, way, step],
            dev(z=zs(ways[way] * jump)),
        )

    def multiply(block):
        pbuf[block] = jnp.dot(wt[...], abuf[blocks[block]], preferred_element_type=F32).astype(BF16)
        for way in range(2):
            if jumps(block, way):
                start(ring_copy(own_piece(block, zs(Z // 2)), block, way, last, 2))
            start(ring_copy(own_piece(block, zs(ways[way] * hops(block, way))), block, way, 0))

    def ring_step(block, step):
        for way in range(2):
            if step + 1 >= hops(block, way):
                continue
            here = rsbuf.at[block, way, step]
            arrived(here, rs_recv.at[block, way, step])
            slot = zs(ways[way] * (hops(block, way) - 1 - step))
            total = here[...].astype(F32) + own_piece(block, slot)[...].astype(F32)
            if step == 0 and jumps(block, way):
                arrived(rsbuf.at[block, way, last], rs_recv.at[block, way, last])
                total += rsbuf[block, way, last].astype(F32)
            here[...] = total.astype(BF16)
            start(ring_copy(here, block, way, step + 1))

    local[7].wait()
    arrived(abuf.at[x, other_rows], a_recv.at[x, other])
    multiply(0)
    arrived(abuf.at[left, second], a_recv.at[left, 1])
    multiply(1)
    arrived(abuf.at[right, first], a_recv.at[right, 0])
    multiply(2)
    ring_step(0, 0)
    ring_step(1, 0)
    arrived(abuf.at[across, first], a_recv.at[across, 0])
    arrived(abuf.at[across, second], a_recv.at[across, 1])

    hslot = hb.at[x * 2 + c]
    hid_local = pltpu.make_async_copy(hl.at[x], hslot, loc_sem.at[12])
    hid_local.start()
    for step in (1, -1, 2):
        start(copy(hl.at[xs(step)], hslot, h_send.at[step % X], h_recv.at[x, c], dev(x=xs(step))))
    start(copy(hl.at[x], hslot, h_send.at[0], h_recv.at[x, c], dev(c=other)))

    multiply(3)

    to_owners = []

    def ring_end(block):
        total = own_piece(block, z)[...].astype(F32)
        for way in range(2):
            here = rsbuf.at[block, way, hops(block, way) - 1]
            arrived(here, rs_recv.at[block, way, hops(block, way) - 1])
            total += here[...].astype(F32)
        here = rsbuf.at[block, 1 - block % 2, last]
        here[...] = total.astype(BF16)
        src = blocks[block]
        run, upper = half_of(src, z)
        to_owners.append(
            copy(
                here,
                own.at[yh, pl.ds(aligned(upper, COL // 2), COL // 2)],
                o_send.at[block],
                o_recv.at[yh, upper],
                dev(z=2 * t + lax.div(src, 2), yh=lax.rem(src, 2), t=run),
            )
        )

    for block, step in ((2, 0), (0, 1), (1, 1), (3, 0), (2, 1), (0, 2), (1, 2), (3, 1), (2, 2)):
        ring_step(block, step)
    for block in range(X):
        ring_end(block)
    for item in to_owners:
        start(item)

    for item in local[3:7]:
        item.wait()
    for h in range(2):
        tiles = [qv[:, (8 * h + j) * HD : (8 * h + j + 1) * HD].astype(F32) for j in range(8)]
        for G in range(3):
            rows = [tiles[j][s * DROWS + 8 * G : s * DROWS + 8 * G + 8] for j in range(8) for s in range(STEPS)]
            qb[h, G] = jnp.concatenate(rows, axis=0).astype(BF16)

    for G in range(3):
        cached(0, G)
    cached(1, 0)

    for item in local[9:]:
        item.wait()
    for from_yh in range(2):
        for upper in range(2):
            arrived(own.at[from_yh, pl.ds(upper * COL // 2, COL // 2)], o_recv.at[from_yh, upper])
    weight_grad = (own[0].astype(F32) + own[1].astype(F32)).T / LEN
    new_m = beta_one * mv[...] + (1.0 - beta_one) * weight_grad
    new_v = beta_two * vv[...] + (1.0 - beta_two) * weight_grad * weight_grad
    weight_f = wv[...].astype(F32)
    direction = new_m / correct_one / (jnp.sqrt(new_v / correct_two) + adam_eps)
    new_weight = (weight_f - learn_rate * (direction + decay_rate * weight_f)).astype(BF16)
    nwb[...] = new_weight

    is_self = c == lax.div(x, 2)
    cols = pl.ds(aligned(lax.rem(x, 2), COL), COL)
    slices = []
    for r in range(2):
        src = nwb.at[pl.ds(r * COL, COL)]
        dst = wall.at[z * 2 + yh, :, cols]
        recv = c_recv.at[yh, lax.rem(x, 2)]
        near = copy(src, dst, c_send.at[r], recv, dev(c=lax.div(x, 2), x=2 * c + r))
        far = copy(src, dst, c_send.at[2 + r], recv, dev(yh=yo, c=lax.div(x, 2), x=2 * c + r))
        here = is_self & (lax.rem(x, 2) == r)
        pl.when(jnp.logical_not(here))(near.start)
        pl.when(here)(pltpu.make_async_copy(src, dst, recv).start)
        start(far)
        slices.append((here, near))

    cached(1, 1)
    cached(1, 2)
    mv[...] = new_m
    vv[...] = new_v
    outs_done = [
        pltpu.make_async_copy(src, refs[dst], out_sem.at[i])
        for i, (src, dst) in enumerate(((nwb, "nw_out"), (mv, "nm_out"), (vv, "nv_out")))
    ]
    for item in outs_done:
        item.start()

    for step in (1, -1, 2):
        slot = hb.at[xs(step) * 2 + c]
        arrived(slot, h_recv.at[xs(step), c])
        start(copy(slot, slot, h_send.at[X + step % X], h_recv.at[xs(step), c], dev(c=other)))

    pairs = (yh, yo)

    def pass_on(zz, k, part_of, way, step, jump=1):
        slot = wall.at[zz * 2 + pairs[k], pl.ds(part_of * 64, 64)]
        sem = 2 * k + part_of
        to = dev(z=zs(ways[way] * jump))
        start(copy(slot, slot, w_send.at[way, sem, step], w_recv.at[zz, sem], to))

    for k in range(2):
        for hh in range(2):
            arrived(wall.at[z * 2 + pairs[k], :, pl.ds(hh * COL, COL)], c_recv.at[pairs[k], hh])
        for part_of in range(2):
            for way in range(2):
                pass_on(z, k, part_of, way, 0)

    hid_local.wait()
    for step in range(X):
        arrived(hb.at[xs(step) * 2 + other], h_recv.at[xs(step), other])

    def project(zz):
        rows = hb[:, :, pl.ds(aligned(zz, 2 * COL), 2 * COL)].reshape(2 * X * ROWS, 2 * COL)
        block = wall[pl.ds(zz * 2, 2)].reshape(2 * COL, 2 * COL)
        return jnp.dot(rows, block, preferred_element_type=F32)

    acc[...] = project(z)
    for step in range(1, Z // 2 + 1):
        for k in range(2):
            for part_of in range(2):
                for way in range(2):
                    if step == Z // 2 and way != k:
                        continue
                    zz = zs(-ways[way] * step)
                    sem = 2 * k + part_of
                    arrived(wall.at[zz * 2 + pairs[k], pl.ds(part_of * 64, 64)], w_recv.at[zz, sem])
                    if k == 1 and step == last - 1 and way == k:
                        pass_on(zz, k, part_of, way, last, 2)
                    if step < last or (k == 0 and step == last and way == k):
                        pass_on(zz, k, part_of, way, step)
        if step < Z // 2:
            acc[...] += project(zs(-step)) + project(zs(step))

    early = list(sends)
    far = zs(Z // 2)
    far_cols = pl.ds(aligned(far, 2 * COL), 2 * COL)
    far_block = wall[pl.ds(far * 2, 2)].reshape(2 * COL, 2 * COL)
    for step in (2, 1, -1, 0):
        to = xs(step)
        rows = hb[pl.ds(to * 2, 2), :, far_cols].reshape(2 * ROWS, 2 * COL)
        sums = acc[pl.ds(aligned(to, 2 * ROWS), 2 * ROWS), :] + jnp.dot(rows, far_block, preferred_element_type=F32)
        part[pl.ds(to * 2, 2)] = sums.astype(BF16).reshape(2, ROWS, 2 * HD)
        for core in range(2):
            to_c = c if core == 0 else other
            if step == 0 and core == 0:
                ebuf[x, c] = part[x * 2 + c]
                continue
            start(
                copy(
                    part.at[to * 2 + to_c],
                    ebuf.at[x, c],
                    e_send.at[2 * (step % X) + core],
                    e_recv.at[x, c],
                    dev(x=to, c=to_c),
                )
            )
    for item in early:
        item.wait_send()
    for here, near in slices:
        pl.when(jnp.logical_not(here))(near.wait_send)
    for step in (0, 1, -1, 2):
        for core in range(2):
            from_c = c if core == 0 else other
            if step == 0 and core == 0:
                continue
            arrived(ebuf.at[xs(step), from_c], e_recv.at[xs(step), from_c])

    row = lax.broadcasted_iota(jnp.int32, (32, 256), 0)
    column = lax.broadcasted_iota(jnp.int32, (32, 256), 1)
    seen = (lax.rem(row, 8) == lax.rem(column, 8)) & (lax.rem(lax.div(column, 8), STEPS) >= lax.div(row, 8))
    news = []
    for h in range(2):
        total = ebuf[0, h].astype(F32)
        for src in range(1, X):
            total += ebuf[src, h].astype(F32)
        entries = total.astype(BF16)
        ent[:, h * 2 * HD : (h + 1) * 2 * HD] = entries
        fresh = entries.astype(F32)
        for G in range(3):
            rows = [fresh[s * DROWS + 8 * G : s * DROWS + 8 * G + 8] for s in range(STEPS)]
            news.append(jnp.concatenate(rows, axis=0).astype(BF16))
    outs_done.append(pltpu.make_async_copy(ent, refs["ent_out"], out_sem.at[3]))
    outs_done[-1].start()
    units = [(h, G) for h in range(2) for G in range(3)]
    scores = [
        lax.dot_general(new[:, :HD], qb[h, G], (((1,), (1,)), ((), ())), preferred_element_type=F32)
        for (h, G), new in zip(units, news)
    ]
    scores = [jnp.where(seen, item * HD ** (-0.5), masked_score) for item in scores]
    before = [ml[h, G, 0:1, :] for h, G in units]
    top = [jnp.maximum(old, jnp.max(item, axis=0, keepdims=True)) for old, item in zip(before, scores)]
    weights = [jnp.exp(item - high) for item, high in zip(scores, top)]
    scale = [jnp.exp(old - high) for old, high in zip(before, top)]
    whole = [
        ml[h, G, 1:2, :] * factor + jnp.sum(item, axis=0, keepdims=True)
        for (h, G), factor, item in zip(units, scale, weights)
    ]
    probs = [(item / full).astype(BF16) for item, full in zip(weights, whole)]
    mixed = [
        lax.dot_general(item, new[:, HD:], (((0,), (0,)), ((), ())), preferred_element_type=F32)
        for item, new in zip(probs, news)
    ]
    kept = [jnp.broadcast_to(factor / full, (HD, 256)).T for factor, full in zip(scale, whole)]
    outs = [oc[h, G] * share + item for (h, G), share, item in zip(units, kept, mixed)]
    for h in range(2):
        for j in range(8):
            rows = [
                outs[3 * h + G][(j * STEPS + s) * 8 : (j * STEPS + s) * 8 + 8] for s in range(STEPS) for G in range(3)
            ]
            att[:, (8 * h + j) * HD : (8 * h + j + 1) * HD] = jnp.concatenate(rows, axis=0).astype(BF16)
        cols_out = pl.ds(h * QW // 2, QW // 2)
        outs_done.append(pltpu.make_async_copy(att.at[:, cols_out], refs["att_out"].at[:, cols_out], out_sem.at[4 + h]))
        outs_done[-1].start()

    for item in outs_done:
        item.wait()
    for item in sends[len(early) :]:
        item.wait_send()


OUT_SHAPES = (
    jax.ShapeDtypeStruct((HALF, COL), BF16),
    jax.ShapeDtypeStruct((HALF, COL), F32),
    jax.ShapeDtypeStruct((HALF, COL), F32),
    jax.ShapeDtypeStruct((ROWS, 4 * HD), BF16),
    jax.ShapeDtypeStruct((ROWS, QW), BF16),
)


def write_out(*refs):
    count = len(OUT_SHAPES)
    sources, results, held, sems = refs[:count], refs[count : 2 * count], refs[2 * count : 3 * count], refs[-1]
    into = [pltpu.make_async_copy(sources[i], held[i], sems.at[0, i]) for i in range(count)]
    away = [pltpu.make_async_copy(held[i], results[i], sems.at[1, i]) for i in range(count)]
    for item in into:
        item.start()
    for first, second in zip(into, away):
        first.wait()
        second.start()
    for item in away:
        item.wait()


def body(
    acts,
    kv_grad,
    rewards,
    group_ids,
    kv_weight,
    adam_m,
    adam_v,
    hidden,
    queries,
    cache_keys,
    cache_values,
    cache_lens,
):
    hbm = pl.BlockSpec(memory_space=pltpu.HBM)
    dma = pltpu.SemaphoreType.DMA
    results = pl.pallas_call(
        kernel,
        out_shape=OUT_SHAPES,
        in_specs=[hbm] * 12,
        out_specs=(hbm,) * 5,
        scratch_shapes=[
            pltpu.VMEM((X, 2 * TOK, HALF), BF16),
            pltpu.VMEM((T, TOK, COL), BF16),
            pltpu.VMEM((T * COL, 2 * TOK), BF16),
            pltpu.VMEM((X, T * COL, HALF), BF16),
            pltpu.VMEM((X, 2, Z // 2, COL // 2, HALF), BF16),
            pltpu.VMEM((2, COL, HALF), BF16),
            pltpu.VMEM((ROWS, WIDTH), BF16),
            pltpu.VMEM((X, ROWS, KSL), BF16),
            pltpu.VMEM((2 * X, ROWS, KSL), BF16),
            pltpu.VMEM((HALF, COL), BF16),
            pltpu.VMEM((2 * Z, COL, 2 * COL), BF16),
            pltpu.VMEM((2 * X * ROWS, 2 * COL), F32),
            pltpu.VMEM((2 * X, ROWS, 2 * COL), BF16),
            pltpu.VMEM((X, 2, ROWS, 2 * COL), BF16),
            pltpu.VMEM((4, 8, 128), F32),
            pltpu.VMEM((Z, 8, 128), F32),
            pltpu.VMEM((HALF, COL), BF16),
            pltpu.VMEM((HALF, COL), F32),
            pltpu.VMEM((HALF, COL), F32),
            pltpu.SMEM((SEQ,), F32),
            pltpu.SMEM((SEQ,), jnp.int32),
            pltpu.SMEM((DROWS,), jnp.int32),
            pltpu.VMEM((ROWS, QW), BF16),
            pltpu.VMEM((2, 3, 256, HD), BF16),
            pltpu.VMEM((DROWS, CACHE, 2 * HD), BF16),
            pltpu.VMEM((DROWS, CACHE, 2 * HD), BF16),
            pltpu.VMEM((2, 3, 256, HD), F32),
            pltpu.VMEM((2, 3, 8, 256), F32),
            pltpu.VMEM((ROWS, 4 * HD), BF16),
            pltpu.VMEM((ROWS, QW), BF16),
            dma((13,)),
            dma((7,)),
            dma((X, 2)),
            dma((2 * T,)),
            dma((2 * T,)),
            dma((Z + 3,)),
            dma((Z + 4,)),
            dma((X, 2, Z // 2)),
            dma((X, 2, Z // 2)),
            dma((X,)),
            dma((2, 2)),
            dma((2 * X,)),
            dma((X, 2)),
            dma((4,)),
            dma((2, 2)),
            dma((2, 4, Z // 2)),
            dma((Z, 4)),
            dma((2 * X,)),
            dma((X, 2)),
            dma((6,)),
        ],
        compiler_params=pltpu.CompilerParams(
            collective_id=0, has_side_effects=True, vmem_limit_bytes=63400000
        ),
        name="update_and_decode",
    )(
        acts,
        kv_grad,
        rewards,
        group_ids,
        kv_weight,
        adam_m,
        adam_v,
        hidden.reshape(ROWS, WIDTH),
        queries.reshape(ROWS, QW),
        cache_keys,
        cache_values,
        cache_lens,
    )
    new_weight, new_m, new_v, new_entries, attention = pl.pallas_call(
        write_out,
        out_shape=OUT_SHAPES,
        in_specs=[hbm] * 5,
        out_specs=(hbm,) * 5,
        scratch_shapes=[pltpu.VMEM(item.shape, item.dtype) for item in OUT_SHAPES] + [dma((2, 5))],
        compiler_params=pltpu.CompilerParams(vmem_limit_bytes=63400000),
        name="write_out",
    )(*results)
    return (
        new_weight,
        new_m,
        new_v,
        new_entries.reshape(STEPS, DROWS, 4 * HD),
        attention.reshape(STEPS, DROWS, QW),
    )


def solution(mesh):
    return jax.shard_map(
        body,
        mesh=mesh,
        in_specs=(
            P("fsdp", ("tp", "dp")),
            P("fsdp", ("tp", "dp")),
            P("fsdp"),
            P("fsdp"),
            P("fsdp", ("tp", "dp")),
            P("fsdp", ("tp", "dp")),
            P("fsdp", ("tp", "dp")),
            P(None, ("fsdp", "dp"), None),
            P(None, ("fsdp", "dp"), "tp"),
            P(("fsdp", "dp"), None, "tp"),
            P(("fsdp", "dp"), None, "tp"),
            P(("fsdp", "dp")),
        ),
        out_specs=(
            P("fsdp", ("tp", "dp")),
            P("fsdp", ("tp", "dp")),
            P("fsdp", ("tp", "dp")),
            P(None, ("fsdp", "dp"), "tp"),
            P(None, ("fsdp", "dp"), "tp"),
        ),
        check_vma=False,
    )
```

```python
import jax
import jax.numpy as jnp
from jax import lax
from jax.experimental import pallas as pl
from jax.experimental.pallas import tpu as pltpu
from jax.sharding import PartitionSpec as P

HD = 128
LEN = 48
GSIZE = 8
X = 4
T = 4
Z = 8
TOK = 384
SEQ = 8
FEAT = 512
HALF = 256
COL = 128
STEPS = 4
DROWS = 24
ROWS = 96
CACHE = 64
QW = 2048
WIDTH = 8192
KSL = WIDTH // X

beta_one = 0.9
beta_two = 0.95
learn_rate = 0.001
decay_rate = 0.1
adam_eps = 1e-08
correct_one = 1.0 - beta_one**10
correct_two = 1.0 - beta_two**10
masked_score = -1e30

MESH = pl.DeviceIdType.MESH
F32 = jnp.float32
BF16 = jnp.bfloat16


def aligned(value, multiple):
    return pl.multiple_of(value * multiple, multiple)

NAMES = (
    "acts", "kv", "rew", "ids", "w_in", "m_in", "v_in", "hid", "qry", "ckey", "cval", "lens", "nw_out",
    "nm_out", "nv_out", "ent_out", "att_out", "abuf", "kbuf", "wt", "pbuf", "rsbuf", "own", "hv", "hl", "hb",
    "nwb", "wall", "acc", "part", "ebuf", "ra", "rb", "wv", "mv", "vv", "rs", "ls", "ns", "qv", "qb", "ck", "cv",
    "oc", "ml", "ent", "att",  "loc_sem", "a_send", "a_recv", "k_send", "k_recv", "r_send", "r_recv", "rs_send",
    "rs_recv", "o_send", "o_recv", "h_send", "h_recv", "c_send", "c_recv", "w_send", "w_recv", "e_send",
    "e_recv", "out_sem",
)


def kernel(*all_refs):
    refs = dict(zip(NAMES, all_refs))
    acts, kv, hid = refs["acts"], refs["kv"], refs["hid"]
    abuf, kbuf, wt, pbuf, rsbuf, own = (refs[k] for k in ("abuf", "kbuf", "wt", "pbuf", "rsbuf", "own"))
    hv, hl, hb, nwb, wall, acc = (refs[k] for k in ("hv", "hl", "hb", "nwb", "wall", "acc"))
    part, ebuf, ra, rb = (refs[k] for k in ("part", "ebuf", "ra", "rb"))
    wv, mv, vv = (refs[k] for k in ("wv", "mv", "vv"))
    qv, qb, ck, cv, oc, ml = (refs[k] for k in ("qv", "qb", "ck", "cv", "oc", "ml"))
    loc_sem, a_send, a_recv, k_send, k_recv = (refs[k] for k in NAMES[NAMES.index("loc_sem") :][:5])
    r_send, r_recv, rs_send, rs_recv, o_send, o_recv = (refs[k] for k in NAMES[NAMES.index("r_send") :][:6])
    h_send, h_recv, c_send, c_recv = (refs[k] for k in NAMES[NAMES.index("h_send") :][:4])
    w_send, w_recv, e_send, e_recv, out_sem = (refs[k] for k in NAMES[NAMES.index("w_send") :][:5])
    ent, att = refs["ent"], refs["att"]

    f, t, x = lax.axis_index("fsdp"), lax.axis_index("tp"), lax.axis_index("dp")
    z, g = lax.div(f, 4), lax.rem(f, 4)
    yh, c = lax.div(g, 2), lax.rem(g, 2)
    other, yo = 1 - c, 1 - yh

    def dev(z=z, yh=yh, c=c, t=t, x=x):
        return (z * 4 + yh * 2 + c, t, x)

    def copy(src, dst, send, recv, to):
        return pltpu.make_async_remote_copy(
            src_ref=src, dst_ref=dst, send_sem=send, recv_sem=recv, device_id=to, device_id_type=MESH
        )

    def arrived(dst, recv):
        copy(dst, dst, o_send.at[0], recv, dev(c=other)).wait_recv()

    def xs(step):
        return lax.rem(x + step + X, X)

    def zs(step):
        return lax.rem(z + step + Z, Z)

    def run_of(order):
        return jnp.bitwise_xor(jnp.bitwise_xor(t, order), 1)

    def half_of(src, slot):
        u = lax.rem(slot - 2 * t - lax.div(src, 2) + 2 * Z, Z)
        upper = jnp.where((u >= 1) & (u <= 4), 1, 0)
        return run_of(jnp.where(upper == 1, u - 1, lax.rem(Z - u, Z))), upper

    half = pl.ds(aligned(c, HALF), HALF)
    mine, other_rows = pl.ds(aligned(c, TOK), TOK), pl.ds(aligned(other, TOK), TOK)
    local = [
        pltpu.make_async_copy(src, dst, loc_sem.at[i])
        for i, (src, dst) in enumerate(
            (
                (refs["rew"], refs["rs"]),
                (refs["ids"], refs["ls"]),
                (kv, kbuf.at[t]),
                (refs["lens"], refs["ns"]),
                (refs["qry"], qv),
                (refs["ckey"], ck),
                (refs["cval"], cv),
                (acts.at[:, half], abuf.at[x, mine]),
                (hid, hv),
                (refs["w_in"], wv),
                (refs["m_in"], mv),
                (refs["v_in"], vv),
            )
        )
    ]
    for item in local[:2]:
        item.start()

    barrier = pltpu.get_barrier_semaphore()
    senders = [dev(z=zs(step)) for step in (4, 3, -3, 2, -2, 1, -1)]
    senders += [dev(yh=yo), dev(yh=yo, c=other)]
    senders += [dev(t=lax.rem(t + step, T)) for step in range(1, T)]
    senders += [dev(x=xs(step), c=core) for step in (1, -1) for core in range(2)]
    senders += [dev(c=other)]
    for sender in senders:
        pl.semaphore_signal(barrier, inc=1, device_id=sender, device_id_type=MESH)

    local[0].wait()
    local[1].wait()
    sub = lax.broadcasted_iota(jnp.int32, (8, 128), 0)
    lane = lax.broadcasted_iota(jnp.int32, (8, 128), 1)
    rew_row = jnp.zeros((8, 128), F32)
    id_row = jnp.full((8, 128), -1, jnp.int32)
    for seq in range(SEQ):
        rew_row = jnp.where(lane == seq, refs["rs"][seq], rew_row)
        id_row = jnp.where(lane == seq, refs["ls"][seq], id_row)
    id_row = id_row.astype(F32)
    ra[g] = jnp.where(sub == 2 * g, rew_row, jnp.where(sub == 2 * g + 1, id_row, 0.0))

    pl.semaphore_wait(barrier, len(senders))

    sends = []

    def start(item):
        item.start()
        sends.append(item)

    trio = ((yh, other), (yo, c), (yo, other))
    for step, (to_yh, to_c) in enumerate(trio):
        start(copy(ra.at[g], ra.at[g], r_send.at[step], r_recv.at[g], dev(yh=to_yh, c=to_c)))

    for step, sign in ((0, 1 - 2 * c), (1, 2 * c - 1)):
        for core in range(2):
            start(
                copy(
                    acts.at[:, pl.ds(core * HALF, HALF)],
                    abuf.at[x, mine],
                    a_send.at[2 * step + core],
                    a_recv.at[x, c],
                    dev(x=xs(sign), c=core),
                )
            )
    for step in range(1, T):
        start(copy(kv, kbuf.at[t], k_send.at[step], k_recv.at[t], dev(t=lax.rem(t + step, T))))
    start(
        copy(
            acts.at[:, pl.ds(aligned(other, HALF), HALF)],
            abuf.at[x, mine],
            a_send.at[4],
            a_recv.at[x, c],
            dev(c=other),
        )
    )

    for item in local[2:]:
        item.start()

    def cached(h, G):
        keys = ck[8 * G : 8 * G + 8, :, h * HD : (h + 1) * HD].reshape(8 * CACHE, HD)
        values = cv[8 * G : 8 * G + 8, :, h * HD : (h + 1) * HD].reshape(8 * CACHE, HD)
        scores = lax.dot_general(qb[h, G], keys, (((1,), (1,)), ((), ())), preferred_element_type=F32)
        scores *= HD ** (-0.5)
        column = lax.broadcasted_iota(jnp.int32, (1, 8 * CACHE), 1)
        limit = jnp.zeros((1, 8 * CACHE), jnp.int32)
        for row in range(8):
            limit = jnp.where(lax.div(column, CACHE) == row, refs["ns"][8 * G + row], limit)
        owner = jnp.where(lax.rem(column, CACHE) < limit, lax.div(column, CACHE), -1)
        row = lax.rem(lax.broadcasted_iota(jnp.int32, (256, 1), 0), 8)
        scores = jnp.where(row == owner, scores, masked_score)
        top = jnp.max(scores, axis=1, keepdims=True)
        weights = jnp.exp(scores - top)
        place = lax.broadcasted_iota(jnp.int32, (256, HD), 1)
        stats = jnp.where(place == 0, top, jnp.where(place == 1, jnp.sum(weights, axis=1, keepdims=True), 0.0))
        ml[h, G] = stats.T[0:8, :]
        oc[h, G] = jnp.dot(weights.astype(BF16), values, preferred_element_type=F32)

    for to_yh, to_c in trio:
        arrived(ra.at[to_yh * 2 + to_c], r_recv.at[to_yh * 2 + to_c])
    rb[z] = ra[0] + ra[1] + ra[2] + ra[3]
    for step in range(1, Z):
        start(copy(rb.at[z], rb.at[z], r_send.at[3 + step], r_recv.at[4 + z], dev(z=zs(step))))

    local[8].wait()
    for q in range(WIDTH // FEAT):
        for to in range(X):
            hl[to, :, q * 128 : (q + 1) * 128] = hv[:, q * FEAT + to * 128 : q * FEAT + (to + 1) * 128]

    for step in range(1, Z):
        arrived(rb.at[zs(step)], r_recv.at[4 + zs(step)])
    rew_col = jnp.sum(jnp.where(sub == lane, rew_row, 0.0), axis=1, keepdims=True)
    id_col = jnp.sum(jnp.where(sub == lane, id_row, 0.0), axis=1, keepdims=True)
    sums = jnp.zeros((8, 128), F32)
    for zz in range(Z):
        for group in range(4):
            same = rb[zz, 2 * group + 1 : 2 * group + 2, :] == id_col
            sums += jnp.where(same, rb[zz, 2 * group : 2 * group + 1, :], 0.0)
    advantage = rew_col - jnp.sum(sums, axis=1, keepdims=True) / GSIZE

    def weigh(src, step):
        columns = [
            advantage[seq : seq + 1, 0:1] * kbuf[src, seq * LEN : (seq + 1) * LEN, :].astype(F32) for seq in range(SEQ)
        ]
        rows = pl.ds(aligned(src, COL), COL)
        wt[rows, mine] = jnp.concatenate(columns, axis=0).T.astype(BF16)
        start(copy(wt.at[rows, mine], wt.at[rows, mine], k_send.at[T + step], k_recv.at[T + src], dev(c=other)))

    local[2].wait()
    weigh(t, 0)

    left, right, across = xs(-1), xs(1), xs(2)
    first, second = pl.ds(0, TOK), pl.ds(TOK, TOK)
    arrived(abuf.at[left, first], a_recv.at[left, 0])
    start(copy(abuf.at[left, first], abuf.at[left, first], a_send.at[5], a_recv.at[left, 0], dev(x=right)))
    arrived(abuf.at[right, second], a_recv.at[right, 1])
    start(copy(abuf.at[right, second], abuf.at[right, second], a_send.at[6], a_recv.at[right, 1], dev(x=left)))

    for step in (1, 3, 2):
        src = jnp.bitwise_xor(t, step)
        arrived(kbuf.at[src], k_recv.at[src])
        weigh(src, step)

    for src in range(T):
        arrived(wt.at[pl.ds(src * COL, COL), other_rows], k_recv.at[T + src])

    blocks = (x, left, right, across)
    ways = (1, -1)

    last = Z // 2 - 1

    def hops(block, way):
        return last + 1 if block == 0 and way == 0 else last

    def jumps(block, way):
        return block > 0 and way == block % 2

    def own_piece(block, slot):
        run, upper = half_of(blocks[block], slot)
        return pbuf.at[block, pl.ds(aligned(2 * run + upper, COL // 2), COL // 2)]

    def ring_copy(src, block, way, step, jump=1):
        return copy(
            src,
            rsbuf.at[block, way, step],
            rs_send.at[block, way, step],
            rs_recv.at[block, way, step],
            dev(z=zs(ways[way] * jump)),
        )

    def multiply(block):
        pbuf[block] = jnp.dot(wt[...], abuf[blocks[block]], preferred_element_type=F32).astype(BF16)
        for way in range(2):
            if jumps(block, way):
                start(ring_copy(own_piece(block, zs(Z // 2)), block, way, last, 2))
            start(ring_copy(own_piece(block, zs(ways[way] * hops(block, way))), block, way, 0))

    def multiply_late(block):
        pbuf[block] = jnp.dot(wt[...], abuf[blocks[block]], preferred_element_type=F32).astype(BF16)
        start(ring_copy(own_piece(block, zs(Z // 2)), block, block % 2, 3, 2))
        for way in range(2):
            start(ring_copy(own_piece(block, zs(ways[way] * 3)), block, way, 0))
        for way in range(2):
            start(ring_copy(own_piece(block, zs(ways[way])), block, way, 2))

    def late_step(block):
        for way in range(2):
            here = rsbuf.at[block, way, 0]
            arrived(here, rs_recv.at[block, way, 0])
            total = here[...].astype(F32) + own_piece(block, zs(ways[way] * 2))[...].astype(F32)
            if way == block % 2:
                arrived(rsbuf.at[block, way, 3], rs_recv.at[block, way, 3])
                total += rsbuf[block, way, 3].astype(F32)
            here[...] = total.astype(BF16)
            start(ring_copy(here, block, way, 1, 2))

    def ring_step(block, step):
        for way in range(2):
            if step + 1 >= hops(block, way):
                continue
            here = rsbuf.at[block, way, step]
            arrived(here, rs_recv.at[block, way, step])
            slot = zs(ways[way] * (hops(block, way) - 1 - step))
            total = here[...].astype(F32) + own_piece(block, slot)[...].astype(F32)
            if step == 0 and jumps(block, way):
                arrived(rsbuf.at[block, way, last], rs_recv.at[block, way, last])
                total += rsbuf[block, way, last].astype(F32)
            here[...] = total.astype(BF16)
            start(ring_copy(here, block, way, step + 1))

    local[7].wait()
    arrived(abuf.at[x, other_rows], a_recv.at[x, other])
    multiply(0)
    arrived(abuf.at[left, second], a_recv.at[left, 1])
    multiply(1)
    arrived(abuf.at[right, first], a_recv.at[right, 0])
    multiply(2)
    ring_step(0, 0)
    arrived(abuf.at[across, first], a_recv.at[across, 0])
    arrived(abuf.at[across, second], a_recv.at[across, 1])

    multiply_late(3)

    hslot = hb.at[x * 2 + c]
    hid_local = pltpu.make_async_copy(hl.at[x], hslot, loc_sem.at[12])
    hid_local.start()
    for step in (1, -1, 2):
        start(copy(hl.at[xs(step)], hslot, h_send.at[step % X], h_recv.at[x, c], dev(x=xs(step))))
    start(copy(hl.at[x], hslot, h_send.at[0], h_recv.at[x, c], dev(c=other)))

    to_owners = []

    def ring_end(block):
        total = own_piece(block, z)[...].astype(F32)
        for way in range(2):
            for step in (2, 1) if block == X - 1 else (hops(block, way) - 1,):
                arrived(rsbuf.at[block, way, step], rs_recv.at[block, way, step])
                total += rsbuf[block, way, step].astype(F32)
        here = rsbuf.at[block, 1 - block % 2, last]
        here[...] = total.astype(BF16)
        src = blocks[block]
        run, upper = half_of(src, z)
        to_owners.append(
            copy(
                here,
                own.at[yh, pl.ds(aligned(upper, COL // 2), COL // 2)],
                o_send.at[block],
                o_recv.at[yh, upper],
                dev(z=2 * t + lax.div(src, 2), yh=lax.rem(src, 2), t=run),
            )
        )

    for block, step in ((1, 0), (2, 0), (0, 1), (1, 1), (3, 0), (2, 1), (0, 2)):
        if block == X - 1:
            late_step(block)
        else:
            ring_step(block, step)
    for block in (1, 2, 3, 0):
        ring_end(block)
    for item in to_owners:
        start(item)

    for item in local[3:7]:
        item.wait()
    for h in range(2):
        tiles = [qv[:, (8 * h + j) * HD : (8 * h + j + 1) * HD].astype(F32) for j in range(8)]
        for G in range(3):
            rows = [tiles[j][s * DROWS + 8 * G : s * DROWS + 8 * G + 8] for j in range(8) for s in range(STEPS)]
            qb[h, G] = jnp.concatenate(rows, axis=0).astype(BF16)

    for G in range(3):
        cached(0, G)
    cached(1, 0)

    for item in local[9:]:
        item.wait()
    for from_yh in range(2):
        for upper in range(2):
            arrived(own.at[from_yh, pl.ds(upper * COL // 2, COL // 2)], o_recv.at[from_yh, upper])
    weight_grad = (own[0].astype(F32) + own[1].astype(F32)).T / LEN
    new_m = beta_one * mv[...] + (1.0 - beta_one) * weight_grad
    new_v = beta_two * vv[...] + (1.0 - beta_two) * weight_grad * weight_grad
    weight_f = wv[...].astype(F32)
    direction = new_m / correct_one / (jnp.sqrt(new_v / correct_two) + adam_eps)
    new_weight = (weight_f - learn_rate * (direction + decay_rate * weight_f)).astype(BF16)
    nwb[...] = new_weight

    is_self = c == lax.div(x, 2)
    cols = pl.ds(aligned(lax.rem(x, 2), COL), COL)
    slices = []
    for r in range(2):
        src = nwb.at[pl.ds(r * COL, COL)]
        dst = wall.at[z * 2 + yh, :, cols]
        recv = c_recv.at[yh, lax.rem(x, 2)]
        near = copy(src, dst, c_send.at[r], recv, dev(c=lax.div(x, 2), x=2 * c + r))
        far = copy(src, dst, c_send.at[2 + r], recv, dev(yh=yo, c=lax.div(x, 2), x=2 * c + r))
        here = is_self & (lax.rem(x, 2) == r)
        pl.when(jnp.logical_not(here))(near.start)
        pl.when(here)(pltpu.make_async_copy(src, dst, recv).start)
        start(far)
        slices.append((here, near))

    cached(1, 1)
    cached(1, 2)
    mv[...] = new_m
    vv[...] = new_v
    outs_done = [
        pltpu.make_async_copy(src, refs[dst], out_sem.at[i])
        for i, (src, dst) in enumerate(((nwb, "nw_out"), (mv, "nm_out"), (vv, "nv_out")))
    ]
    for item in outs_done:
        item.start()

    for step in (1, -1, 2):
        slot = hb.at[xs(step) * 2 + c]
        arrived(slot, h_recv.at[xs(step), c])
        start(copy(slot, slot, h_send.at[X + step % X], h_recv.at[xs(step), c], dev(c=other)))

    pairs = (yh, yo)

    def pass_on(zz, k, part_of, way, step, jump=1):
        slot = wall.at[zz * 2 + pairs[k], pl.ds(part_of * 64, 64)]
        sem = 2 * k + part_of
        to = dev(z=zs(ways[way] * jump))
        start(copy(slot, slot, w_send.at[way, sem, step], w_recv.at[zz, sem], to))

    for k in range(2):
        for hh in range(2):
            arrived(wall.at[z * 2 + pairs[k], :, pl.ds(hh * COL, COL)], c_recv.at[pairs[k], hh])
        for part_of in range(2):
            for way in range(2):
                pass_on(z, k, part_of, way, 0)

    hid_local.wait()
    for step in range(X):
        arrived(hb.at[xs(step) * 2 + other], h_recv.at[xs(step), other])

    def project(zz):
        rows = hb[:, :, pl.ds(aligned(zz, 2 * COL), 2 * COL)].reshape(2 * X * ROWS, 2 * COL)
        block = wall[pl.ds(zz * 2, 2)].reshape(2 * COL, 2 * COL)
        return jnp.dot(rows, block, preferred_element_type=F32)

    acc[...] = project(z)
    for step in range(1, Z // 2 + 1):
        for k in range(2):
            for part_of in range(2):
                for way in range(2):
                    if step == Z // 2 and way != k:
                        continue
                    zz = zs(-ways[way] * step)
                    sem = 2 * k + part_of
                    arrived(wall.at[zz * 2 + pairs[k], pl.ds(part_of * 64, 64)], w_recv.at[zz, sem])
                    if k == 1 and step == last - 1 and way == k:
                        pass_on(zz, k, part_of, way, last, 2)
                    if step < last or (k == 0 and step == last and way == k):
                        pass_on(zz, k, part_of, way, step)
        if step < Z // 2:
            acc[...] += project(zs(-step)) + project(zs(step))

    early = list(sends)
    far = zs(Z // 2)
    far_cols = pl.ds(aligned(far, 2 * COL), 2 * COL)
    far_block = wall[pl.ds(far * 2, 2)].reshape(2 * COL, 2 * COL)
    for step in (2, 1, -1, 0):
        to = xs(step)
        rows = hb[pl.ds(to * 2, 2), :, far_cols].reshape(2 * ROWS, 2 * COL)
        sums = acc[pl.ds(aligned(to, 2 * ROWS), 2 * ROWS), :] + jnp.dot(rows, far_block, preferred_element_type=F32)
        part[pl.ds(to * 2, 2)] = sums.astype(BF16).reshape(2, ROWS, 2 * HD)
        for core in range(2):
            to_c = c if core == 0 else other
            if step == 0 and core == 0:
                ebuf[x, c] = part[x * 2 + c]
                continue
            start(
                copy(
                    part.at[to * 2 + to_c],
                    ebuf.at[x, c],
                    e_send.at[2 * (step % X) + core],
                    e_recv.at[x, c],
                    dev(x=to, c=to_c),
                )
            )
    for item in early:
        item.wait_send()
    for here, near in slices:
        pl.when(jnp.logical_not(here))(near.wait_send)
    for step in (0, 1, -1, 2):
        for core in range(2):
            from_c = c if core == 0 else other
            if step == 0 and core == 0:
                continue
            arrived(ebuf.at[xs(step), from_c], e_recv.at[xs(step), from_c])

    row = lax.broadcasted_iota(jnp.int32, (32, 256), 0)
    column = lax.broadcasted_iota(jnp.int32, (32, 256), 1)
    seen = (lax.rem(row, 8) == lax.rem(column, 8)) & (lax.rem(lax.div(column, 8), STEPS) >= lax.div(row, 8))
    news = []
    for h in range(2):
        total = ebuf[0, h].astype(F32)
        for src in range(1, X):
            total += ebuf[src, h].astype(F32)
        entries = total.astype(BF16)
        ent[:, h * 2 * HD : (h + 1) * 2 * HD] = entries
        fresh = entries.astype(F32)
        for G in range(3):
            rows = [fresh[s * DROWS + 8 * G : s * DROWS + 8 * G + 8] for s in range(STEPS)]
            news.append(jnp.concatenate(rows, axis=0).astype(BF16))
    outs_done.append(pltpu.make_async_copy(ent, refs["ent_out"], out_sem.at[3]))
    outs_done[-1].start()
    units = [(h, G) for h in range(2) for G in range(3)]
    scores = [
        lax.dot_general(new[:, :HD], qb[h, G], (((1,), (1,)), ((), ())), preferred_element_type=F32)
        for (h, G), new in zip(units, news)
    ]
    scores = [jnp.where(seen, item * HD ** (-0.5), masked_score) for item in scores]
    before = [ml[h, G, 0:1, :] for h, G in units]
    top = [jnp.maximum(old, jnp.max(item, axis=0, keepdims=True)) for old, item in zip(before, scores)]
    weights = [jnp.exp(item - high) for item, high in zip(scores, top)]
    scale = [jnp.exp(old - high) for old, high in zip(before, top)]
    whole = [
        ml[h, G, 1:2, :] * factor + jnp.sum(item, axis=0, keepdims=True)
        for (h, G), factor, item in zip(units, scale, weights)
    ]
    probs = [(item / full).astype(BF16) for item, full in zip(weights, whole)]
    mixed = [
        lax.dot_general(item, new[:, HD:], (((0,), (0,)), ((), ())), preferred_element_type=F32)
        for item, new in zip(probs, news)
    ]
    kept = [jnp.broadcast_to(factor / full, (HD, 256)).T for factor, full in zip(scale, whole)]
    outs = [oc[h, G] * share + item for (h, G), share, item in zip(units, kept, mixed)]
    for h in range(2):
        for j in range(8):
            rows = [
                outs[3 * h + G][(j * STEPS + s) * 8 : (j * STEPS + s) * 8 + 8] for s in range(STEPS) for G in range(3)
            ]
            att[:, (8 * h + j) * HD : (8 * h + j + 1) * HD] = jnp.concatenate(rows, axis=0).astype(BF16)
        cols_out = pl.ds(h * QW // 2, QW // 2)
        outs_done.append(pltpu.make_async_copy(att.at[:, cols_out], refs["att_out"].at[:, cols_out], out_sem.at[4 + h]))
        outs_done[-1].start()

    for item in outs_done:
        item.wait()
    for item in sends[len(early) :]:
        item.wait_send()


OUT_SHAPES = (
    jax.ShapeDtypeStruct((HALF, COL), BF16),
    jax.ShapeDtypeStruct((HALF, COL), F32),
    jax.ShapeDtypeStruct((HALF, COL), F32),
    jax.ShapeDtypeStruct((ROWS, 4 * HD), BF16),
    jax.ShapeDtypeStruct((ROWS, QW), BF16),
)


def write_out(*refs):
    count = len(OUT_SHAPES)
    sources, results, held, sems = refs[:count], refs[count : 2 * count], refs[2 * count : 3 * count], refs[-1]
    into = [pltpu.make_async_copy(sources[i], held[i], sems.at[0, i]) for i in range(count)]
    away = [pltpu.make_async_copy(held[i], results[i], sems.at[1, i]) for i in range(count)]
    for item in into:
        item.start()
    for first, second in zip(into, away):
        first.wait()
        second.start()
    for item in away:
        item.wait()


def body(
    acts,
    kv_grad,
    rewards,
    group_ids,
    kv_weight,
    adam_m,
    adam_v,
    hidden,
    queries,
    cache_keys,
    cache_values,
    cache_lens,
):
    hbm = pl.BlockSpec(memory_space=pltpu.HBM)
    dma = pltpu.SemaphoreType.DMA
    results = pl.pallas_call(
        kernel,
        out_shape=OUT_SHAPES,
        in_specs=[hbm] * 12,
        out_specs=(hbm,) * 5,
        scratch_shapes=[
            pltpu.VMEM((X, 2 * TOK, HALF), BF16),
            pltpu.VMEM((T, TOK, COL), BF16),
            pltpu.VMEM((T * COL, 2 * TOK), BF16),
            pltpu.VMEM((X, T * COL, HALF), BF16),
            pltpu.VMEM((X, 2, Z // 2, COL // 2, HALF), BF16),
            pltpu.VMEM((2, COL, HALF), BF16),
            pltpu.VMEM((ROWS, WIDTH), BF16),
            pltpu.VMEM((X, ROWS, KSL), BF16),
            pltpu.VMEM((2 * X, ROWS, KSL), BF16),
            pltpu.VMEM((HALF, COL), BF16),
            pltpu.VMEM((2 * Z, COL, 2 * COL), BF16),
            pltpu.VMEM((2 * X * ROWS, 2 * COL), F32),
            pltpu.VMEM((2 * X, ROWS, 2 * COL), BF16),
            pltpu.VMEM((X, 2, ROWS, 2 * COL), BF16),
            pltpu.VMEM((4, 8, 128), F32),
            pltpu.VMEM((Z, 8, 128), F32),
            pltpu.VMEM((HALF, COL), BF16),
            pltpu.VMEM((HALF, COL), F32),
            pltpu.VMEM((HALF, COL), F32),
            pltpu.SMEM((SEQ,), F32),
            pltpu.SMEM((SEQ,), jnp.int32),
            pltpu.SMEM((DROWS,), jnp.int32),
            pltpu.VMEM((ROWS, QW), BF16),
            pltpu.VMEM((2, 3, 256, HD), BF16),
            pltpu.VMEM((DROWS, CACHE, 2 * HD), BF16),
            pltpu.VMEM((DROWS, CACHE, 2 * HD), BF16),
            pltpu.VMEM((2, 3, 256, HD), F32),
            pltpu.VMEM((2, 3, 8, 256), F32),
            pltpu.VMEM((ROWS, 4 * HD), BF16),
            pltpu.VMEM((ROWS, QW), BF16),
            dma((13,)),
            dma((7,)),
            dma((X, 2)),
            dma((2 * T,)),
            dma((2 * T,)),
            dma((Z + 3,)),
            dma((Z + 4,)),
            dma((X, 2, Z // 2)),
            dma((X, 2, Z // 2)),
            dma((X,)),
            dma((2, 2)),
            dma((2 * X,)),
            dma((X, 2)),
            dma((4,)),
            dma((2, 2)),
            dma((2, 4, Z // 2)),
            dma((Z, 4)),
            dma((2 * X,)),
            dma((X, 2)),
            dma((6,)),
        ],
        compiler_params=pltpu.CompilerParams(
            collective_id=0, has_side_effects=True, vmem_limit_bytes=63400000
        ),
        name="update_and_decode",
    )(
        acts,
        kv_grad,
        rewards,
        group_ids,
        kv_weight,
        adam_m,
        adam_v,
        hidden.reshape(ROWS, WIDTH),
        queries.reshape(ROWS, QW),
        cache_keys,
        cache_values,
        cache_lens,
    )
    new_weight, new_m, new_v, new_entries, attention = pl.pallas_call(
        write_out,
        out_shape=OUT_SHAPES,
        in_specs=[hbm] * 5,
        out_specs=(hbm,) * 5,
        scratch_shapes=[pltpu.VMEM(item.shape, item.dtype) for item in OUT_SHAPES] + [dma((2, 5))],
        compiler_params=pltpu.CompilerParams(vmem_limit_bytes=63400000),
        name="write_out",
    )(*results)
    return (
        new_weight,
        new_m,
        new_v,
        new_entries.reshape(STEPS, DROWS, 4 * HD),
        attention.reshape(STEPS, DROWS, QW),
    )


def solution(mesh):
    return jax.shard_map(
        body,
        mesh=mesh,
        in_specs=(
            P("fsdp", ("tp", "dp")),
            P("fsdp", ("tp", "dp")),
            P("fsdp"),
            P("fsdp"),
            P("fsdp", ("tp", "dp")),
            P("fsdp", ("tp", "dp")),
            P("fsdp", ("tp", "dp")),
            P(None, ("fsdp", "dp"), None),
            P(None, ("fsdp", "dp"), "tp"),
            P(("fsdp", "dp"), None, "tp"),
            P(("fsdp", "dp"), None, "tp"),
            P(("fsdp", "dp")),
        ),
        out_specs=(
            P("fsdp", ("tp", "dp")),
            P("fsdp", ("tp", "dp")),
            P("fsdp", ("tp", "dp")),
            P(None, ("fsdp", "dp"), "tp"),
            P(None, ("fsdp", "dp"), "tp"),
        ),
        check_vma=False,
    )
```

```python
import jax
import jax.numpy as jnp
from jax import lax
from jax.experimental import pallas as pl
from jax.experimental.pallas import tpu as pltpu
from jax.sharding import PartitionSpec as P

HD = 128
LEN = 48
GSIZE = 8
X = 4
T = 4
Z = 8
TOK = 384
SEQ = 8
FEAT = 512
HALF = 256
COL = 128
STEPS = 4
DROWS = 24
ROWS = 96
CACHE = 64
QW = 2048
WIDTH = 8192
KSL = WIDTH // X

beta_one = 0.9
beta_two = 0.95
learn_rate = 0.001
decay_rate = 0.1
adam_eps = 1e-08
correct_one = 1.0 - beta_one**10
correct_two = 1.0 - beta_two**10
masked_score = -1e30

MESH = pl.DeviceIdType.MESH
F32 = jnp.float32
BF16 = jnp.bfloat16


def aligned(value, multiple):
    return pl.multiple_of(value * multiple, multiple)

NAMES = (
    "acts", "kv", "rew", "ids", "w_in", "m_in", "v_in", "hid", "qry", "ckey", "cval", "lens", "nw_out",
    "nm_out", "nv_out", "ent_out", "att_out", "abuf", "kbuf", "wt", "pbuf", "rsbuf", "own", "hv", "hl", "hb",
    "nwb", "wall", "acc", "part", "ebuf", "ra", "rb", "wv", "mv", "vv", "rs", "ls", "ns", "qv", "qb", "ck", "cv",
    "oc", "ml", "pb", "ent", "att",  "loc_sem", "a_send", "a_recv", "k_send", "k_recv", "r_send", "r_recv", "rs_send",
    "rs_recv", "o_send", "o_recv", "h_send", "h_recv", "c_send", "c_recv", "w_send", "w_recv", "e_send",
    "e_recv", "out_sem",
)


def kernel(*all_refs):
    refs = dict(zip(NAMES, all_refs))
    acts, kv, hid = refs["acts"], refs["kv"], refs["hid"]
    abuf, kbuf, wt, pbuf, rsbuf, own = (refs[k] for k in ("abuf", "kbuf", "wt", "pbuf", "rsbuf", "own"))
    hv, hl, hb, nwb, wall, acc = (refs[k] for k in ("hv", "hl", "hb", "nwb", "wall", "acc"))
    part, ebuf, ra, rb = (refs[k] for k in ("part", "ebuf", "ra", "rb"))
    wv, mv, vv = (refs[k] for k in ("wv", "mv", "vv"))
    qv, qb, ck, cv, oc, ml, pb = (refs[k] for k in ("qv", "qb", "ck", "cv", "oc", "ml", "pb"))
    loc_sem, a_send, a_recv, k_send, k_recv = (refs[k] for k in NAMES[NAMES.index("loc_sem") :][:5])
    r_send, r_recv, rs_send, rs_recv, o_send, o_recv = (refs[k] for k in NAMES[NAMES.index("r_send") :][:6])
    h_send, h_recv, c_send, c_recv = (refs[k] for k in NAMES[NAMES.index("h_send") :][:4])
    w_send, w_recv, e_send, e_recv, out_sem = (refs[k] for k in NAMES[NAMES.index("w_send") :][:5])
    ent, att = refs["ent"], refs["att"]

    f, t, x = lax.axis_index("fsdp"), lax.axis_index("tp"), lax.axis_index("dp")
    z, g = lax.div(f, 4), lax.rem(f, 4)
    yh, c = lax.div(g, 2), lax.rem(g, 2)
    other, yo = 1 - c, 1 - yh

    def dev(z=z, yh=yh, c=c, t=t, x=x):
        return (z * 4 + yh * 2 + c, t, x)

    def copy(src, dst, send, recv, to):
        return pltpu.make_async_remote_copy(
            src_ref=src, dst_ref=dst, send_sem=send, recv_sem=recv, device_id=to, device_id_type=MESH
        )

    def arrived(dst, recv):
        copy(dst, dst, o_send.at[0], recv, dev(c=other)).wait_recv()

    def xs(step):
        return lax.rem(x + step + X, X)

    def zs(step):
        return lax.rem(z + step + Z, Z)

    def run_of(order):
        return jnp.bitwise_xor(jnp.bitwise_xor(t, order), 1)

    def half_of(src, slot):
        u = lax.rem(slot - 2 * t - lax.div(src, 2) + 2 * Z, Z)
        upper = jnp.where((u >= 1) & (u <= 4), 1, 0)
        return run_of(jnp.where(upper == 1, u - 1, lax.rem(Z - u, Z))), upper

    half = pl.ds(aligned(c, HALF), HALF)
    mine, other_rows = pl.ds(aligned(c, TOK), TOK), pl.ds(aligned(other, TOK), TOK)
    local = [
        pltpu.make_async_copy(src, dst, loc_sem.at[i])
        for i, (src, dst) in enumerate(
            (
                (refs["rew"], refs["rs"]),
                (refs["ids"], refs["ls"]),
                (kv, kbuf.at[t]),
                (refs["lens"], refs["ns"]),
                (refs["qry"], qv),
                (refs["ckey"], ck),
                (refs["cval"], cv),
                (acts.at[:, half], abuf.at[x, mine]),
                (hid, hv),
                (refs["w_in"], wv),
                (refs["m_in"], mv),
                (refs["v_in"], vv),
            )
        )
    ]
    for item in local[:2]:
        item.start()

    barrier = pltpu.get_barrier_semaphore()
    senders = [dev(z=zs(step)) for step in (4, 3, -3, 2, -2, 1, -1)]
    senders += [dev(yh=yo), dev(yh=yo, c=other)]
    senders += [dev(t=lax.rem(t + step, T)) for step in range(1, T)]
    senders += [dev(x=xs(step), c=core) for step in (1, -1) for core in range(2)]
    senders += [dev(c=other)]
    for sender in senders:
        pl.semaphore_signal(barrier, inc=1, device_id=sender, device_id_type=MESH)

    local[0].wait()
    local[1].wait()
    sub = lax.broadcasted_iota(jnp.int32, (8, 128), 0)
    lane = lax.broadcasted_iota(jnp.int32, (8, 128), 1)
    rew_row = jnp.zeros((8, 128), F32)
    id_row = jnp.full((8, 128), -1, jnp.int32)
    for seq in range(SEQ):
        rew_row = jnp.where(lane == seq, refs["rs"][seq], rew_row)
        id_row = jnp.where(lane == seq, refs["ls"][seq], id_row)
    id_row = id_row.astype(F32)
    ra[g] = jnp.where(sub == 2 * g, rew_row, jnp.where(sub == 2 * g + 1, id_row, 0.0))

    pl.semaphore_wait(barrier, len(senders))

    sends = []

    def start(item):
        item.start()
        sends.append(item)

    def sent(like, send):
        copy(like, like, send, o_recv.at[0], dev(c=other)).wait_send()

    trio = ((yh, other), (yo, c), (yo, other))
    for to_yh, to_c in trio:
        copy(ra.at[g], ra.at[g], r_send.at[0], r_recv.at[0], dev(yh=to_yh, c=to_c)).start()

    for sign in (1 - 2 * c, 2 * c - 1):
        for core in range(2):
            copy(
                acts.at[:, pl.ds(core * HALF, HALF)],
                abuf.at[x, mine],
                a_send.at[0],
                a_recv.at[x, c],
                dev(x=xs(sign), c=core),
            ).start()
    for step in range(1, T):
        copy(kv, kbuf.at[t], k_send.at[0], k_recv.at[t], dev(t=lax.rem(t + step, T))).start()
    copy(
        acts.at[:, pl.ds(aligned(other, HALF), HALF)],
        abuf.at[x, mine],
        a_send.at[0],
        a_recv.at[x, c],
        dev(c=other),
    ).start()

    for item in local[2:]:
        item.start()

    def cached(h, G):
        keys = ck[8 * G : 8 * G + 8, :, h * HD : (h + 1) * HD].reshape(8 * CACHE, HD)
        values = cv[8 * G : 8 * G + 8, :, h * HD : (h + 1) * HD].reshape(8 * CACHE, HD)
        scores = lax.dot_general(qb[h, G], keys, (((1,), (1,)), ((), ())), preferred_element_type=F32)
        scores *= HD ** (-0.5)
        column = lax.broadcasted_iota(jnp.int32, (1, 8 * CACHE), 1)
        limit = jnp.zeros((1, 8 * CACHE), jnp.int32)
        for row in range(8):
            limit = jnp.where(lax.div(column, CACHE) == row, refs["ns"][8 * G + row], limit)
        owner = jnp.where(lax.rem(column, CACHE) < limit, lax.div(column, CACHE), -1)
        row = lax.rem(lax.broadcasted_iota(jnp.int32, (256, 1), 0), 8)
        scores = jnp.where(row == owner, scores, masked_score)
        top = jnp.max(scores, axis=1, keepdims=True)
        weights = jnp.exp(scores - top)
        place = lax.broadcasted_iota(jnp.int32, (256, HD), 1)
        stats = jnp.where(place == 0, top, jnp.where(place == 1, jnp.sum(weights, axis=1, keepdims=True), 0.0))
        ml[h, G] = stats.T[0:8, :]
        oc[h, G] = jnp.dot(weights.astype(BF16), values, preferred_element_type=F32)

    arrived(ra.at[pl.ds(0, 3)], r_recv.at[0])
    rb[z] = ra[0] + ra[1] + ra[2] + ra[3]
    for step in range(1, Z):
        copy(rb.at[z], rb.at[z], r_send.at[0], r_recv.at[1], dev(z=zs(step))).start()

    local[8].wait()
    for q in range(WIDTH // FEAT):
        for to in range(X):
            hl[to, :, q * 128 : (q + 1) * 128] = hv[:, q * FEAT + to * 128 : q * FEAT + (to + 1) * 128]

    arrived(rb.at[pl.ds(0, Z - 1)], r_recv.at[1])
    rew_col = jnp.sum(jnp.where(sub == lane, rew_row, 0.0), axis=1, keepdims=True)
    id_col = jnp.sum(jnp.where(sub == lane, id_row, 0.0), axis=1, keepdims=True)
    sums = jnp.zeros((8, 128), F32)
    for zz in range(Z):
        for group in range(4):
            same = rb[zz, 2 * group + 1 : 2 * group + 2, :] == id_col
            sums += jnp.where(same, rb[zz, 2 * group : 2 * group + 1, :], 0.0)
    advantage = rew_col - jnp.sum(sums, axis=1, keepdims=True) / GSIZE

    def weigh(src):
        columns = [
            advantage[seq : seq + 1, 0:1] * kbuf[src, seq * LEN : (seq + 1) * LEN, :].astype(F32) for seq in range(SEQ)
        ]
        rows = pl.ds(aligned(src, COL), COL)
        wt[rows, mine] = jnp.concatenate(columns, axis=0).T.astype(BF16)
        copy(wt.at[rows, mine], wt.at[rows, mine], k_send.at[0], k_recv.at[T], dev(c=other)).start()

    local[2].wait()
    weigh(t)

    left, right, across = xs(-1), xs(1), xs(2)
    first, second = pl.ds(0, TOK), pl.ds(TOK, TOK)
    arrived(abuf.at[left, first], a_recv.at[left, 0])
    copy(abuf.at[left, first], abuf.at[left, first], a_send.at[0], a_recv.at[left, 0], dev(x=right)).start()
    arrived(abuf.at[right, second], a_recv.at[right, 1])
    copy(abuf.at[right, second], abuf.at[right, second], a_send.at[0], a_recv.at[right, 1], dev(x=left)).start()

    for step in (1, 3, 2):
        src = jnp.bitwise_xor(t, step)
        arrived(kbuf.at[src], k_recv.at[src])
        weigh(src)

    arrived(wt.at[:, other_rows], k_recv.at[T])

    blocks = (x, left, right, across)
    ways = (1, -1)

    last = Z // 2 - 1

    def hops(block, way):
        return last + 1 if block == 0 and way == 0 else last

    def jumps(block, way):
        return block > 0 and way == block % 2

    def own_piece(block, slot):
        run, upper = half_of(blocks[block], slot)
        return pbuf.at[block, pl.ds(aligned(2 * run + upper, COL // 2), COL // 2)]

    def begin(item):
        item.start()

    def ring_copy(src, block, way, step, jump=1):
        return copy(
            src,
            rsbuf.at[block, way, step],
            rs_send.at[0],
            rs_recv.at[block, way, step],
            dev(z=zs(ways[way] * jump)),
        )

    def multiply(block):
        pbuf[block] = jnp.dot(wt[...], abuf[blocks[block]], preferred_element_type=F32).astype(BF16)
        for way in range(2):
            if jumps(block, way):
                begin(ring_copy(own_piece(block, zs(Z // 2)), block, way, last, 2))
            begin(ring_copy(own_piece(block, zs(ways[way] * hops(block, way))), block, way, 0))

    def multiply_late(block):
        pbuf[block] = jnp.dot(wt[...], abuf[blocks[block]], preferred_element_type=F32).astype(BF16)
        begin(ring_copy(own_piece(block, zs(Z // 2)), block, block % 2, 3, 2))
        for way in range(2):
            begin(ring_copy(own_piece(block, zs(ways[way] * 3)), block, way, 0))
        for way in range(2):
            begin(ring_copy(own_piece(block, zs(ways[way])), block, way, 2))

    def late_step(block):
        for way in range(2):
            here = rsbuf.at[block, way, 0]
            arrived(here, rs_recv.at[block, way, 0])
            total = here[...].astype(F32) + own_piece(block, zs(ways[way] * 2))[...].astype(F32)
            if way == block % 2:
                arrived(rsbuf.at[block, way, 3], rs_recv.at[block, way, 3])
                total += rsbuf[block, way, 3].astype(F32)
            here[...] = total.astype(BF16)
            begin(ring_copy(here, block, way, 1, 2))

    def ring_step(block, step):
        for way in range(2):
            if step + 1 >= hops(block, way):
                continue
            here = rsbuf.at[block, way, step]
            arrived(here, rs_recv.at[block, way, step])
            slot = zs(ways[way] * (hops(block, way) - 1 - step))
            total = here[...].astype(F32) + own_piece(block, slot)[...].astype(F32)
            if step == 0 and jumps(block, way):
                arrived(rsbuf.at[block, way, last], rs_recv.at[block, way, last])
                total += rsbuf[block, way, last].astype(F32)
            here[...] = total.astype(BF16)
            begin(ring_copy(here, block, way, step + 1))

    local[7].wait()
    arrived(abuf.at[x, other_rows], a_recv.at[x, other])
    multiply(0)
    arrived(abuf.at[left, second], a_recv.at[left, 1])
    multiply(1)
    arrived(abuf.at[right, first], a_recv.at[right, 0])
    multiply(2)
    ring_step(0, 0)
    arrived(abuf.at[across, first], a_recv.at[across, 0])
    arrived(abuf.at[across, second], a_recv.at[across, 1])

    multiply_late(3)

    hslot = hb.at[x * 2 + c]
    hid_local = pltpu.make_async_copy(hl.at[x], hslot, loc_sem.at[12])
    hid_local.start()
    for step in (1, -1, 2):
        copy(hl.at[xs(step)], hslot, h_send.at[0], h_recv.at[x], dev(x=xs(step))).start()
    copy(hl.at[x], hslot, h_send.at[0], h_recv.at[X], dev(c=other)).start()

    to_owners = []

    def ring_end(block):
        total = own_piece(block, z)[...].astype(F32)
        for way in range(2):
            for step in (2, 1) if block == X - 1 else (hops(block, way) - 1,):
                arrived(rsbuf.at[block, way, step], rs_recv.at[block, way, step])
                total += rsbuf[block, way, step].astype(F32)
        here = rsbuf.at[block, 1 - block % 2, last]
        here[...] = total.astype(BF16)
        src = blocks[block]
        run, upper = half_of(src, z)
        to_owners.append(
            copy(
                here,
                own.at[yh, pl.ds(aligned(upper, COL // 2), COL // 2)],
                o_send.at[block],
                o_recv.at[0],
                dev(z=2 * t + lax.div(src, 2), yh=lax.rem(src, 2), t=run),
            )
        )

    for block, step in ((1, 0), (2, 0), (0, 1), (1, 1), (3, 0), (2, 1), (0, 2)):
        if block == X - 1:
            late_step(block)
        else:
            ring_step(block, step)
    for block in (1, 2, 3, 0):
        ring_end(block)
    for item in to_owners:
        start(item)

    for item in local[3:7]:
        item.wait()
    for h in range(2):
        tiles = [qv[:, (8 * h + j) * HD : (8 * h + j + 1) * HD].astype(F32) for j in range(8)]
        for G in range(3):
            rows = [tiles[j][s * DROWS + 8 * G : s * DROWS + 8 * G + 8] for j in range(8) for s in range(STEPS)]
            qb[h, G] = jnp.concatenate(rows, axis=0).astype(BF16)

    for G in range(3):
        cached(0, G)
    cached(1, 0)

    for item in local[9:]:
        item.wait()
    arrived(own, o_recv.at[0])
    weight_grad = (own[0].astype(F32) + own[1].astype(F32)).T / LEN
    new_m = beta_one * mv[...] + (1.0 - beta_one) * weight_grad
    new_v = beta_two * vv[...] + (1.0 - beta_two) * weight_grad * weight_grad
    weight_f = wv[...].astype(F32)
    direction = new_m / correct_one / (jnp.sqrt(new_v / correct_two) + adam_eps)
    new_weight = (weight_f - learn_rate * (direction + decay_rate * weight_f)).astype(BF16)
    nwb[...] = new_weight

    is_self = c == lax.div(x, 2)
    cols = pl.ds(aligned(lax.rem(x, 2), COL), COL)
    slices = []
    for r in range(2):
        src = nwb.at[pl.ds(r * COL, COL)]
        dst = wall.at[z * 2 + yh, :, cols]
        recv = c_recv.at[yh, lax.rem(x, 2)]
        near = copy(src, dst, c_send.at[r], recv, dev(c=lax.div(x, 2), x=2 * c + r))
        far = copy(src, dst, c_send.at[2 + r], recv, dev(yh=yo, c=lax.div(x, 2), x=2 * c + r))
        here = is_self & (lax.rem(x, 2) == r)
        pl.when(jnp.logical_not(here))(near.start)
        pl.when(here)(pltpu.make_async_copy(src, dst, recv).start)
        start(far)
        slices.append((here, near))

    cached(1, 1)
    cached(1, 2)
    mv[...] = new_m
    vv[...] = new_v
    outs_done = [
        pltpu.make_async_copy(src, refs[dst], out_sem.at[i])
        for i, (src, dst) in enumerate(((nwb, "nw_out"), (mv, "nm_out"), (vv, "nv_out")))
    ]
    for item in outs_done:
        item.start()

    for step in (1, -1, 2):
        slot = hb.at[xs(step) * 2 + c]
        arrived(slot, h_recv.at[xs(step)])
        copy(slot, slot, h_send.at[0], h_recv.at[X], dev(c=other)).start()

    pairs = (yh, yo)

    def pass_on(zz, k, part_of, way, jump=1):
        slot = wall.at[zz * 2 + pairs[k], :, pl.ds(part_of * COL, COL)]
        sem = 2 * k + part_of
        to = dev(z=zs(ways[way] * jump))
        copy(slot, slot, w_send.at[0], w_recv.at[zz, sem], to).start()

    for k in range(2):
        for part_of in range(2):
            arrived(wall.at[z * 2 + pairs[k], :, pl.ds(part_of * COL, COL)], c_recv.at[pairs[k], part_of])
            for way in range(2):
                pass_on(z, k, part_of, way)

    hid_local.wait()
    arrived(hb.at[pl.ds(0, X)], h_recv.at[X])

    def project(zz):
        rows = hb[:, :, pl.ds(aligned(zz, 2 * COL), 2 * COL)].reshape(2 * X * ROWS, 2 * COL)
        block = wall[pl.ds(zz * 2, 2)].reshape(2 * COL, 2 * COL)
        return jnp.dot(rows, block, preferred_element_type=F32)

    def received(step, k, part_of, way):
        zz = zs(-ways[way] * step)
        sem = 2 * k + part_of
        arrived(wall.at[zz * 2 + pairs[k], :, pl.ds(part_of * COL, COL)], w_recv.at[zz, sem])
        return zz

    acc[...] = project(z)
    for step in range(1, last):
        for k in range(2):
            for part_of in range(2):
                for way in range(2):
                    zz = received(step, k, part_of, way)
                    if step == last - 1 and way == k:
                        pass_on(zz, k, part_of, way, 2)
                    pass_on(zz, k, part_of, way)
        acc[...] += project(zs(-step)) + project(zs(step))


    def last_dot(rows, zz, cols):
        left_rows = rows[:, :, pl.ds(aligned(zz, 2 * COL), 2 * COL)]
        left_rows = left_rows.reshape(left_rows.shape[0] * ROWS, 2 * COL)
        block = wall[pl.ds(zz * 2, 2), :, cols].reshape(2 * COL, COL)
        return jnp.dot(left_rows, block, preferred_element_type=F32)

    for part_of in range(2):
        cols = pl.ds(part_of * COL, COL)
        for k in range(2):
            for way in range(2):
                received(last, k, part_of, way)
        acc[:, cols] += last_dot(hb, zs(-last), cols) + last_dot(hb, zs(last), cols)
        for k in range(2):
            received(Z // 2, k, part_of, k)
        for step in (2, 1, -1, 0):
            to = xs(step)
            sums = acc[pl.ds(aligned(to, 2 * ROWS), 2 * ROWS), cols]
            sums += last_dot(hb.at[pl.ds(to * 2, 2)], zs(Z // 2), cols)
            part[pl.ds(to * 2, 2), :, cols] = sums.astype(BF16).reshape(2, ROWS, HD)
            for core in range(2):
                to_c = c if core == 0 else other
                if step == 0 and core == 0:
                    ebuf[x, c, :, cols] = part[x * 2 + c, :, cols]
                    continue
                copy(
                    part.at[to * 2 + to_c, :, cols],
                    ebuf.at[x, c, :, cols],
                    e_send.at[0],
                    e_recv.at[part_of],
                    dev(x=to, c=to_c),
                ).start()
    for item in sends:
        item.wait_send()
    sent(oc.at[0, 0, pl.ds(0, 80)], r_send.at[0])
    sent(hb.at[pl.ds(0, 7), :, pl.ds(0, KSL // 2)], a_send.at[0])
    sent(wt.at[pl.ds(0, 448)], k_send.at[0])
    sent(wall.at[pl.ds(0, 14)], rs_send.at[0])
    sent(hb.at[pl.ds(0, 7)], h_send.at[0])
    sent(wall.at[pl.ds(0, 14)], w_send.at[0])
    for here, near in slices:
        pl.when(jnp.logical_not(here))(near.wait_send)

    units = [(h, G) for h in range(2) for G in range(3)]

    def fresh_rows(part_of):
        cols = pl.ds(part_of * COL, COL)
        arrived(part.at[pl.ds(0, 2 * X - 1), :, cols], e_recv.at[part_of])
        found = []
        for h in range(2):
            total = ebuf[0, h, :, cols].astype(F32)
            for src in range(1, X):
                total += ebuf[src, h, :, cols].astype(F32)
            found.append(total.astype(BF16))
            ent[:, (2 * h + part_of) * HD : (2 * h + part_of + 1) * HD] = found[h]
        return found

    row = lax.broadcasted_iota(jnp.int32, (ROWS, 256), 0)
    column = lax.broadcasted_iota(jnp.int32, (ROWS, 256), 1)
    order = lax.rem(lax.div(column, 8), STEPS) >= lax.div(row, DROWS)
    seen = [order & (lax.rem(row, DROWS) == lax.rem(column, 8) + 8 * G) for G in range(3)]
    keys = fresh_rows(0)
    scores = [
        lax.dot_general(keys[h], qb[h, G], (((1,), (1,)), ((), ())), preferred_element_type=F32) for h, G in units
    ]
    scores = [jnp.where(seen[G], item * HD ** (-0.5), masked_score) for (h, G), item in zip(units, scores)]
    before = [ml[h, G, 0:1, :] for h, G in units]
    top = [jnp.maximum(old, jnp.max(item, axis=0, keepdims=True)) for old, item in zip(before, scores)]
    weights = [jnp.exp(item - high) for item, high in zip(scores, top)]
    scale = [jnp.exp(old - high) for old, high in zip(before, top)]
    whole = [
        ml[h, G, 1:2, :] * factor + jnp.sum(item, axis=0, keepdims=True)
        for (h, G), factor, item in zip(units, scale, weights)
    ]
    for (h, G), factor, full, item in zip(units, scale, whole, weights):
        pb[h, pl.ds(256 * G, 256), :] = (item / full).T.astype(BF16)
        oc[h, G] = oc[h, G] * jnp.broadcast_to(factor / full, (HD, 256)).T
    values = fresh_rows(1)
    outs_done.append(pltpu.make_async_copy(ent, refs["ent_out"], out_sem.at[3]))
    outs_done[-1].start()
    outs = []
    for h in range(2):
        mixed = jnp.dot(pb[h], values[h], preferred_element_type=F32)
        outs += [oc[h, G] + mixed[256 * G : 256 * G + 256] for G in range(3)]
    for h in range(2):
        for j in range(8):
            rows = [
                outs[3 * h + G][(j * STEPS + s) * 8 : (j * STEPS + s) * 8 + 8] for s in range(STEPS) for G in range(3)
            ]
            att[:, (8 * h + j) * HD : (8 * h + j + 1) * HD] = jnp.concatenate(rows, axis=0).astype(BF16)
            if j % 4 == 3:
                quarter = 2 * h + j // 4
                cols = pl.ds(quarter * QW // 4, QW // 4)
                done = pltpu.make_async_copy(att.at[:, cols], refs["att_out"].at[:, cols], out_sem.at[4 + quarter])
                done.start()
                outs_done.append(done)

    for item in outs_done:
        item.wait()
    sent(part.at[pl.ds(0, 2 * X - 1)], e_send.at[0])


OUT_SHAPES = (
    jax.ShapeDtypeStruct((HALF, COL), BF16),
    jax.ShapeDtypeStruct((HALF, COL), F32),
    jax.ShapeDtypeStruct((HALF, COL), F32),
    jax.ShapeDtypeStruct((ROWS, 4 * HD), BF16),
    jax.ShapeDtypeStruct((ROWS, QW), BF16),
)


def write_out(*refs):
    count = len(OUT_SHAPES)
    sources, results, held, sems = refs[:count], refs[count : 2 * count], refs[2 * count : 3 * count], refs[-1]
    pieces = [(i, pl.ds(0, OUT_SHAPES[i].shape[1])) for i in range(count - 1)]
    pieces = [(count - 1, pl.ds(i * QW // 4, QW // 4)) for i in range(4)] + pieces
    into, away = [], []
    for n, (i, cols) in enumerate(pieces):
        into.append(pltpu.make_async_copy(sources[i].at[:, cols], held[i].at[:, cols], sems.at[0, n]))
        away.append(pltpu.make_async_copy(held[i].at[:, cols], results[i].at[:, cols], sems.at[1, n]))
    for item in into:
        item.start()
    for first, second in zip(into, away):
        first.wait()
        second.start()
    for item in away:
        item.wait()


def body(
    acts,
    kv_grad,
    rewards,
    group_ids,
    kv_weight,
    adam_m,
    adam_v,
    hidden,
    queries,
    cache_keys,
    cache_values,
    cache_lens,
):
    hbm = pl.BlockSpec(memory_space=pltpu.HBM)
    dma = pltpu.SemaphoreType.DMA
    results = pl.pallas_call(
        kernel,
        out_shape=OUT_SHAPES,
        in_specs=[hbm] * 12,
        out_specs=(hbm,) * 5,
        scratch_shapes=[
            pltpu.VMEM((X, 2 * TOK, HALF), BF16),
            pltpu.VMEM((T, TOK, COL), BF16),
            pltpu.VMEM((T * COL, 2 * TOK), BF16),
            pltpu.VMEM((X, T * COL, HALF), BF16),
            pltpu.VMEM((X, 2, Z // 2, COL // 2, HALF), BF16),
            pltpu.VMEM((2, COL, HALF), BF16),
            pltpu.VMEM((ROWS, WIDTH), BF16),
            pltpu.VMEM((X, ROWS, KSL), BF16),
            pltpu.VMEM((2 * X, ROWS, KSL), BF16),
            pltpu.VMEM((HALF, COL), BF16),
            pltpu.VMEM((2 * Z, COL, 2 * COL), BF16),
            pltpu.VMEM((2 * X * ROWS, 2 * COL), F32),
            pltpu.VMEM((2 * X, ROWS, 2 * COL), BF16),
            pltpu.VMEM((X, 2, ROWS, 2 * COL), BF16),
            pltpu.VMEM((4, 8, 128), F32),
            pltpu.VMEM((Z, 8, 128), F32),
            pltpu.VMEM((HALF, COL), BF16),
            pltpu.VMEM((HALF, COL), F32),
            pltpu.VMEM((HALF, COL), F32),
            pltpu.SMEM((SEQ,), F32),
            pltpu.SMEM((SEQ,), jnp.int32),
            pltpu.SMEM((DROWS,), jnp.int32),
            pltpu.VMEM((ROWS, QW), BF16),
            pltpu.VMEM((2, 3, 256, HD), BF16),
            pltpu.VMEM((DROWS, CACHE, 2 * HD), BF16),
            pltpu.VMEM((DROWS, CACHE, 2 * HD), BF16),
            pltpu.VMEM((2, 3, 256, HD), F32),
            pltpu.VMEM((2, 3, 8, 256), F32),
            pltpu.VMEM((2, 768, ROWS), BF16),
            pltpu.VMEM((ROWS, 4 * HD), BF16),
            pltpu.VMEM((ROWS, QW), BF16),
            dma((13,)),
            dma((1,)),
            dma((X, 2)),
            dma((1,)),
            dma((T + 1,)),
            dma((1,)),
            dma((2,)),
            dma((1,)),
            dma((X, 2, Z // 2)),
            dma((X,)),
            dma((1,)),
            dma((1,)),
            dma((X + 1,)),
            dma((4,)),
            dma((2, 2)),
            dma((1,)),
            dma((Z, 4)),
            dma((1,)),
            dma((2,)),
            dma((8,)),
        ],
        compiler_params=pltpu.CompilerParams(
            collective_id=0, has_side_effects=True, vmem_limit_bytes=63400000
        ),
        name="update_and_decode",
    )(
        acts,
        kv_grad,
        rewards,
        group_ids,
        kv_weight,
        adam_m,
        adam_v,
        hidden.reshape(ROWS, WIDTH),
        queries.reshape(ROWS, QW),
        cache_keys,
        cache_values,
        cache_lens,
    )
    new_weight, new_m, new_v, new_entries, attention = pl.pallas_call(
        write_out,
        out_shape=OUT_SHAPES,
        in_specs=[hbm] * 5,
        out_specs=(hbm,) * 5,
        scratch_shapes=[pltpu.VMEM(item.shape, item.dtype) for item in OUT_SHAPES] + [dma((2, 8))],
        compiler_params=pltpu.CompilerParams(vmem_limit_bytes=63400000),
        name="write_out",
    )(*results)
    return (
        new_weight,
        new_m,
        new_v,
        new_entries.reshape(STEPS, DROWS, 4 * HD),
        attention.reshape(STEPS, DROWS, QW),
    )


def solution(mesh):
    return jax.shard_map(
        body,
        mesh=mesh,
        in_specs=(
            P("fsdp", ("tp", "dp")),
            P("fsdp", ("tp", "dp")),
            P("fsdp"),
            P("fsdp"),
            P("fsdp", ("tp", "dp")),
            P("fsdp", ("tp", "dp")),
            P("fsdp", ("tp", "dp")),
            P(None, ("fsdp", "dp"), None),
            P(None, ("fsdp", "dp"), "tp"),
            P(("fsdp", "dp"), None, "tp"),
            P(("fsdp", "dp"), None, "tp"),
            P(("fsdp", "dp")),
        ),
        out_specs=(
            P("fsdp", ("tp", "dp")),
            P("fsdp", ("tp", "dp")),
            P("fsdp", ("tp", "dp")),
            P(None, ("fsdp", "dp"), "tp"),
            P(None, ("fsdp", "dp"), "tp"),
        ),
        check_vma=False,
    )
```

```python
import jax
import jax.numpy as jnp
from jax import lax
from jax.experimental import pallas as pl
from jax.experimental.pallas import tpu as pltpu
from jax.sharding import PartitionSpec as P

HD = 128
LEN = 48
GSIZE = 8
X = 4
T = 4
Z = 8
TOK = 384
SEQ = 8
FEAT = 512
HALF = 256
COL = 128
STEPS = 4
DROWS = 24
ROWS = 96
CACHE = 64
QW = 2048
WIDTH = 8192
KSL = WIDTH // X

beta_one = 0.9
beta_two = 0.95
learn_rate = 0.001
decay_rate = 0.1
adam_eps = 1e-08
correct_one = 1.0 - beta_one**10
correct_two = 1.0 - beta_two**10
masked_score = -1e30

MESH = pl.DeviceIdType.MESH
F32 = jnp.float32
BF16 = jnp.bfloat16


def aligned(value, multiple):
    return pl.multiple_of(value * multiple, multiple)

NAMES = (
    "acts", "kv", "rew", "ids", "w_in", "m_in", "v_in", "hid", "qry", "ckey", "cval", "lens", "nw_out",
    "nm_out", "nv_out", "ent_out", "att_out", "abuf", "kbuf", "wt", "pbuf", "rsbuf", "own", "hv", "hl", "hb",
    "nwb", "wall", "acc", "part", "ebuf", "ra", "rb", "wv", "mv", "vv", "rs", "ls", "ns", "qv", "qb", "ck", "cv",
    "oc", "ml", "pb", "ent", "att",  "loc_sem", "a_send", "a_recv", "k_send", "k_recv", "r_send", "r_recv", "rs_send",
    "rs_recv", "o_send", "o_recv", "h_send", "h_recv", "c_send", "c_recv", "w_send", "w_recv", "e_send",
    "e_recv", "out_sem",
)


def kernel(*all_refs):
    refs = dict(zip(NAMES, all_refs))
    acts, kv, hid = refs["acts"], refs["kv"], refs["hid"]
    abuf, kbuf, wt, pbuf, rsbuf, own = (refs[k] for k in ("abuf", "kbuf", "wt", "pbuf", "rsbuf", "own"))
    hv, hl, hb, nwb, wall, acc = (refs[k] for k in ("hv", "hl", "hb", "nwb", "wall", "acc"))
    part, ebuf, ra, rb = (refs[k] for k in ("part", "ebuf", "ra", "rb"))
    wv, mv, vv = (refs[k] for k in ("wv", "mv", "vv"))
    qv, qb, ck, cv, oc, ml, pb = (refs[k] for k in ("qv", "qb", "ck", "cv", "oc", "ml", "pb"))
    loc_sem, a_send, a_recv, k_send, k_recv = (refs[k] for k in NAMES[NAMES.index("loc_sem") :][:5])
    r_send, r_recv, rs_send, rs_recv, o_send, o_recv = (refs[k] for k in NAMES[NAMES.index("r_send") :][:6])
    h_send, h_recv, c_send, c_recv = (refs[k] for k in NAMES[NAMES.index("h_send") :][:4])
    w_send, w_recv, e_send, e_recv, out_sem = (refs[k] for k in NAMES[NAMES.index("w_send") :][:5])
    ent, att = refs["ent"], refs["att"]

    f, t, x = lax.axis_index("fsdp"), lax.axis_index("tp"), lax.axis_index("dp")
    z, g = lax.div(f, 4), lax.rem(f, 4)
    yh, c = lax.div(g, 2), lax.rem(g, 2)
    other, yo = 1 - c, 1 - yh

    def dev(z=z, yh=yh, c=c, t=t, x=x):
        return (z * 4 + yh * 2 + c, t, x)

    def copy(src, dst, send, recv, to):
        return pltpu.make_async_remote_copy(
            src_ref=src, dst_ref=dst, send_sem=send, recv_sem=recv, device_id=to, device_id_type=MESH
        )

    def arrived(dst, recv):
        copy(dst, dst, o_send.at[0], recv, dev(c=other)).wait_recv()

    def xs(step):
        return lax.rem(x + step + X, X)

    def zs(step):
        return lax.rem(z + step + Z, Z)

    def run_of(order):
        return jnp.bitwise_xor(jnp.bitwise_xor(t, order), 1)

    def half_of(src, slot):
        u = lax.rem(slot - 2 * t - lax.div(src, 2) + 2 * Z, Z)
        upper = jnp.where((u >= 1) & (u <= 4), 1, 0)
        return run_of(jnp.where(upper == 1, u - 1, lax.rem(Z - u, Z))), upper

    half = pl.ds(aligned(c, HALF), HALF)
    mine, other_rows = pl.ds(aligned(c, TOK), TOK), pl.ds(aligned(other, TOK), TOK)
    local = [
        pltpu.make_async_copy(src, dst, loc_sem.at[i])
        for i, (src, dst) in enumerate(
            (
                (refs["rew"], refs["rs"]),
                (refs["ids"], refs["ls"]),
                (kv, kbuf.at[t]),
                (refs["lens"], refs["ns"]),
                (refs["qry"], qv),
                (refs["ckey"], ck),
                (refs["cval"], cv),
                (acts.at[:, half], abuf.at[x, mine]),
                (hid, hv),
                (refs["w_in"], wv),
                (refs["m_in"], mv),
                (refs["v_in"], vv),
            )
        )
    ]
    for item in local[:2]:
        item.start()

    barrier = pltpu.get_barrier_semaphore()
    senders = [dev(z=zs(step)) for step in (4, 3, -3, 2, -2, 1, -1)]
    senders += [dev(yh=yo), dev(yh=yo, c=other)]
    senders += [dev(t=lax.rem(t + step, T)) for step in range(1, T)]
    senders += [dev(x=xs(step), c=core) for step in (1, -1) for core in range(2)]
    senders += [dev(c=other)]
    for sender in senders:
        pl.semaphore_signal(barrier, inc=1, device_id=sender, device_id_type=MESH)

    local[0].wait()
    local[1].wait()
    sub = lax.broadcasted_iota(jnp.int32, (8, 128), 0)
    lane = lax.broadcasted_iota(jnp.int32, (8, 128), 1)
    rew_row = jnp.zeros((8, 128), F32)
    id_row = jnp.full((8, 128), -1, jnp.int32)
    for seq in range(SEQ):
        rew_row = jnp.where(lane == seq, refs["rs"][seq], rew_row)
        id_row = jnp.where(lane == seq, refs["ls"][seq], id_row)
    id_row = id_row.astype(F32)
    ra[g] = jnp.where(sub == 2 * g, rew_row, jnp.where(sub == 2 * g + 1, id_row, 0.0))

    pl.semaphore_wait(barrier, len(senders))

    sends = []

    def start(item):
        item.start()
        sends.append(item)

    def sent(like, send):
        copy(like, like, send, o_recv.at[0], dev(c=other)).wait_send()

    trio = ((yh, other), (yo, c), (yo, other))
    for to_yh, to_c in trio:
        copy(ra.at[g], ra.at[g], r_send.at[0], r_recv.at[0], dev(yh=to_yh, c=to_c)).start()

    for sign in (1 - 2 * c, 2 * c - 1):
        for core in range(2):
            copy(
                acts.at[:, pl.ds(core * HALF, HALF)],
                abuf.at[x, mine],
                a_send.at[0],
                a_recv.at[x, c],
                dev(x=xs(sign), c=core),
            ).start()
    for step in range(1, T):
        copy(kv, kbuf.at[t], k_send.at[0], k_recv.at[t], dev(t=lax.rem(t + step, T))).start()
    copy(
        acts.at[:, pl.ds(aligned(other, HALF), HALF)],
        abuf.at[x, mine],
        a_send.at[0],
        a_recv.at[x, c],
        dev(c=other),
    ).start()

    for item in local[2:]:
        item.start()

    def cached(h, G):
        keys = ck[8 * G : 8 * G + 8, :, h * HD : (h + 1) * HD].reshape(8 * CACHE, HD)
        values = cv[8 * G : 8 * G + 8, :, h * HD : (h + 1) * HD].reshape(8 * CACHE, HD)
        scores = lax.dot_general(qb[h, G], keys, (((1,), (1,)), ((), ())), preferred_element_type=F32)
        scores *= HD ** (-0.5)
        column = lax.broadcasted_iota(jnp.int32, (1, 8 * CACHE), 1)
        limit = jnp.zeros((1, 8 * CACHE), jnp.int32)
        for row in range(8):
            limit = jnp.where(lax.div(column, CACHE) == row, refs["ns"][8 * G + row], limit)
        owner = jnp.where(lax.rem(column, CACHE) < limit, lax.div(column, CACHE), -1)
        row = lax.rem(lax.broadcasted_iota(jnp.int32, (256, 1), 0), 8)
        scores = jnp.where(row == owner, scores, masked_score)
        top = jnp.max(scores, axis=1, keepdims=True)
        weights = jnp.exp(scores - top)
        place = lax.broadcasted_iota(jnp.int32, (256, HD), 1)
        stats = jnp.where(place == 0, top, jnp.where(place == 1, jnp.sum(weights, axis=1, keepdims=True), 0.0))
        ml[h, G] = stats.T[0:8, :]
        oc[h, G] = jnp.dot(weights.astype(BF16), values, preferred_element_type=F32)

    arrived(ra.at[pl.ds(0, 3)], r_recv.at[0])
    rb[z] = ra[0] + ra[1] + ra[2] + ra[3]
    for step in range(1, Z):
        copy(rb.at[z], rb.at[z], r_send.at[0], r_recv.at[1], dev(z=zs(step))).start()

    local[8].wait()
    for q in range(WIDTH // FEAT):
        for to in range(X):
            hl[to, :, q * 128 : (q + 1) * 128] = hv[:, q * FEAT + to * 128 : q * FEAT + (to + 1) * 128]

    arrived(rb.at[pl.ds(0, Z - 1)], r_recv.at[1])
    rew_col = jnp.sum(jnp.where(sub == lane, rew_row, 0.0), axis=1, keepdims=True)
    id_col = jnp.sum(jnp.where(sub == lane, id_row, 0.0), axis=1, keepdims=True)
    sums = jnp.zeros((8, 128), F32)
    for zz in range(Z):
        for group in range(4):
            same = rb[zz, 2 * group + 1 : 2 * group + 2, :] == id_col
            sums += jnp.where(same, rb[zz, 2 * group : 2 * group + 1, :], 0.0)
    advantage = rew_col - jnp.sum(sums, axis=1, keepdims=True) / GSIZE

    def weigh(src):
        columns = [
            advantage[seq : seq + 1, 0:1] * kbuf[src, seq * LEN : (seq + 1) * LEN, :].astype(F32) for seq in range(SEQ)
        ]
        rows = pl.ds(aligned(src, COL), COL)
        wt[rows, mine] = jnp.concatenate(columns, axis=0).T.astype(BF16)
        copy(wt.at[rows, mine], wt.at[rows, mine], k_send.at[0], k_recv.at[T], dev(c=other)).start()

    local[2].wait()
    weigh(t)

    left, right, across = xs(-1), xs(1), xs(2)
    first, second = pl.ds(0, TOK), pl.ds(TOK, TOK)
    arrived(abuf.at[left, first], a_recv.at[left, 0])
    copy(abuf.at[left, first], abuf.at[left, first], a_send.at[0], a_recv.at[left, 0], dev(x=right)).start()
    arrived(abuf.at[right, second], a_recv.at[right, 1])
    copy(abuf.at[right, second], abuf.at[right, second], a_send.at[0], a_recv.at[right, 1], dev(x=left)).start()

    for step in (1, 3, 2):
        src = jnp.bitwise_xor(t, step)
        arrived(kbuf.at[src], k_recv.at[src])
        weigh(src)

    arrived(wt.at[:, other_rows], k_recv.at[T])

    blocks = (x, left, right, across)
    ways = (1, -1)

    last = Z // 2 - 1

    def hops(block, way):
        return last + 1 if block == 0 and way == 0 else last

    def jumps(block, way):
        return block > 0 and way == block % 2

    def own_piece(block, slot):
        run, upper = half_of(blocks[block], slot)
        return pbuf.at[block, pl.ds(aligned(2 * run + upper, COL // 2), COL // 2)]

    def begin(item):
        item.start()

    def ring_copy(src, block, way, step, jump=1):
        return copy(
            src,
            rsbuf.at[block, way, step],
            rs_send.at[0],
            rs_recv.at[block, way, step],
            dev(z=zs(ways[way] * jump)),
        )

    def multiply(block):
        pbuf[block] = jnp.dot(wt[...], abuf[blocks[block]], preferred_element_type=F32).astype(BF16)
        for way in range(2):
            if jumps(block, way):
                begin(ring_copy(own_piece(block, zs(Z // 2)), block, way, last, 2))
            begin(ring_copy(own_piece(block, zs(ways[way] * hops(block, way))), block, way, 0))

    def ring_step(block, step):
        for way in range(2):
            if step + 1 >= hops(block, way):
                continue
            here = rsbuf.at[block, way, step]
            arrived(here, rs_recv.at[block, way, step])
            slot = zs(ways[way] * (hops(block, way) - 1 - step))
            total = here[...].astype(F32) + own_piece(block, slot)[...].astype(F32)
            if step == 0 and jumps(block, way):
                arrived(rsbuf.at[block, way, last], rs_recv.at[block, way, last])
                total += rsbuf[block, way, last].astype(F32)
            here[...] = total.astype(BF16)
            begin(ring_copy(here, block, way, step + 1))

    local[7].wait()
    arrived(abuf.at[x, other_rows], a_recv.at[x, other])
    multiply(0)
    arrived(abuf.at[left, second], a_recv.at[left, 1])
    multiply(1)
    arrived(abuf.at[right, first], a_recv.at[right, 0])
    multiply(2)
    ring_step(0, 0)
    arrived(abuf.at[across, first], a_recv.at[across, 0])
    arrived(abuf.at[across, second], a_recv.at[across, 1])

    multiply(3)

    hslot = hb.at[x * 2 + c]
    hid_local = pltpu.make_async_copy(hl.at[x], hslot, loc_sem.at[12])
    hid_local.start()
    for step in (1, -1, 2):
        copy(hl.at[xs(step)], hslot, h_send.at[0], h_recv.at[x], dev(x=xs(step))).start()
    copy(hl.at[x], hslot, h_send.at[0], h_recv.at[X], dev(c=other)).start()

    to_owners = []

    def ring_end(block):
        total = own_piece(block, z)[...].astype(F32)
        for way in range(2):
            end = hops(block, way) - 1
            arrived(rsbuf.at[block, way, end], rs_recv.at[block, way, end])
            total += rsbuf[block, way, end].astype(F32)
        here = rsbuf.at[block, 1 - block % 2, last]
        here[...] = total.astype(BF16)
        src = blocks[block]
        run, upper = half_of(src, z)
        to_owners.append(
            copy(
                here,
                own.at[yh, pl.ds(aligned(upper, COL // 2), COL // 2)],
                o_send.at[block],
                o_recv.at[0],
                dev(z=2 * t + lax.div(src, 2), yh=lax.rem(src, 2), t=run),
            )
        )

    for block, step in ((1, 0), (2, 0), (0, 1), (1, 1), (3, 0), (2, 1), (0, 2), (3, 1)):
        ring_step(block, step)
    for block in (1, 2, 0, 3):
        ring_end(block)
    for item in to_owners:
        start(item)

    for item in local[3:7]:
        item.wait()
    for h in range(2):
        tiles = [qv[:, (8 * h + j) * HD : (8 * h + j + 1) * HD].astype(F32) for j in range(8)]
        for G in range(3):
            rows = [tiles[j][s * DROWS + 8 * G : s * DROWS + 8 * G + 8] for j in range(8) for s in range(STEPS)]
            qb[h, G] = jnp.concatenate(rows, axis=0).astype(BF16)

    for G in range(3):
        cached(0, G)
    cached(1, 0)

    for item in local[9:]:
        item.wait()
    arrived(own, o_recv.at[0])
    weight_grad = (own[0].astype(F32) + own[1].astype(F32)).T / LEN
    new_m = beta_one * mv[...] + (1.0 - beta_one) * weight_grad
    new_v = beta_two * vv[...] + (1.0 - beta_two) * weight_grad * weight_grad
    weight_f = wv[...].astype(F32)
    direction = new_m / correct_one / (jnp.sqrt(new_v / correct_two) + adam_eps)
    new_weight = (weight_f - learn_rate * (direction + decay_rate * weight_f)).astype(BF16)
    nwb[...] = new_weight

    is_self = c == lax.div(x, 2)
    cols = pl.ds(aligned(lax.rem(x, 2), COL), COL)
    slices = []
    for r in range(2):
        src = nwb.at[pl.ds(r * COL, COL)]
        dst = wall.at[z * 2 + yh, :, cols]
        recv = c_recv.at[yh, lax.rem(x, 2)]
        near = copy(src, dst, c_send.at[r], recv, dev(c=lax.div(x, 2), x=2 * c + r))
        far = copy(src, dst, c_send.at[2 + r], recv, dev(yh=yo, c=lax.div(x, 2), x=2 * c + r))
        here = is_self & (lax.rem(x, 2) == r)
        pl.when(jnp.logical_not(here))(near.start)
        pl.when(here)(pltpu.make_async_copy(src, dst, recv).start)
        start(far)
        slices.append((here, near))

    cached(1, 1)
    cached(1, 2)
    mv[...] = new_m
    vv[...] = new_v
    outs_done = [
        pltpu.make_async_copy(src, refs[dst], out_sem.at[i])
        for i, (src, dst) in enumerate(((nwb, "nw_out"), (mv, "nm_out"), (vv, "nv_out")))
    ]
    for item in outs_done:
        item.start()

    for step in (1, -1, 2):
        slot = hb.at[xs(step) * 2 + c]
        arrived(slot, h_recv.at[xs(step)])
        copy(slot, slot, h_send.at[0], h_recv.at[X], dev(c=other)).start()

    pairs = (yh, yo)

    def pass_on(zz, k, part_of, way, jump=1):
        slot = wall.at[zz * 2 + pairs[k], :, pl.ds(part_of * COL, COL)]
        sem = 2 * k + part_of
        to = dev(z=zs(ways[way] * jump))
        copy(slot, slot, w_send.at[0], w_recv.at[zz, sem], to).start()

    for k in range(2):
        for part_of in range(2):
            arrived(wall.at[z * 2 + pairs[k], :, pl.ds(part_of * COL, COL)], c_recv.at[pairs[k], part_of])
            for way in range(2):
                pass_on(z, k, part_of, way)

    hid_local.wait()
    arrived(hb.at[pl.ds(0, X)], h_recv.at[X])

    def project(zz):
        rows = hb[:, :, pl.ds(aligned(zz, 2 * COL), 2 * COL)].reshape(2 * X * ROWS, 2 * COL)
        block = wall[pl.ds(zz * 2, 2)].reshape(2 * COL, 2 * COL)
        return jnp.dot(rows, block, preferred_element_type=F32)

    def received(step, k, part_of, way):
        zz = zs(-ways[way] * step)
        sem = 2 * k + part_of
        arrived(wall.at[zz * 2 + pairs[k], :, pl.ds(part_of * COL, COL)], w_recv.at[zz, sem])
        return zz

    acc[...] = project(z)
    for step in range(1, last):
        for k in range(2):
            for part_of in range(2):
                for way in range(2):
                    zz = received(step, k, part_of, way)
                    if step == last - 1 and way == k:
                        pass_on(zz, k, part_of, way, 2)
                    pass_on(zz, k, part_of, way)
        acc[...] += project(zs(-step)) + project(zs(step))


    def last_dot(rows, zz, cols):
        left_rows = rows[:, :, pl.ds(aligned(zz, 2 * COL), 2 * COL)]
        left_rows = left_rows.reshape(left_rows.shape[0] * ROWS, 2 * COL)
        block = wall[pl.ds(zz * 2, 2), :, cols].reshape(2 * COL, COL)
        return jnp.dot(left_rows, block, preferred_element_type=F32)

    for part_of in range(2):
        cols = pl.ds(part_of * COL, COL)
        for k in range(2):
            for way in range(2):
                received(last, k, part_of, way)
        acc[:, cols] += last_dot(hb, zs(-last), cols) + last_dot(hb, zs(last), cols)
        for k in range(2):
            received(Z // 2, k, part_of, k)
        for step in (2, 1, -1, 0):
            to = xs(step)
            sums = acc[pl.ds(aligned(to, 2 * ROWS), 2 * ROWS), cols]
            sums += last_dot(hb.at[pl.ds(to * 2, 2)], zs(Z // 2), cols)
            part[pl.ds(to * 2, 2), :, cols] = sums.astype(BF16).reshape(2, ROWS, HD)
            for core in range(2):
                to_c = c if core == 0 else other
                if step == 0 and core == 0:
                    ebuf[x, c, :, cols] = part[x * 2 + c, :, cols]
                    continue
                copy(
                    part.at[to * 2 + to_c, :, cols],
                    ebuf.at[x, c, :, cols],
                    e_send.at[0],
                    e_recv.at[part_of],
                    dev(x=to, c=to_c),
                ).start()
    for item in sends:
        item.wait_send()
    sent(oc.at[0, 0, pl.ds(0, 80)], r_send.at[0])
    sent(hb.at[pl.ds(0, 7), :, pl.ds(0, KSL // 2)], a_send.at[0])
    sent(wt.at[pl.ds(0, 448)], k_send.at[0])
    sent(wall.at[pl.ds(0, 14)], rs_send.at[0])
    sent(hb.at[pl.ds(0, 7)], h_send.at[0])
    sent(wall.at[pl.ds(0, 14)], w_send.at[0])
    for here, near in slices:
        pl.when(jnp.logical_not(here))(near.wait_send)

    units = [(h, G) for h in range(2) for G in range(3)]

    def fresh_rows(part_of):
        cols = pl.ds(part_of * COL, COL)
        arrived(part.at[pl.ds(0, 2 * X - 1), :, cols], e_recv.at[part_of])
        found = []
        for h in range(2):
            total = ebuf[0, h, :, cols].astype(F32)
            for src in range(1, X):
                total += ebuf[src, h, :, cols].astype(F32)
            found.append(total.astype(BF16))
            ent[:, (2 * h + part_of) * HD : (2 * h + part_of + 1) * HD] = found[h]
        return found

    row = lax.broadcasted_iota(jnp.int32, (ROWS, 256), 0)
    column = lax.broadcasted_iota(jnp.int32, (ROWS, 256), 1)
    order = lax.rem(lax.div(column, 8), STEPS) >= lax.div(row, DROWS)
    seen = [order & (lax.rem(row, DROWS) == lax.rem(column, 8) + 8 * G) for G in range(3)]
    keys = fresh_rows(0)
    scores = [
        lax.dot_general(keys[h], qb[h, G], (((1,), (1,)), ((), ())), preferred_element_type=F32) for h, G in units
    ]
    scores = [jnp.where(seen[G], item * HD ** (-0.5), masked_score) for (h, G), item in zip(units, scores)]
    before = [ml[h, G, 0:1, :] for h, G in units]
    top = [jnp.maximum(old, jnp.max(item, axis=0, keepdims=True)) for old, item in zip(before, scores)]
    weights = [jnp.exp(item - high) for item, high in zip(scores, top)]
    scale = [jnp.exp(old - high) for old, high in zip(before, top)]
    whole = [
        ml[h, G, 1:2, :] * factor + jnp.sum(item, axis=0, keepdims=True)
        for (h, G), factor, item in zip(units, scale, weights)
    ]
    for (h, G), factor, full, item in zip(units, scale, whole, weights):
        pb[h, pl.ds(256 * G, 256), :] = (item / full).T.astype(BF16)
        oc[h, G] = oc[h, G] * jnp.broadcast_to(factor / full, (HD, 256)).T
    values = fresh_rows(1)
    outs_done.append(pltpu.make_async_copy(ent, refs["ent_out"], out_sem.at[3]))
    outs_done[-1].start()
    outs = []
    for h in range(2):
        mixed = jnp.dot(pb[h], values[h], preferred_element_type=F32)
        outs += [oc[h, G] + mixed[256 * G : 256 * G + 256] for G in range(3)]
    for h in range(2):
        for j in range(8):
            rows = [
                outs[3 * h + G][(j * STEPS + s) * 8 : (j * STEPS + s) * 8 + 8] for s in range(STEPS) for G in range(3)
            ]
            att[:, (8 * h + j) * HD : (8 * h + j + 1) * HD] = jnp.concatenate(rows, axis=0).astype(BF16)
            if j % 4 == 3:
                quarter = 2 * h + j // 4
                cols = pl.ds(quarter * QW // 4, QW // 4)
                done = pltpu.make_async_copy(att.at[:, cols], refs["att_out"].at[:, cols], out_sem.at[4 + quarter])
                done.start()
                outs_done.append(done)

    for item in outs_done:
        item.wait()
    sent(part.at[pl.ds(0, 2 * X - 1)], e_send.at[0])


OUT_SHAPES = (
    jax.ShapeDtypeStruct((HALF, COL), BF16),
    jax.ShapeDtypeStruct((HALF, COL), F32),
    jax.ShapeDtypeStruct((HALF, COL), F32),
    jax.ShapeDtypeStruct((ROWS, 4 * HD), BF16),
    jax.ShapeDtypeStruct((ROWS, QW), BF16),
)


def write_out(*refs):
    count = len(OUT_SHAPES)
    sources, results, held, sems = refs[:count], refs[count : 2 * count], refs[2 * count : 3 * count], refs[-1]
    pieces = [(i, pl.ds(0, OUT_SHAPES[i].shape[1])) for i in range(count - 1)]
    pieces = [(count - 1, pl.ds(i * QW // 4, QW // 4)) for i in range(4)] + pieces
    into, away = [], []
    for n, (i, cols) in enumerate(pieces):
        into.append(pltpu.make_async_copy(sources[i].at[:, cols], held[i].at[:, cols], sems.at[0, n]))
        away.append(pltpu.make_async_copy(held[i].at[:, cols], results[i].at[:, cols], sems.at[1, n]))
    for item in into:
        item.start()
    for first, second in zip(into, away):
        first.wait()
        second.start()
    for item in away:
        item.wait()


def body(
    acts,
    kv_grad,
    rewards,
    group_ids,
    kv_weight,
    adam_m,
    adam_v,
    hidden,
    queries,
    cache_keys,
    cache_values,
    cache_lens,
):
    hbm = pl.BlockSpec(memory_space=pltpu.HBM)
    dma = pltpu.SemaphoreType.DMA
    results = pl.pallas_call(
        kernel,
        out_shape=OUT_SHAPES,
        in_specs=[hbm] * 12,
        out_specs=(hbm,) * 5,
        scratch_shapes=[
            pltpu.VMEM((X, 2 * TOK, HALF), BF16),
            pltpu.VMEM((T, TOK, COL), BF16),
            pltpu.VMEM((T * COL, 2 * TOK), BF16),
            pltpu.VMEM((X, T * COL, HALF), BF16),
            pltpu.VMEM((X, 2, Z // 2, COL // 2, HALF), BF16),
            pltpu.VMEM((2, COL, HALF), BF16),
            pltpu.VMEM((ROWS, WIDTH), BF16),
            pltpu.VMEM((X, ROWS, KSL), BF16),
            pltpu.VMEM((2 * X, ROWS, KSL), BF16),
            pltpu.VMEM((HALF, COL), BF16),
            pltpu.VMEM((2 * Z, COL, 2 * COL), BF16),
            pltpu.VMEM((2 * X * ROWS, 2 * COL), F32),
            pltpu.VMEM((2 * X, ROWS, 2 * COL), BF16),
            pltpu.VMEM((X, 2, ROWS, 2 * COL), BF16),
            pltpu.VMEM((4, 8, 128), F32),
            pltpu.VMEM((Z, 8, 128), F32),
            pltpu.VMEM((HALF, COL), BF16),
            pltpu.VMEM((HALF, COL), F32),
            pltpu.VMEM((HALF, COL), F32),
            pltpu.SMEM((SEQ,), F32),
            pltpu.SMEM((SEQ,), jnp.int32),
            pltpu.SMEM((DROWS,), jnp.int32),
            pltpu.VMEM((ROWS, QW), BF16),
            pltpu.VMEM((2, 3, 256, HD), BF16),
            pltpu.VMEM((DROWS, CACHE, 2 * HD), BF16),
            pltpu.VMEM((DROWS, CACHE, 2 * HD), BF16),
            pltpu.VMEM((2, 3, 256, HD), F32),
            pltpu.VMEM((2, 3, 8, 256), F32),
            pltpu.VMEM((2, 768, ROWS), BF16),
            pltpu.VMEM((ROWS, 4 * HD), BF16),
            pltpu.VMEM((ROWS, QW), BF16),
            dma((13,)),
            dma((1,)),
            dma((X, 2)),
            dma((1,)),
            dma((T + 1,)),
            dma((1,)),
            dma((2,)),
            dma((1,)),
            dma((X, 2, Z // 2)),
            dma((X,)),
            dma((1,)),
            dma((1,)),
            dma((X + 1,)),
            dma((4,)),
            dma((2, 2)),
            dma((1,)),
            dma((Z, 4)),
            dma((1,)),
            dma((2,)),
            dma((8,)),
        ],
        compiler_params=pltpu.CompilerParams(
            collective_id=0, has_side_effects=True, vmem_limit_bytes=63400000
        ),
        name="update_and_decode",
    )(
        acts,
        kv_grad,
        rewards,
        group_ids,
        kv_weight,
        adam_m,
        adam_v,
        hidden.reshape(ROWS, WIDTH),
        queries.reshape(ROWS, QW),
        cache_keys,
        cache_values,
        cache_lens,
    )
    new_weight, new_m, new_v, new_entries, attention = pl.pallas_call(
        write_out,
        out_shape=OUT_SHAPES,
        in_specs=[hbm] * 5,
        out_specs=(hbm,) * 5,
        scratch_shapes=[pltpu.VMEM(item.shape, item.dtype) for item in OUT_SHAPES] + [dma((2, 8))],
        compiler_params=pltpu.CompilerParams(vmem_limit_bytes=63400000),
        name="write_out",
    )(*results)
    return (
        new_weight,
        new_m,
        new_v,
        new_entries.reshape(STEPS, DROWS, 4 * HD),
        attention.reshape(STEPS, DROWS, QW),
    )


def solution(mesh):
    return jax.shard_map(
        body,
        mesh=mesh,
        in_specs=(
            P("fsdp", ("tp", "dp")),
            P("fsdp", ("tp", "dp")),
            P("fsdp"),
            P("fsdp"),
            P("fsdp", ("tp", "dp")),
            P("fsdp", ("tp", "dp")),
            P("fsdp", ("tp", "dp")),
            P(None, ("fsdp", "dp"), None),
            P(None, ("fsdp", "dp"), "tp"),
            P(("fsdp", "dp"), None, "tp"),
            P(("fsdp", "dp"), None, "tp"),
            P(("fsdp", "dp")),
        ),
        out_specs=(
            P("fsdp", ("tp", "dp")),
            P("fsdp", ("tp", "dp")),
            P("fsdp", ("tp", "dp")),
            P(None, ("fsdp", "dp"), "tp"),
            P(None, ("fsdp", "dp"), "tp"),
        ),
        check_vma=False,
    )
```
